128 devices in a mesh: section: 2 (over core), seq: 16 (over y, x), wshard: 4 (over z).
Axes of the slice: x: 4, y: 4, z: 4, core: 2. Of those that a mesh axis runs over, the one named last changes fastest.
Arguments:
- block_input: bfloat16 [2, 4, 1024, 1024], P(None, 'wshard', 'seq'), may hold values from -6 to 6
- doc_ids: int32 [2, 4, 1024], P(None, 'wshard'), may hold values from 0 to 3, never falling along the last dimension, each value on 1 to 961 neighbouring positions
- out_grad: bfloat16 [2, 4, 1024, 1024], P(None, 'wshard', 'seq'), may hold values from -6 to 6
- in_proj: bfloat16 [2, 1024, 4384], P('section', 'wshard'), may hold values from -0.1875 to 0.1875
- out_proj: bfloat16 [2, 2048, 1024], P('section', 'wshard'), may hold values from -0.125 to 0.125
- conv_weight: float32 [2, 4, 2304], P('section'), may hold values from -3 to 3
- conv_bias: float32 [2, 2304], P('section'), may hold values from -3 to 3
- dt_bias: float32 [2, 32], P('section'), may hold values from -6.9 to -2.3
- a_log: float32 [2, 32], P('section'), may hold values from 0 to 2.77
- skip_scale: float32 [2, 32], P('section'), may hold values from 0.5 to 1.5
- pre_gain: float32 [2, 1024], P('section'), may hold values from 0.5 to 1.5
- norm_gain: float32 [2, 2048], P('section'), may hold values from 0.5 to 1.5
Outputs:
- hidden: float32 [2, 2, 4, 1024, 1024], P('section', None, 'wshard', 'seq')
- input_grads: float32 [2, 2, 4, 1024, 1024], P('section', None, 'wshard', 'seq')
- grad_in_proj: float32 [2, 1024, 4384], P('section', 'wshard')
- grad_out_proj: float32 [2, 2048, 1024], P('section', 'wshard')
- grad_conv_weight: float32 [2, 4, 2304], P('section')
- grad_conv_bias: float32 [2, 2304], P('section')
- grad_dt_bias: float32 [2, 32], P('section')
- grad_a_log: float32 [2, 32], P('section')
- grad_skip_scale: float32 [2, 32], P('section')
- grad_pre_gain: float32 [2, 1024], P('section')
- grad_norm_gain: float32 [2, 2048], P('section')
The draws below stay inside these ranges and needn't reach their ends.
Inputs may be any that keep to these rules, and one draw needn't show every extreme that they name: `doc_ids`: within a sequence the document numbers never fall, and one document covers all positions but fewer than 64.
All inputs are finite; a program needn't handle non-finite values.
Results may differ from the reference program's by a relative error of at most 0.02.
Values may be sent and summed in bfloat16 or wider, within the bound.
A program may use at most 256 MiB of HBM per device.

```python
import math
import jax
import jax.numpy as jnp
import numpy as np
from jax import lax

D = 1024
H = 32
NSTATE = 128
CONV_K = 4
SPAN = 256
MB = 2
DOCS = 4
INNER = 2048
PROJ = 4384
CONV_CH = 2304
SEQ_LEN = 1024
BATCH = 4
N_SECTION = 2
N_SEQ = 16


def block_scale(key, extent, cuts, least, high):
    def one(axis_at, parts):
        draws = jax.random.uniform(jax.random.fold_in(jax.random.fold_in(key, 6), axis_at), (parts,), jnp.float32, least / len(cuts), high / len(cuts))
        return jnp.repeat(jnp.exp(draws), extent[axis_at] // parts).reshape((-1,) + (1,) * (len(extent) - axis_at - 1))

    level = one(*cuts[0])
    for cut in cuts[1:]:
        level = level * one(*cut)
    return level


def split_up(amount, total, limit, slope):
    portions = [(1 << 20) // math.isqrt(rank ** slope) + 1 for rank in range(2, amount + 1)]
    rest, given = total - limit - (amount - 1), [1] * (amount - 1)
    while rest > 0:
        free = [i for i in range(amount - 1) if given[i] < limit]
        mass, remaining = sum([portions[i] for i in free]), rest
        for i in free:
            more = min(limit - given[i], max(1, remaining * portions[i] // mass), rest)
            given[i] = given[i] + more
            rest = rest - more
    return np.array([limit] + given)


def ragged(stream_key, amount, total, reach, skew):
    if amount == 2:
        one = jax.random.randint(stream_key, (), max(1, total - reach), min(reach, total - 1) + 1)
        return jnp.stack([one, total - one])
    tallies = jnp.asarray(split_up(amount, total, reach, skew), jnp.int32)
    pairs = (amount - 1) // 2
    giver, receiver = tallies[1:1 + 2 * pairs:2], tallies[2:2 + 2 * pairs:2]
    margin = jnp.minimum(giver - 1, reach - receiver)
    moved = jax.random.randint(jax.random.fold_in(stream_key, 1), (pairs,), 0, 1 << 20) % (margin + 1)
    tallies = tallies.at[1:1 + 2 * pairs:2].set(giver - moved).at[2:2 + 2 * pairs:2].set(receiver + moved)
    return tallies[jax.random.permutation(jax.random.fold_in(stream_key, 2), amount)]


def scatter_about(own_key, dims, deviation, most, split=(), held_as=jnp.bfloat16):
    values = jax.random.normal(own_key, dims, jnp.float32) * deviation
    if len(split) > 0:
        values = block_scale(own_key, dims, split, -0.22, 0.18) * values
    return jnp.clip(values, min=-most, max=most).astype(held_as)


def setup_inputs(seed: int = 0) -> dict:
    key_list = jax.random.split(jax.random.key(seed), 13)
    block_input = scatter_about(key_list[0], (MB, BATCH, SEQ_LEN, D), 1.0, 6.0, ((1, 4), (2, 16)))
    doc_ids = jax.vmap(lambda own: jnp.searchsorted(jnp.cumsum(ragged(own, DOCS, SEQ_LEN, SEQ_LEN - SEQ_LEN // N_SEQ + 1, 0)), jnp.arange(SEQ_LEN), side="right"))(jax.random.split(key_list[1], MB * BATCH)).reshape((MB, BATCH, SEQ_LEN)).astype(jnp.int32)
    out_grad = scatter_about(key_list[2], (MB, BATCH, SEQ_LEN, D), 1.0, 6.0, ((1, 4), (2, 16)))
    in_proj = scatter_about(key_list[3], (N_SECTION, D, PROJ), D ** -0.5, 0.1875, ((0, 2), (1, 4)))
    out_proj = scatter_about(key_list[4], (N_SECTION, INNER, D), INNER ** -0.5, 0.125, ((0, 2), (1, 4)))
    conv_weight = scatter_about(key_list[5], (N_SECTION, CONV_K, CONV_CH), CONV_K ** -0.5, 3.0, ((0, 2),), jnp.float32)
    conv_bias = scatter_about(key_list[6], (N_SECTION, CONV_CH), 0.5, 3.0, ((0, 2),), jnp.float32)
    dt_bias = jnp.clip(-6.9 + 4.6000001430511475 * jax.random.uniform(key_list[7], (N_SECTION, H), jnp.float32) ** block_scale(key_list[7], (N_SECTION, H), ((0, 2),), -0.2, 0.2), -6.9, -2.3)
    a_log = jnp.clip(2.77 * jax.random.uniform(key_list[8], (N_SECTION, H), jnp.float32) ** block_scale(key_list[8], (N_SECTION, H), ((0, 2),), -0.2, 0.2), 0.0, 2.77)
    skip_scale = jnp.clip(0.5 + 1.0 * jax.random.uniform(key_list[9], (N_SECTION, H), jnp.float32) ** block_scale(key_list[9], (N_SECTION, H), ((0, 2),), -0.2, 0.2), 0.5, 1.5)
    pre_gain = jnp.clip(1.0 + 0.1 * jax.random.normal(key_list[10], (N_SECTION, D), jnp.float32), 0.5, 1.5)
    norm_gain = jnp.clip(1.0 + 0.1 * jax.random.normal(key_list[11], (N_SECTION, INNER), jnp.float32), 0.5, 1.5)
    return {"block_input": block_input, "doc_ids": doc_ids, "out_grad": out_grad, "in_proj": in_proj, "out_proj": out_proj, "conv_weight": conv_weight, "conv_bias": conv_bias, "dt_bias": dt_bias, "a_log": a_log, "skip_scale": skip_scale, "pre_gain": pre_gain, "norm_gain": norm_gain}


epsilon = 1e-05
exact_matmul_accuracy = lax.Precision.HIGHEST

@jax.custom_vjp
def low(v):
    return lax.optimization_barrier(v.astype(jnp.bfloat16)).astype(jnp.float32)

@jax.custom_vjp
def low_back(v):
    return v

def low_keep(v):
    return (low(v), None)

def low_pass(kept, grad):
    return (grad,)

def back_keep(v):
    return (v, None)

def back_low(kept, grad):
    return (low(grad),)
low.defvjp(low_keep, low_pass)
low_back.defvjp(back_keep, back_low)

def rms_scale(values, gain):
    return values * lax.rsqrt(lax.optimization_barrier(jnp.mean(values * values, axis=-1, keepdims=True)) + epsilon) * gain

def conv_segment(signal, doc_row, kernel, offset):
    tap_count = kernel.shape[0]
    length = signal.shape[0]
    padded = jnp.pad(signal, ((tap_count - 1, 0), (0, 0)))
    doc_padded = jnp.pad(doc_row, (tap_count - 1, 0), constant_values=-1)
    summed = jnp.zeros_like(signal) + offset
    for tap_index in range(tap_count):
        matching_document_mask = (doc_padded[tap_index:tap_index + length] == doc_row)[:, None]
        summed = summed + jnp.where(matching_document_mask, padded[tap_index:tap_index + length] * kernel[tap_index], 0.0)
    return jax.nn.silu(summed)

def span_update(carried, block_data):
    scaled_x, b_rows, c_rows, log_decay, doc_block, prev_doc = block_data
    block_len = doc_block.shape[0]
    running = jnp.cumsum(log_decay, axis=0)
    positions = jnp.arange(block_len)
    causal = (positions[:, None] >= positions[None, :]) & (doc_block[:, None] == doc_block[None, :])
    gaps = running.T[:, :, None] - running.T[:, None, :]
    decay_matrix = jnp.exp(jnp.where(causal[None], gaps, -1e+30))
    scores = jnp.dot(c_rows, b_rows.T, precision=exact_matmul_accuracy)
    within = jnp.einsum('hij,jhp->ihp', scores[None] * decay_matrix, scaled_x, precision=exact_matmul_accuracy)
    keep_row = (doc_block == prev_doc).astype(jnp.float32)
    reach_row = jnp.exp(running) * keep_row[:, None]
    across = jnp.einsum('in,hnp->ihp', c_rows, carried, precision=exact_matmul_accuracy) * reach_row[:, :, None]
    block_total = running[-1]
    tail_weight = jnp.exp(block_total[None, :] - running) * (doc_block == doc_block[-1]).astype(jnp.float32)[:, None]
    carry_factor = jnp.exp(block_total) * (doc_block[-1] == prev_doc).astype(jnp.float32)
    updated = carried * carry_factor[:, None, None] + jnp.einsum('jn,jhp->hnp', b_rows, scaled_x * tail_weight[:, :, None], precision=exact_matmul_accuracy)
    return (updated, within + across)

def mixing(x_head, bc_rows, dt_raw, doc_row, conv_x, bias_x, conv_bc, bias_bc, dt_shift, decay_log, skip_part):
    length, channels = x_head.shape
    head_count = dt_raw.shape[1]
    attention_head_breadth = channels // head_count
    state_size = bc_rows.shape[1] // 2
    conv_out = conv_segment(x_head, doc_row, conv_x, bias_x)
    bc_conv = conv_segment(bc_rows, doc_row, conv_bc, bias_bc)
    step_size = jax.nn.softplus(dt_raw + dt_shift)
    log_decay = -step_size * jnp.exp(decay_log)
    heads_x = conv_out.reshape(length, head_count, attention_head_breadth)
    scaled_x = heads_x * step_size[:, :, None]
    block_count = length // SPAN
    doc_blocks = doc_row.reshape(block_count, SPAN)
    prev_docs = jnp.concatenate([doc_row[:1].astype(jnp.int32), doc_blocks[:-1, -1].astype(jnp.int32)])
    inputs = (scaled_x.reshape(block_count, SPAN, head_count, attention_head_breadth), bc_conv[:, :state_size].reshape(block_count, SPAN, state_size), bc_conv[:, state_size:].reshape(block_count, SPAN, state_size), log_decay.reshape(block_count, SPAN, head_count), doc_blocks, prev_docs)
    start_state = jnp.zeros((head_count, state_size, attention_head_breadth), jnp.float32)
    unused, outputs = lax.scan(jax.checkpoint(span_update), start_state, inputs)
    mixed = outputs.reshape(length, head_count, attention_head_breadth) + heads_x * skip_part[None, :, None]
    return mixed.reshape(length, channels)

def block_layer(hidden_in, doc_rows, input_weight, final_mapping_matrix, conv_weight, conv_bias, dt_bias, a_log, skip_scale, pre_gain, norm_gain):
    inner_width = final_mapping_matrix.shape[0]
    bc_end = 2 * inner_width + 2 * NSTATE
    normalized_rows = low(rms_scale(hidden_in, pre_gain))
    projected_rows = low_back(jnp.einsum('rvm,mc->rvc', normalized_rows, input_weight, precision=exact_matmul_accuracy))
    gate_part = projected_rows[..., :inner_width]
    x_part = low(projected_rows[..., inner_width:2 * inner_width])
    bc_part = low(projected_rows[..., 2 * inner_width:bc_end])
    dt_part = low(projected_rows[..., bc_end:])

    def per_sequence(pieces):
        return mixing(pieces[0], pieces[1], pieces[2], pieces[3], conv_weight[:, :inner_width], conv_bias[:inner_width], conv_weight[:, inner_width:], conv_bias[inner_width:], dt_bias, a_log, skip_scale)
    mixed = lax.map(per_sequence, (x_part, bc_part, dt_part, doc_rows))
    mixed = low_back(low(mixed))
    rescaled_result_vector = low(rms_scale(mixed * jax.nn.silu(gate_part), norm_gain))
    auxiliary_residual_path = low_back(jnp.einsum('gmt,td->gmd', rescaled_result_vector, final_mapping_matrix, precision=exact_matmul_accuracy))
    return hidden_in + auxiliary_residual_path

def reference(block_input, doc_ids, out_grad, in_proj, out_proj, conv_weight, conv_bias, dt_bias, a_log, skip_scale, pre_gain, norm_gain):
    seq_total = MB * BATCH
    start_values = block_input.astype(jnp.float32).reshape(seq_total, SEQ_LEN, D)
    doc_rows = doc_ids.reshape(seq_total, SEQ_LEN)
    cotangent = out_grad.astype(jnp.float32).reshape(seq_total, SEQ_LEN, D)
    params = (in_proj.astype(jnp.float32), out_proj.astype(jnp.float32), conv_weight, conv_bias, dt_bias, a_log, skip_scale, pre_gain, norm_gain)

    def forward(inputs, weights, probe_add):
        first_out = block_layer(inputs, doc_rows, *[param_array[0] for param_array in weights]) + probe_add
        second_out = block_layer(first_out, doc_rows, *[param_array[1] for param_array in weights])
        return (first_out, second_out)
    probe_zero = jnp.zeros_like(start_values)
    outputs, pull = jax.vjp(forward, start_values, params, probe_zero)
    grad_start, grad_params, grad_probe = pull((jnp.zeros_like(outputs[0]), cotangent))
    hidden = jnp.stack([outputs[0], outputs[1]]).reshape(N_SECTION, MB, BATCH, SEQ_LEN, D)
    input_grads = jnp.stack([grad_start, grad_probe]).reshape(N_SECTION, MB, BATCH, SEQ_LEN, D)
    return (hidden, input_grads, grad_params[0], grad_params[1], grad_params[2], grad_params[3], grad_params[4], grad_params[5], grad_params[6], grad_params[7], grad_params[8])
```

```python
import jax
import jax.numpy as jnp
from jax import lax
from jax.experimental import pallas as pl
from jax.experimental.pallas import tpu as pltpu
from jax.sharding import PartitionSpec as P

SPAN = 256
EPS = 1e-05
F32 = jnp.float32
BF16 = jnp.bfloat16
MESH = pl.DeviceIdType.MESH
VMEM_ASK = 48 * 1024 * 1024

HC = 128
NS = 128
PC = 640
AUX = 128
HEAD = 64


def dot_nn(a, b):
    return lax.dot_general(a, b, (((1,), (0,)), ((), ())), preferred_element_type=F32)


def dot_nt(a, b):
    return lax.dot_general(a, b, (((1,), (1,)), ((), ())), preferred_element_type=F32)


def dot_tn(a, b):
    return lax.dot_general(a, b, (((0,), (0,)), ((), ())), preferred_element_type=F32)


def three(x):
    hi = x.astype(BF16)
    rest = x - hi.astype(F32)
    mid = rest.astype(BF16)
    low = (rest - mid.astype(F32)).astype(BF16)
    return hi, mid, low


def exact_left(ones, x):
    hi, mid, low = three(x)
    return dot_nn(ones, hi) + dot_nn(ones, mid) + dot_nn(ones, low)


def exact_right(x, ones):
    hi, mid, low = three(x)
    return dot_nn(hi, ones) + dot_nn(mid, ones) + dot_nn(low, ones)


def iota(shape, dim):
    return lax.broadcasted_iota(jnp.int32, shape, dim)


def sigmoid(x):
    return 1.0 / (1.0 + jnp.exp(-x))


def softplus(x):
    return jnp.maximum(x, 0.0) + jnp.log1p(jnp.exp(-jnp.abs(x)))


def conv_rows(vbuf, cw_ref, mask):
    z = vbuf[pl.ds(8, SPAN), :] * cw_ref[3:4, :] + cw_ref[4:5, :]
    for k in (1, 2, 3):
        z = z + vbuf[pl.ds(8 - k, SPAN), :] * cw_ref[3 - k : 4 - k, :] * mask[:, k - 1 : k]
    return z


def block_terms(dt, vec_ref, mask, docr_ref):
    step = softplus(dt + vec_ref[0:1, :])
    log_decay = -step * vec_ref[1:2, :]
    rows, cols = iota((SPAN, SPAN), 0), iota((SPAN, SPAN), 1)
    lower = rows >= cols
    running = exact_left(lower.astype(F32).astype(BF16), log_decay)
    turned = running.T
    allowed = lower & (mask[:, 8:9] == docr_ref[...])
    decays = []
    for h in (0, 1):
        gaps = running[:, h * HEAD : h * HEAD + 1] - turned[h * HEAD : h * HEAD + 1, :]
        decays.append(jnp.exp(jnp.where(allowed, gaps, -1e30)))
    reach = jnp.exp(running) * mask[:, 6:7]
    total = running[SPAN - 1 :, :]
    tail = jnp.exp(total - running) * mask[:, 7:8]
    carry = jnp.exp(total) * mask[SPAN - 1 :, 6:7]
    return step, log_decay, decays, reach, tail, carry


def fwd_kernel(
    n_ref, w_ref, wo_ref, cw_ref, vec_ref, mask_ref, docr_ref,
    part_ref, vh_ref, gate_ref, dt_ref, mix_ref, scan_ref, st_ref,
    vbuf, state,
):
    @pl.when(pl.program_id(0) == 0)
    def _():
        vbuf[0:8, :] = jnp.zeros((8, 3 * HC), F32)
        state[...] = jnp.zeros_like(state)

    mask = mask_ref[...]
    proj = dot_nn(n_ref[...], w_ref[...])
    gate = proj[:, :HC]
    v = proj[:, HC : 4 * HC].astype(BF16).astype(F32)
    dt = proj[:, 4 * HC :].astype(BF16).astype(F32)
    vbuf[8:, :] = v
    z = conv_rows(vbuf, cw_ref, mask)
    vh_ref[0] = vbuf[...]
    vbuf[0:8, :] = v[SPAN - 8 :, :]
    act = z * sigmoid(z)
    xc = act[:, :HC]
    b16 = act[:, HC : 2 * HC].astype(BF16)
    c16 = act[:, 2 * HC :].astype(BF16)
    step, _, decays, reach, tail, carry = block_terms(dt, vec_ref, mask, docr_ref)
    xs = xc * step
    xs16 = xs.astype(BF16)
    scores = dot_nt(c16, b16)
    within = [dot_nn((scores * d).astype(BF16), xs16) for d in decays]
    first = iota((SPAN, HC), 1) < HEAD
    st = state[...]
    st_ref[0] = st
    scan = jnp.where(first, within[0], within[1]) + dot_nn(c16, st.astype(BF16)) * reach
    state[...] = st * carry + dot_tn(b16, (xs * tail).astype(BF16))
    mixed = (scan + xc * vec_ref[2:3, :]).astype(BF16)
    g = mixed.astype(F32) * (gate * sigmoid(gate))
    part_ref[:, : wo_ref.shape[1]] = dot_nn(
        (g * vec_ref[3:4, :]).astype(BF16), wo_ref[...]
    ).astype(BF16)
    hi, mid, low = three(jnp.sum(g * g, axis=1, keepdims=True))
    lane = iota((SPAN, AUX), 1)
    aux = jnp.where(lane == 0, hi.astype(F32), 0.0)
    aux = jnp.where(lane == 1, mid.astype(F32), aux)
    aux = jnp.where(lane == 2, low.astype(F32), aux)
    part_ref[:, wo_ref.shape[1] :] = aux.astype(BF16)
    gate_ref[...] = gate
    dt_ref[...] = dt
    mix_ref[...] = mixed
    scan_ref[...] = scan


def whole(shape):
    return pl.BlockSpec(shape, lambda i: (0,) * len(shape))


def forward_core(n, w, wo, cw, vec, mask, docr):
    length, width = n.shape
    blocks = length // SPAN

    def rows(cols):
        return pl.BlockSpec((SPAN, cols), lambda i: (i, 0))

    return pl.pallas_call(
        fwd_kernel,
        grid=(blocks,),
        in_specs=[
            rows(width), whole(w.shape), whole(wo.shape), whole(cw.shape), whole(vec.shape),
            rows(mask.shape[1]), pl.BlockSpec((1, SPAN), lambda i: (0, i)),
        ],
        out_specs=[
            rows(width + AUX),
            pl.BlockSpec((1, SPAN + 8, 3 * HC), lambda i: (i, 0, 0)),
            rows(HC), rows(HC), rows(HC), rows(HC),
            pl.BlockSpec((1, NS, HC), lambda i: (i, 0, 0)),
        ],
        out_shape=[
            jax.ShapeDtypeStruct((length, width + AUX), BF16),
            jax.ShapeDtypeStruct((blocks, SPAN + 8, 3 * HC), F32),
            jax.ShapeDtypeStruct((length, HC), F32),
            jax.ShapeDtypeStruct((length, HC), F32),
            jax.ShapeDtypeStruct((length, HC), BF16),
            jax.ShapeDtypeStruct((length, HC), F32),
            jax.ShapeDtypeStruct((blocks, NS, HC), F32),
        ],
        scratch_shapes=[pltpu.VMEM((SPAN + 8, 3 * HC), F32), pltpu.VMEM((NS, HC), F32)],
        compiler_params=pltpu.CompilerParams(vmem_limit_bytes=VMEM_ASK),
        name="forward_core",
    )(n, w, wo, cw, vec, mask, docr)


def bwd_kernel(
    c_ref, n_ref, w_ref, wo_ref, cw_ref, vec_ref, mask_ref, docr_ref,
    vh_ref, gate_ref, dt_ref, mix_ref, scan_ref, st_ref,
    part_ref, gin_ref, gout_ref, small_ref,
    dzbuf, dstate,
):
    @pl.when(pl.program_id(0) == 0)
    def _():
        dzbuf[SPAN:, :] = jnp.zeros((8, 3 * HC), F32)
        dstate[...] = jnp.zeros_like(dstate)
        gin_ref[...] = jnp.zeros_like(gin_ref)
        gout_ref[...] = jnp.zeros_like(gout_ref)
        small_ref[...] = jnp.zeros_like(small_ref)

    width = wo_ref.shape[1]
    mask = mask_ref[...]
    cot = c_ref[:, :width]
    aux = c_ref[:, width:].astype(F32)
    r = aux[:, 0:1] + aux[:, 1:2] + aux[:, 2:3]
    pull = aux[:, 3:4] + aux[:, 4:5]
    gate = gate_ref[...]
    sg = sigmoid(gate)
    silu = gate * sg
    mixed = mix_ref[...].astype(F32)
    g = mixed * silu
    gain = vec_ref[3:4, :]
    dy = dot_nt(cot, wo_ref[...])
    gr = g * r
    gout_ref[...] += dot_tn((gr * gain).astype(BF16), cot)
    d_gain = jnp.sum(dy * gr, axis=0, keepdims=True)
    dg = dy * (r * gain) - g * pull
    dm16 = (dg * silu).astype(BF16)
    dm = dm16.astype(F32)
    dgate = dg * mixed * (sg * (1.0 + gate * (1.0 - sg)))

    vbuf = vh_ref.at[0]
    z = conv_rows(vbuf, cw_ref, mask)
    sz = sigmoid(z)
    act = z * sz
    xc = act[:, :HC]
    b16 = act[:, HC : 2 * HC].astype(BF16)
    c16 = act[:, 2 * HC :].astype(BF16)
    dt = dt_ref[...]
    step, log_decay, decays, reach, tail, carry = block_terms(dt, vec_ref, mask, docr_ref)
    xs16 = (xc * step).astype(BF16)
    xs = xs16.astype(F32)
    scores = dot_nt(c16, b16)
    first = iota((SPAN, HC), 1) < HEAD
    zero16 = jnp.zeros((SPAN, HC), BF16)
    dscores = jnp.zeros((SPAN, SPAN), F32)
    dxs = []
    for h in (0, 1):
        own = jnp.where(first, dm16, zero16) if h == 0 else jnp.where(first, zero16, dm16)
        dp = dot_nt(own, xs16)
        dscores = dscores + dp * decays[h]
        dxs.append(dot_tn((scores * decays[h]).astype(BF16), dm16))
    ds16 = dscores.astype(BF16)
    st = st_ref[0]
    dst = dstate[...]
    dst16 = dst.astype(BF16)
    dcs16 = (dm * reach).astype(BF16)
    dc = dot_nn(ds16, b16) + dot_nt(dcs16, st.astype(BF16))
    db = dot_tn(ds16, c16) + dot_nt((xs * tail).astype(BF16), dst16)
    dxs_tail = dot_nn(b16, dst16) * tail
    dxs_all = jnp.where(first, dxs[0], dxs[1]) + dxs_tail
    dstate[...] = dst * carry + dot_tn(c16, dcs16)

    d_total = jnp.sum(xs * dxs_tail, axis=0, keepdims=True) + carry * jnp.sum(
        dst * st, axis=0, keepdims=True
    )
    flow = dm * scan_ref[...] - xs * dxs_all
    rows, cols = iota((SPAN, SPAN), 0), iota((SPAN, SPAN), 1)
    upper = (cols >= rows).astype(F32).astype(BF16)
    flow = exact_left(upper, flow) + d_total
    same_head = ((iota((HC, HC), 0) < HEAD) == (iota((HC, HC), 1) < HEAD)).astype(F32).astype(BF16)
    d_log = exact_right(flow, same_head)
    d_step = exact_right(dxs_all * xc, same_head) - d_log * vec_ref[1:2, :]
    d_alog = jnp.sum(d_log * log_decay, axis=0, keepdims=True)
    d_dt = d_step * sigmoid(dt + vec_ref[0:1, :])
    d_skip = jnp.sum(dm * xc, axis=0, keepdims=True)
    d_xc = dm * vec_ref[2:3, :] + dxs_all * step

    dact = sz * (1.0 + z * (1.0 - sz))
    dzbuf[:SPAN, 0:HC] = d_xc * dact[:, :HC]
    dzbuf[:SPAN, HC : 2 * HC] = db * dact[:, HC : 2 * HC]
    dzbuf[:SPAN, 2 * HC :] = dc * dact[:, 2 * HC :]
    dz = dzbuf[:SPAN, :]
    dv = dz * cw_ref[3:4, :]
    small_ref[3:4, :] += jnp.sum(dz * vbuf[pl.ds(8, SPAN), :], axis=0, keepdims=True)
    small_ref[4:5, :] += jnp.sum(dz, axis=0, keepdims=True)
    for k in (1, 2, 3):
        dv = dv + dzbuf[pl.ds(k, SPAN), :] * cw_ref[3 - k : 4 - k, :] * mask[:, 2 + k : 3 + k]
        small_ref[3 - k : 4 - k, :] += jnp.sum(
            dz * vbuf[pl.ds(8 - k, SPAN), :] * mask[:, k - 1 : k], axis=0, keepdims=True
        )
    dzbuf[SPAN:, :] = dz[:8, :]
    small_ref[5:6, 0:HC] += d_gain
    small_ref[5:6, HC : 2 * HC] += d_skip
    small_ref[6:7, 0:HC] += jnp.sum(d_dt, axis=0, keepdims=True)
    small_ref[6:7, HC : 2 * HC] += d_alog

    lane = iota((SPAN, HC), 1)
    one_each = jnp.where((lane == 0) | (lane == HEAD), d_dt, 0.0)
    gp = jnp.concatenate(
        [dgate.astype(BF16), dv.astype(BF16), one_each.astype(BF16)], axis=1
    )
    part_ref[...] = dot_nt(gp, w_ref[...]).astype(BF16)
    gin_ref[...] += dot_tn(n_ref[...], gp)


def backward_core(cot, n, w, wo, cw, vec, mask, docr, kept):
    length, width = n.shape
    blocks = length // SPAN
    last = blocks - 1

    def rows(cols):
        return pl.BlockSpec((SPAN, cols), lambda i: (last - i, 0))

    def stack(a):
        return pl.BlockSpec((1,) + a.shape[1:], lambda i: (last - i, 0, 0))

    return pl.pallas_call(
        bwd_kernel,
        grid=(blocks,),
        in_specs=[
            rows(width + AUX), rows(width), whole(w.shape), whole(wo.shape), whole(cw.shape),
            whole(vec.shape), rows(mask.shape[1]), pl.BlockSpec((1, SPAN), lambda i: (0, last - i)),
            stack(kept[0]), rows(HC), rows(HC), rows(HC), rows(HC), stack(kept[5]),
        ],
        out_specs=[rows(width), whole(w.shape), whole(wo.shape), whole((8, 3 * HC))],
        out_shape=[
            jax.ShapeDtypeStruct((length, width), BF16),
            jax.ShapeDtypeStruct(w.shape, F32),
            jax.ShapeDtypeStruct(wo.shape, F32),
            jax.ShapeDtypeStruct((8, 3 * HC), F32),
        ],
        scratch_shapes=[pltpu.VMEM((SPAN + 8, 3 * HC), F32), pltpu.VMEM((NS, HC), F32)],
        compiler_params=pltpu.CompilerParams(vmem_limit_bytes=VMEM_ASK),
        name="backward_core",
    )(cot, n, w, wo, cw, vec, mask, docr, *kept)


def greet_all(axis, count, me):
    barrier = pltpu.get_barrier_semaphore()
    for d in range(1, count):
        pl.semaphore_signal(
            barrier, inc=1, device_id={axis: lax.rem(me + d, count)}, device_id_type=MESH
        )
    pl.semaphore_wait(barrier, count - 1)


def spread_kernel(axis, count, x_ref, o_ref, send, recv, own):
    me = lax.axis_index(axis)
    rows = x_ref.shape[0]
    place = o_ref.at[pl.ds(pl.multiple_of(me * rows, rows), rows)]
    mine = pltpu.make_async_copy(x_ref, place, own)
    mine.start()
    greet_all(axis, count, me)
    copies = []
    for d in range(1, count):
        copy = pltpu.make_async_remote_copy(
            src_ref=x_ref, dst_ref=place, send_sem=send.at[d], recv_sem=recv.at[d],
            device_id={axis: lax.rem(me + d, count)}, device_id_type=MESH,
        )
        copy.start()
        copies.append(copy)
    mine.wait()
    for copy in copies:
        copy.wait()


def spread(x, axis, call_id):
    count = lax.axis_size(axis)
    return pl.pallas_call(
        lambda *refs: spread_kernel(axis, count, *refs),
        in_specs=[pl.BlockSpec(memory_space=pl.ANY)],
        out_specs=pl.BlockSpec(memory_space=pl.ANY),
        out_shape=jax.ShapeDtypeStruct((count * x.shape[0],) + x.shape[1:], x.dtype),
        scratch_shapes=[
            pltpu.SemaphoreType.DMA((count,)), pltpu.SemaphoreType.DMA((count,)),
            pltpu.SemaphoreType.DMA,
        ],
        compiler_params=pltpu.CompilerParams(collective_id=call_id, has_side_effects=True),
        name="spread",
    )(x)


def collect_kernel(axis, count, x_ref, o_ref, landing, send, recv, own):
    me = lax.axis_index(axis)
    rows = o_ref.shape[0]

    def block(j):
        return x_ref.at[pl.ds(pl.multiple_of(j * rows, rows), rows)]

    mine = pltpu.make_async_copy(block(me), landing.at[0], own)
    mine.start()
    greet_all(axis, count, me)
    copies = []
    for d in range(1, count):
        to = lax.rem(me + d, count)
        copy = pltpu.make_async_remote_copy(
            src_ref=block(to), dst_ref=landing.at[d], send_sem=send.at[d], recv_sem=recv.at[d],
            device_id={axis: to}, device_id_type=MESH,
        )
        copy.start()
        copies.append(copy)
    mine.wait()
    for copy in copies:
        copy.wait()
    total = landing[0].astype(F32)
    for d in range(1, count):
        total = total + landing[d].astype(F32)
    o_ref[...] = total


def collect(x, axis, call_id):
    count = lax.axis_size(axis)
    rows = x.shape[0] // count
    return pl.pallas_call(
        lambda *refs: collect_kernel(axis, count, *refs),
        in_specs=[pl.BlockSpec(memory_space=pl.ANY)],
        out_specs=pl.BlockSpec(memory_space=pltpu.VMEM),
        out_shape=jax.ShapeDtypeStruct((rows, x.shape[1]), F32),
        scratch_shapes=[
            pltpu.VMEM((count, rows, x.shape[1]), x.dtype),
            pltpu.SemaphoreType.DMA((count,)), pltpu.SemaphoreType.DMA((count,)),
            pltpu.SemaphoreType.DMA,
        ],
        compiler_params=pltpu.CompilerParams(
            collective_id=call_id, has_side_effects=True, vmem_limit_bytes=VMEM_ASK
        ),
        name="collect",
    )(x)


def rms_scale(values, gain):
    return values * lax.rsqrt(jnp.mean(values * values, axis=-1, keepdims=True) + EPS) * gain


def document_masks(doc):
    length = doc.shape[0]
    cols = []
    for k in (1, 2, 3):
        before = jnp.pad(doc, (k, 0), constant_values=-1)[:length]
        cols.append(before == doc)
    for k in (1, 2, 3):
        after = jnp.pad(doc, (0, k), constant_values=-1)[k:]
        cols.append(after == doc)
    blocks = doc.reshape(-1, SPAN)
    previous = jnp.concatenate([doc[:1], blocks[:-1, -1]])
    cols.append((blocks == previous[:, None]).reshape(-1))
    cols.append((blocks == blocks[:, -1:]).reshape(-1))
    cols.append(doc)
    cols = [c.astype(F32) for c in cols]
    cols += [jnp.zeros_like(cols[0])] * (16 - len(cols))
    return jnp.stack(cols, axis=1), doc.astype(F32)[None, :]


def forward_layer(u, n, layer, mask, docr, inner, reduce_rows):
    w, wo, cw, vec, _ = layer
    out = forward_core(n, w, wo, cw, vec, mask, docr)
    summed = reduce_rows(out[0])
    width = u.shape[1]
    square = summed[:, width] + summed[:, width + 1] + summed[:, width + 2]
    r = lax.rsqrt(square / inner + EPS)[:, None]
    branch = summed[:, :width] * r
    return u + branch, (branch, r, out[1:])


def backward_payload(c, branch, r, inner):
    low = c.astype(BF16)
    pull = r * r * jnp.sum(low.astype(F32) * branch, axis=1, keepdims=True) / inner
    hi, mid, lo = three(r)
    phi, pmid, _ = three(pull)
    pad = jnp.zeros((c.shape[0], AUX - 5), BF16)
    return jnp.concatenate([low, hi, mid, lo, phi, pmid, pad], axis=1)


def layer_weights(in_proj, out_proj, conv_weight, conv_bias, dt_bias, a_log, skip_scale, pre_gain, norm_gain, inner, q):
    heads = dt_bias.shape[0]
    def cols(a, start, size):
        return lax.dynamic_slice_in_dim(a, start, size, a.ndim - 1)
    bc = 2 * inner
    wdt = jnp.repeat(cols(in_proj, bc + 2 * NS + 2 * q, 2), HEAD, axis=1)
    w = jnp.concatenate(
        [cols(in_proj, q * HC, HC), cols(in_proj, inner + q * HC, HC),
         in_proj[:, bc : bc + 2 * NS], wdt], axis=1,
    )
    cw = jnp.concatenate([cols(conv_weight, q * HC, HC), conv_weight[:, inner:]], axis=1)
    cb = jnp.concatenate([cols(conv_bias, q * HC, HC), conv_bias[inner:]])
    def lanes(a):
        return jnp.repeat(cols(a, 2 * q, 2), HEAD)
    vec = jnp.stack(
        [lanes(dt_bias), jnp.exp(lanes(a_log)), lanes(skip_scale), cols(norm_gain, q * HC, HC)]
    )
    return w, cw, cb, vec, pre_gain


def body(
    block_input, doc_ids, out_grad, in_proj, out_proj, conv_weight, conv_bias,
    dt_bias, a_log, skip_scale, pre_gain, norm_gain,
):
    part = lax.axis_index("section")
    q = lax.axis_index("seq")
    n_seq = lax.axis_size("seq")
    n_z = lax.axis_size("wshard")
    inner = norm_gain.shape[1]
    width = block_input.shape[3]
    heads = dt_bias.shape[1]

    w, cw, cb, vec, pre = layer_weights(
        in_proj[0], None, conv_weight[0], conv_bias[0], dt_bias[0], a_log[0], skip_scale[0],
        pre_gain[0], norm_gain[0], inner, q,
    )
    out_rows = out_proj.shape[1]
    per_plane = out_rows // HC
    wo = lax.dynamic_slice_in_dim(out_proj[0], lax.rem(q, per_plane) * HC, HC, 0)
    both = ("section", "wshard")
    w_all = lax.all_gather(w, both, axis=0, tiled=True).reshape(2, width, PC)
    wo_all = lax.all_gather(wo, both, axis=0).reshape(2, n_z, HC, width)
    wo_all = lax.dynamic_index_in_dim(wo_all, q // per_plane, 1, keepdims=False)
    small = jnp.concatenate([cw.ravel(), cb, vec.ravel(), pre])
    small_all = lax.all_gather(small, "section", axis=0)
    layers = []
    for l in (0, 1):
        s = small_all[l]
        cwl = jnp.concatenate([s[: 5 * 3 * HC].reshape(5, 3 * HC), jnp.zeros((3, 3 * HC), F32)])
        at = 5 * 3 * HC
        vecl = jnp.concatenate([s[at : at + 4 * HC].reshape(4, HC), jnp.zeros((4, HC), F32)])
        layers.append((w_all[l], wo_all[l], cwl, vecl, s[at + 4 * HC :]))

    doc = lax.dynamic_index_in_dim(doc_ids[:, 0], part, 0, keepdims=False)
    mask, docr = document_masks(doc)
    u = lax.dynamic_index_in_dim(block_input[:, 0], part, 0, keepdims=False).astype(F32)
    cot = lax.dynamic_index_in_dim(out_grad[:, 0], part, 0, keepdims=False).astype(F32)

    inputs, normed, saved, hidden = [], [], [], []
    for l in (0, 1):
        inputs.append(u)
        n = spread(rms_scale(u, layers[l][4]).astype(BF16), "seq", 1)
        normed.append(n)
        u, s = forward_layer(
            u, n, layers[l], mask, docr, inner, lambda x: collect(x, "seq", 2)
        )
        hidden.append(u)
        saved.append(s)

    grads_in, grads = [None, None], [None, None]
    for l in (1, 0):
        branch, r, kept = saved[l]
        w, wo, cwl, vecl, gain = layers[l]
        payload = spread(backward_payload(cot, branch, r, inner), "seq", 3)
        gpart, gin, gout, gsmall = backward_core(
            payload, normed[l], w, wo, cwl, vecl, mask, docr, kept
        )
        g_normed = collect(gpart, "seq", 4)
        _, pull = jax.vjp(rms_scale, inputs[l], gain)
        path, g_pre = pull(g_normed)
        cot = cot + path
        grads_in[l] = cot
        grads[l] = (gin, gout, gsmall, g_pre)

    def swap(a):
        return lax.ppermute(a, "section", [(0, 1), (1, 0)])

    def by_layer(pair):
        mine = jnp.where(part == 0, pair[0], pair[1])
        other = swap(jnp.where(part == 0, pair[1], pair[0]))
        return jnp.where(part == 0, jnp.stack([mine, other]), jnp.stack([other, mine]))

    hidden_out = by_layer(hidden)
    grads_out = by_layer(grads_in)

    def sent_and_summed(x, axis):
        arrived = lax.all_to_all(x, axis, split_axis=0, concat_axis=0, tiled=True)
        return arrived.astype(F32).sum(axis=0)

    n_rows = width // n_z
    gin = jnp.stack([grads[0][0], grads[1][0]]).astype(BF16).reshape(2 * n_z, n_rows * PC)
    gout = jnp.stack([grads[0][1], grads[1][1]]).astype(BF16).reshape(2 * n_z, -1)
    piece = HC // n_z
    summed = sent_and_summed(jnp.concatenate([gin, gout], axis=1), both)
    gin = summed[: n_rows * PC].reshape(n_rows, PC)
    gout = summed[n_rows * PC :].reshape(piece, width).astype(BF16)
    n_y = n_seq // per_plane
    route = []
    for y in range(n_y):
        for x in range(per_plane):
            for z in range(n_z):
                route.append(((y * per_plane + x) * n_z + z, (z * per_plane + x) * n_z + y))
    gout = lax.ppermute(gout, ("seq", "wshard"), route)
    g_bc = gin[:, 2 * HC : 4 * HC].astype(BF16).reshape(n_seq, -1)
    g_bc = sent_and_summed(g_bc, "seq").astype(BF16)
    g_own = jnp.concatenate([gin[:, : 2 * HC], gin[:, 4 * HC :: HEAD]], axis=1).astype(BF16)
    flat = jnp.concatenate([g_own.ravel(), g_bc, gout.ravel()])
    everyone = lax.all_gather(flat, "seq", axis=0)
    own = everyone[:, : g_own.size].reshape(n_seq, n_rows, -1)
    own = jnp.moveaxis(own, 0, 1).astype(F32)
    shard_in = jnp.concatenate(
        [
            own[:, :, :HC].reshape(n_rows, -1),
            own[:, :, HC : 2 * HC].reshape(n_rows, -1),
            everyone[:, g_own.size : g_own.size + g_bc.size].reshape(n_rows, -1).astype(F32),
            own[:, :, 2 * HC :].reshape(n_rows, -1),
        ],
        axis=1,
    )
    shard_out = everyone[:, g_own.size + g_bc.size :].reshape(n_z, per_plane, piece, width)
    shard_out = jnp.moveaxis(shard_out, 0, 1).reshape(out_rows, width).astype(F32)

    def placed(values, extent, start):
        full = jnp.zeros(values.shape[:-1] + (extent,), F32)
        return lax.dynamic_update_slice_in_dim(full, values, start, values.ndim - 1)

    def small_vector(g):
        _, _, s, g_pre = g
        conv = jnp.concatenate([placed(s[:5, :HC], inner, q * HC), s[:5, HC:]], axis=1)
        per_head = jnp.stack([
            s[6, 0:HC:HEAD],
            s[6, HC : 2 * HC : HEAD],
            s[5, HC : 2 * HC].reshape(-1, HEAD).sum(axis=1),
        ])
        return jnp.concatenate([
            conv.ravel(), placed(per_head, heads, 2 * q).ravel(), g_pre,
            placed(s[5, :HC], inner, q * HC),
        ])

    vectors = [small_vector(g) for g in grads]
    mine = jnp.where(part == 0, vectors[0], vectors[1])
    mine = mine + swap(jnp.where(part == 0, vectors[1], vectors[0]))
    sums = lax.psum(mine, ("seq", "wshard"))
    channels = conv_weight.shape[2]
    at = 0
    pieces = []
    for shape in (
        conv_weight.shape[1:], (channels,), (heads,), (heads,), (heads,), (width,), (inner,)
    ):
        size = 1
        for extent in shape:
            size *= extent
        pieces.append(sums[at : at + size].reshape((1,) + shape))
        at += size
    return (
        hidden_out[None, :, None], grads_out[None, :, None], shard_in[None], shard_out[None],
        *pieces,
    )


def solution(mesh):
    specs = (
        P(None, "wshard", "seq", None),
        P(None, "wshard", None),
        P(None, "wshard", "seq", None),
        P("section", "wshard", None),
        P("section", "wshard", None),
        P("section", None, None),
        P("section", None),
        P("section", None),
        P("section", None),
        P("section", None),
        P("section", None),
        P("section", None),
    )
    outs = (
        P("section", None, "wshard", "seq", None),
        P("section", None, "wshard", "seq", None),
        P("section", "wshard", None),
        P("section", "wshard", None),
        P("section", None, None),
    ) + (P("section", None),) * 6
    return jax.shard_map(body, mesh=mesh, in_specs=specs, out_specs=outs, check_vma=False)
```

```python
import jax
import jax.numpy as jnp
from jax import lax
from jax.experimental import pallas as pl
from jax.experimental.pallas import tpu as pltpu
from jax.sharding import PartitionSpec as P

SPAN = 256
EPS = 1e-05
F32 = jnp.float32
BF16 = jnp.bfloat16
MESH = pl.DeviceIdType.MESH
VMEM_ASK = 48 * 1024 * 1024

HC = 128
NS = 128
PC = 640
AUX = 128
HEAD = 64
SIDE = 4
SPREAD_SPACE = pltpu.VMEM


def dot_nn(a, b):
    return lax.dot_general(a, b, (((1,), (0,)), ((), ())), preferred_element_type=F32)


def dot_nt(a, b):
    return lax.dot_general(a, b, (((1,), (1,)), ((), ())), preferred_element_type=F32)


def dot_tn(a, b):
    return lax.dot_general(a, b, (((0,), (0,)), ((), ())), preferred_element_type=F32)


def three(x):
    hi = x.astype(BF16)
    rest = x - hi.astype(F32)
    mid = rest.astype(BF16)
    low = (rest - mid.astype(F32)).astype(BF16)
    return hi, mid, low


def exact_left(ones, x):
    hi, mid, low = three(x)
    return dot_nn(ones, hi) + dot_nn(ones, mid) + dot_nn(ones, low)


def exact_right(x, ones):
    hi, mid, low = three(x)
    return dot_nn(hi, ones) + dot_nn(mid, ones) + dot_nn(low, ones)


def iota(shape, dim):
    return lax.broadcasted_iota(jnp.int32, shape, dim)


def sigmoid(x):
    return 1.0 / (1.0 + jnp.exp(-x))


def softplus(x):
    return jnp.maximum(x, 0.0) + jnp.log1p(jnp.exp(-jnp.abs(x)))


def conv_rows(vbuf, cw_ref, mask):
    z = vbuf[pl.ds(8, SPAN), :] * cw_ref[3:4, :] + cw_ref[4:5, :]
    for k in (1, 2, 3):
        z = z + vbuf[pl.ds(8 - k, SPAN), :] * cw_ref[3 - k : 4 - k, :] * mask[:, k - 1 : k]
    return z


def block_terms(dt, vec_ref, mask, docr_ref):
    step = softplus(dt + vec_ref[0:1, :])
    log_decay = -step * vec_ref[1:2, :]
    rows, cols = iota((SPAN, SPAN), 0), iota((SPAN, SPAN), 1)
    lower = rows >= cols
    running = exact_left(lower.astype(F32).astype(BF16), log_decay)
    turned = running.T
    allowed = lower & (mask[:, 8:9] == docr_ref[...])
    decays = []
    for h in (0, 1):
        gaps = running[:, h * HEAD : h * HEAD + 1] - turned[h * HEAD : h * HEAD + 1, :]
        decays.append(jnp.exp(jnp.where(allowed, gaps, -1e30)))
    reach = jnp.exp(running) * mask[:, 6:7]
    total = running[SPAN - 1 :, :]
    tail = jnp.exp(total - running) * mask[:, 7:8]
    carry = jnp.exp(total) * mask[SPAN - 1 :, 6:7]
    return step, log_decay, decays, reach, tail, carry


def fwd_kernel(
    n_ref, w_ref, wo_ref, cw_ref, vec_ref, mask_ref, docr_ref,
    part_ref, vh_ref, gate_ref, dt_ref, mix_ref, scan_ref, st_ref,
    vbuf, state,
):
    @pl.when(pl.program_id(0) == 0)
    def _():
        vbuf[0:8, :] = jnp.zeros((8, 3 * HC), F32)
        state[...] = jnp.zeros_like(state)

    mask = mask_ref[...]
    proj = dot_nn(n_ref[...], w_ref[...])
    gate = proj[:, :HC]
    v = proj[:, HC : 4 * HC].astype(BF16).astype(F32)
    dt = proj[:, 4 * HC :].astype(BF16).astype(F32)
    vbuf[8:, :] = v
    z = conv_rows(vbuf, cw_ref, mask)
    vh_ref[0] = vbuf[...]
    vbuf[0:8, :] = v[SPAN - 8 :, :]
    act = z * sigmoid(z)
    xc = act[:, :HC]
    b16 = act[:, HC : 2 * HC].astype(BF16)
    c16 = act[:, 2 * HC :].astype(BF16)
    step, _, decays, reach, tail, carry = block_terms(dt, vec_ref, mask, docr_ref)
    xs = xc * step
    xs16 = xs.astype(BF16)
    scores = dot_nt(c16, b16)
    within = [dot_nn((scores * d).astype(BF16), xs16) for d in decays]
    first = iota((SPAN, HC), 1) < HEAD
    st = state[...]
    st_ref[0] = st
    scan = jnp.where(first, within[0], within[1]) + dot_nn(c16, st.astype(BF16)) * reach
    state[...] = st * carry + dot_tn(b16, (xs * tail).astype(BF16))
    mixed = (scan + xc * vec_ref[2:3, :]).astype(BF16)
    g = mixed.astype(F32) * (gate * sigmoid(gate))
    part_ref[:, : wo_ref.shape[1]] = dot_nn(
        (g * vec_ref[3:4, :]).astype(BF16), wo_ref[...]
    ).astype(BF16)
    hi, mid, low = three(jnp.sum(g * g, axis=1, keepdims=True))
    lane = iota((SPAN, AUX), 1)
    aux = jnp.where(lane == 0, hi.astype(F32), 0.0)
    aux = jnp.where(lane == 1, mid.astype(F32), aux)
    aux = jnp.where(lane == 2, low.astype(F32), aux)
    part_ref[:, wo_ref.shape[1] :] = aux.astype(BF16)
    gate_ref[...] = gate
    dt_ref[...] = dt
    mix_ref[...] = mixed
    scan_ref[...] = scan


def whole(shape):
    return pl.BlockSpec(shape, lambda i: (0,) * len(shape))


def forward_core(n, w, wo, cw, vec, mask, docr):
    length, width = n.shape
    blocks = length // SPAN

    def rows(cols):
        return pl.BlockSpec((SPAN, cols), lambda i: (i, 0))

    return pl.pallas_call(
        fwd_kernel,
        grid=(blocks,),
        in_specs=[
            rows(width), whole(w.shape), whole(wo.shape), whole(cw.shape), whole(vec.shape),
            rows(mask.shape[1]), pl.BlockSpec((1, SPAN), lambda i: (0, i)),
        ],
        out_specs=[
            rows(width + AUX),
            pl.BlockSpec((1, SPAN + 8, 3 * HC), lambda i: (i, 0, 0)),
            rows(HC), rows(HC), rows(HC), rows(HC),
            pl.BlockSpec((1, NS, HC), lambda i: (i, 0, 0)),
        ],
        out_shape=[
            jax.ShapeDtypeStruct((length, width + AUX), BF16),
            jax.ShapeDtypeStruct((blocks, SPAN + 8, 3 * HC), F32),
            jax.ShapeDtypeStruct((length, HC), F32),
            jax.ShapeDtypeStruct((length, HC), F32),
            jax.ShapeDtypeStruct((length, HC), BF16),
            jax.ShapeDtypeStruct((length, HC), F32),
            jax.ShapeDtypeStruct((blocks, NS, HC), F32),
        ],
        scratch_shapes=[pltpu.VMEM((SPAN + 8, 3 * HC), F32), pltpu.VMEM((NS, HC), F32)],
        compiler_params=pltpu.CompilerParams(vmem_limit_bytes=VMEM_ASK),
        name="forward_core",
    )(n, w, wo, cw, vec, mask, docr)


def bwd_kernel(
    c_ref, n_ref, w_ref, wo_ref, cw_ref, vec_ref, mask_ref, docr_ref,
    vh_ref, gate_ref, dt_ref, mix_ref, scan_ref, st_ref,
    part_ref, gin_ref, gout_ref, small_ref,
    dzbuf, dstate,
):
    @pl.when(pl.program_id(0) == 0)
    def _():
        dzbuf[SPAN:, :] = jnp.zeros((8, 3 * HC), F32)
        dstate[...] = jnp.zeros_like(dstate)
        gin_ref[...] = jnp.zeros_like(gin_ref)
        gout_ref[...] = jnp.zeros_like(gout_ref)
        small_ref[...] = jnp.zeros_like(small_ref)

    width = wo_ref.shape[1]
    mask = mask_ref[...]
    cot = c_ref[:, :width]
    aux = c_ref[:, width:].astype(F32)
    r = aux[:, 0:1] + aux[:, 1:2] + aux[:, 2:3]
    pull = aux[:, 3:4] + aux[:, 4:5]
    gate = gate_ref[...]
    sg = sigmoid(gate)
    silu = gate * sg
    mixed = mix_ref[...].astype(F32)
    g = mixed * silu
    gain = vec_ref[3:4, :]
    dy = dot_nt(cot, wo_ref[...])
    gr = g * r
    gout_ref[...] += dot_tn((gr * gain).astype(BF16), cot)
    d_gain = jnp.sum(dy * gr, axis=0, keepdims=True)
    dg = dy * (r * gain) - g * pull
    dm16 = (dg * silu).astype(BF16)
    dm = dm16.astype(F32)
    dgate = dg * mixed * (sg * (1.0 + gate * (1.0 - sg)))

    vbuf = vh_ref.at[0]
    z = conv_rows(vbuf, cw_ref, mask)
    sz = sigmoid(z)
    act = z * sz
    xc = act[:, :HC]
    b16 = act[:, HC : 2 * HC].astype(BF16)
    c16 = act[:, 2 * HC :].astype(BF16)
    dt = dt_ref[...]
    step, log_decay, decays, reach, tail, carry = block_terms(dt, vec_ref, mask, docr_ref)
    xs16 = (xc * step).astype(BF16)
    xs = xs16.astype(F32)
    scores = dot_nt(c16, b16)
    first = iota((SPAN, HC), 1) < HEAD
    zero16 = jnp.zeros((SPAN, HC), BF16)
    dscores = jnp.zeros((SPAN, SPAN), F32)
    dxs = []
    for h in (0, 1):
        own = jnp.where(first, dm16, zero16) if h == 0 else jnp.where(first, zero16, dm16)
        dp = dot_nt(own, xs16)
        dscores = dscores + dp * decays[h]
        dxs.append(dot_tn((scores * decays[h]).astype(BF16), dm16))
    ds16 = dscores.astype(BF16)
    st = st_ref[0]
    dst = dstate[...]
    dst16 = dst.astype(BF16)
    dcs16 = (dm * reach).astype(BF16)
    dc = dot_nn(ds16, b16) + dot_nt(dcs16, st.astype(BF16))
    db = dot_tn(ds16, c16) + dot_nt((xs * tail).astype(BF16), dst16)
    dxs_tail = dot_nn(b16, dst16) * tail
    dxs_all = jnp.where(first, dxs[0], dxs[1]) + dxs_tail
    dstate[...] = dst * carry + dot_tn(c16, dcs16)

    d_total = jnp.sum(xs * dxs_tail, axis=0, keepdims=True) + carry * jnp.sum(
        dst * st, axis=0, keepdims=True
    )
    flow = dm * scan_ref[...] - xs * dxs_all
    rows, cols = iota((SPAN, SPAN), 0), iota((SPAN, SPAN), 1)
    upper = (cols >= rows).astype(F32).astype(BF16)
    flow = exact_left(upper, flow) + d_total
    same_head = ((iota((HC, HC), 0) < HEAD) == (iota((HC, HC), 1) < HEAD)).astype(F32).astype(BF16)
    d_log = exact_right(flow, same_head)
    d_step = exact_right(dxs_all * xc, same_head) - d_log * vec_ref[1:2, :]
    d_alog = jnp.sum(d_log * log_decay, axis=0, keepdims=True)
    d_dt = d_step * sigmoid(dt + vec_ref[0:1, :])
    d_skip = jnp.sum(dm * xc, axis=0, keepdims=True)
    d_xc = dm * vec_ref[2:3, :] + dxs_all * step

    dact = sz * (1.0 + z * (1.0 - sz))
    dzbuf[:SPAN, 0:HC] = d_xc * dact[:, :HC]
    dzbuf[:SPAN, HC : 2 * HC] = db * dact[:, HC : 2 * HC]
    dzbuf[:SPAN, 2 * HC :] = dc * dact[:, 2 * HC :]
    dz = dzbuf[:SPAN, :]
    dv = dz * cw_ref[3:4, :]
    small_ref[3:4, :] += jnp.sum(dz * vbuf[pl.ds(8, SPAN), :], axis=0, keepdims=True)
    small_ref[4:5, :] += jnp.sum(dz, axis=0, keepdims=True)
    for k in (1, 2, 3):
        dv = dv + dzbuf[pl.ds(k, SPAN), :] * cw_ref[3 - k : 4 - k, :] * mask[:, 2 + k : 3 + k]
        small_ref[3 - k : 4 - k, :] += jnp.sum(
            dz * vbuf[pl.ds(8 - k, SPAN), :] * mask[:, k - 1 : k], axis=0, keepdims=True
        )
    dzbuf[SPAN:, :] = dz[:8, :]
    small_ref[5:6, 0:HC] += d_gain
    small_ref[5:6, HC : 2 * HC] += d_skip
    small_ref[6:7, 0:HC] += jnp.sum(d_dt, axis=0, keepdims=True)
    small_ref[6:7, HC : 2 * HC] += d_alog

    lane = iota((SPAN, HC), 1)
    one_each = jnp.where((lane == 0) | (lane == HEAD), d_dt, 0.0)
    gp = jnp.concatenate(
        [dgate.astype(BF16), dv.astype(BF16), one_each.astype(BF16)], axis=1
    )
    part_ref[...] = dot_nt(gp, w_ref[...]).astype(BF16)
    gin_ref[...] += dot_tn(n_ref[...], gp)


def backward_core(cot, n, w, wo, cw, vec, mask, docr, kept):
    length, width = n.shape
    blocks = length // SPAN
    last = blocks - 1

    def rows(cols):
        return pl.BlockSpec((SPAN, cols), lambda i: (last - i, 0))

    def stack(a):
        return pl.BlockSpec((1,) + a.shape[1:], lambda i: (last - i, 0, 0))

    return pl.pallas_call(
        bwd_kernel,
        grid=(blocks,),
        in_specs=[
            rows(width + AUX), rows(width), whole(w.shape), whole(wo.shape), whole(cw.shape),
            whole(vec.shape), rows(mask.shape[1]), pl.BlockSpec((1, SPAN), lambda i: (0, last - i)),
            stack(kept[0]), rows(HC), rows(HC), rows(HC), rows(HC), stack(kept[5]),
        ],
        out_specs=[rows(width), whole(w.shape), whole(wo.shape), whole((8, 3 * HC))],
        out_shape=[
            jax.ShapeDtypeStruct((length, width), BF16),
            jax.ShapeDtypeStruct(w.shape, F32),
            jax.ShapeDtypeStruct(wo.shape, F32),
            jax.ShapeDtypeStruct((8, 3 * HC), F32),
        ],
        scratch_shapes=[pltpu.VMEM((SPAN + 8, 3 * HC), F32), pltpu.VMEM((NS, HC), F32)],
        compiler_params=pltpu.CompilerParams(vmem_limit_bytes=VMEM_ASK),
        name="backward_core",
    )(cot, n, w, wo, cw, vec, mask, docr, *kept)


def ring_places(axis):
    me = lax.axis_index(axis)
    return me % SIDE, me // SIDE


def place_of(half, f, s):
    f, s = lax.rem(f, SIDE), lax.rem(s, SIDE)
    return s * SIDE + f if half == 0 else f * SIDE + s


def greet_neighbours(axis, x, y):
    barrier = pltpu.get_barrier_semaphore()
    for dx, dy in ((1, 0), (3, 0), (0, 1), (0, 3)):
        pl.semaphore_signal(
            barrier, inc=1, device_id={axis: place_of(0, x + dx, y + dy)}, device_id_type=MESH
        )
    pl.semaphore_wait(barrier, 4)


def rows_at(ref, start, size):
    return ref.at[pl.ds(pl.multiple_of(start, 16), size)]


def spread_kernel(axis, x_ref, o_ref, send, recv, own):
    x, y = ring_places(axis)
    greet_neighbours(axis, x, y)
    spread_steps(axis, x_ref, o_ref, send, recv, own)


def spread_steps(axis, x_ref, o_ref, send, recv, own):
    x, y = ring_places(axis)
    rows = x_ref.shape[0]
    half_rows, quarter = rows // 2, rows // 4
    mine = pltpu.make_async_copy(x_ref, rows_at(o_ref, place_of(0, x, y) * rows, rows), own)
    mine.start()
    copies = {}

    def go(name, half, block, offset, size, to, source=None):
        index = len(copies)
        place = rows_at(o_ref, block * rows + half * half_rows + offset, size)
        copy = pltpu.make_async_remote_copy(
            src_ref=place if source is None else source, dst_ref=place,
            send_sem=send.at[index], recv_sem=recv.at[index],
            device_id={axis: to}, device_id_type=MESH,
        )
        copy.start()
        copies[half, name] = copy

    firsts = ((x, y), (y, x))

    def across(half, d):
        f, s = firsts[half]
        block = place_of(half, f + d, s)
        source = None
        if d == 0:
            source = x_ref.at[pl.ds(half * half_rows, half_rows)]
        go(("t1", d), half, block, 0, half_rows, place_of(half, f, s + 1), source)
        go(("t2", d), half, block, 0, half_rows, place_of(half, f, s + 3), source)

    def onward(half, d):
        f, s = firsts[half]
        copies[half, ("t1", d)].wait_recv()
        go(("u1", d), half, place_of(half, f + d, s + 3), 0, quarter, place_of(half, f, s + 1))
        copies[half, ("t2", d)].wait_recv()
        go(("u2", d), half, place_of(half, f + d, s + 1), quarter, quarter, place_of(half, f, s + 3))

    for half in (0, 1):
        f, s = firsts[half]
        source = x_ref.at[pl.ds(half * half_rows, half_rows)]
        block = place_of(half, f, s)
        go("s1", half, block, 0, half_rows, place_of(half, f + 1, s), source)
        go("s2", half, block, 0, half_rows, place_of(half, f + 3, s), source)
    for half in (0, 1):
        across(half, 0)
    for half in (0, 1):
        f, s = firsts[half]
        copies[half, "s1"].wait_recv()
        go("s3", half, place_of(half, f + 3, s), 0, quarter, place_of(half, f + 1, s))
        copies[half, "s2"].wait_recv()
        go("s4", half, place_of(half, f + 1, s), quarter, quarter, place_of(half, f + 3, s))
    for half in (0, 1):
        across(half, 3)
        across(half, 1)
    for half in (0, 1):
        onward(half, 0)
    for half in (0, 1):
        copies[half, "s3"].wait_recv()
        copies[half, "s4"].wait_recv()
        across(half, 2)
    for d in (3, 1, 2):
        for half in (0, 1):
            onward(half, d)
    for half in (0, 1):
        for d in range(SIDE):
            copies[half, ("u1", d)].wait_recv()
            copies[half, ("u2", d)].wait_recv()
    for copy in copies.values():
        copy.wait_send()
    mine.wait()


def spread(x, axis, call_id):
    count = lax.axis_size(axis)
    return pl.pallas_call(
        lambda *refs: spread_kernel(axis, *refs),
        in_specs=[pl.BlockSpec(memory_space=SPREAD_SPACE)],
        out_specs=pl.BlockSpec(memory_space=SPREAD_SPACE),
        out_shape=jax.ShapeDtypeStruct((count * x.shape[0],) + x.shape[1:], x.dtype),
        scratch_shapes=[
            pltpu.SemaphoreType.DMA((40,)), pltpu.SemaphoreType.DMA((40,)),
            pltpu.SemaphoreType.DMA,
        ],
        compiler_params=pltpu.CompilerParams(
            collective_id=call_id, has_side_effects=True, vmem_limit_bytes=VMEM_ASK
        ),
        name="spread",
    )(x)


def collect_kernel(axis, x_ref, o_ref, far, near, stage, reduced, far2, near2, stage2, send, recv):
    x, y = ring_places(axis)
    rows = o_ref.shape[0]
    half_rows, quarter = rows // 2, rows // 4
    greet_neighbours(axis, x, y)
    copies = {}
    firsts = ((x, y), (y, x))
    order = (2, 1, 3, 0)

    def go(name, half, source, target, to):
        index = len(copies)
        copy = pltpu.make_async_remote_copy(
            src_ref=source, dst_ref=target, send_sem=send.at[index], recv_sem=recv.at[index],
            device_id={axis: to}, device_id_type=MESH,
        )
        copy.start()
        copies[half, name] = copy

    def start_of(half, f, s):
        return pl.multiple_of(place_of(half, f, s) * rows + half * half_rows, 16)

    for d in order:
        for half in (0, 1):
            f, s = firsts[half]
            start = start_of(half, f + d, s + 2)
            go(("a1", d), half, rows_at(x_ref, start, quarter), far.at[half, d, 0],
               place_of(half, f, s + 1))
            go(("a2", d), half, rows_at(x_ref, start + quarter, quarter), far.at[half, d, 1],
               place_of(half, f, s + 3))
    for d in order:
        for half in (0, 1):
            f, s = firsts[half]
            for side, (step, other) in enumerate(((1, 0), (3, 1))):
                start = start_of(half, f + d, s + step)
                plain = quarter * (1 - side)
                through = quarter * side
                stage[half, d, side, pl.ds(plain, quarter)] = x_ref[
                    pl.ds(pl.multiple_of(start + plain, 16), quarter), :
                ]
                copies[half, (("a1", "a2")[side], d)].wait_recv()
                stage[half, d, side, pl.ds(through, quarter)] = (
                    x_ref[pl.ds(pl.multiple_of(start + through, 16), quarter), :].astype(F32)
                    + far[half, d, side].astype(F32)
                ).astype(BF16)
                go((("b1", "b2")[side], d), half, stage.at[half, d, side], near.at[half, d, side],
                   place_of(half, f, s + step))

    def reduce_second(half, d):
        f, s = firsts[half]
        copies[half, ("b1", d)].wait_recv()
        copies[half, ("b2", d)].wait_recv()
        reduced[half, d] = (
            x_ref[pl.ds(start_of(half, f + d, s), half_rows), :].astype(F32)
            + near[half, d, 0].astype(F32) + near[half, d, 1].astype(F32)
        )

    for half in (0, 1):
        f, s = firsts[half]
        reduce_second(half, 2)
        stage2[half, 2] = reduced[half, 2].astype(BF16)
        go("c1", half, stage2.at[half, 2, pl.ds(0, quarter)], far2.at[half, 0],
           place_of(half, f + 1, s))
        go("c2", half, stage2.at[half, 2, pl.ds(quarter, quarter)], far2.at[half, 1],
           place_of(half, f + 3, s))
    for d, side in ((1, 0), (3, 1)):
        for half in (0, 1):
            f, s = firsts[half]
            reduce_second(half, d)
            plain, through = quarter * (1 - side), quarter * side
            copies[half, ("c1", "c2")[side]].wait_recv()
            stage2[half, side, pl.ds(plain, quarter)] = reduced[
                half, d, pl.ds(plain, quarter)
            ].astype(BF16)
            stage2[half, side, pl.ds(through, quarter)] = (
                reduced[half, d, pl.ds(through, quarter)] + far2[half, side].astype(F32)
            ).astype(BF16)
            go(("d1", "d2")[side], half, stage2.at[half, side], near2.at[half, side],
               place_of(half, f + d, s))
    for half in (0, 1):
        reduce_second(half, 0)
        copies[half, "d1"].wait_recv()
        copies[half, "d2"].wait_recv()
        o_ref[pl.ds(half * half_rows, half_rows), :] = (
            reduced[half, 0] + near2[half, 0].astype(F32) + near2[half, 1].astype(F32)
        )
    for copy in copies.values():
        copy.wait_send()


def collect(x, axis, call_id):
    count = lax.axis_size(axis)
    rows, cols = x.shape[0] // count, x.shape[1]
    half_rows, quarter = rows // 2, rows // 4
    return pl.pallas_call(
        lambda *refs: collect_kernel(axis, *refs),
        in_specs=[pl.BlockSpec(memory_space=pltpu.VMEM)],
        out_specs=pl.BlockSpec(memory_space=pltpu.VMEM),
        out_shape=jax.ShapeDtypeStruct((rows, cols), F32),
        scratch_shapes=[
            pltpu.VMEM((2, SIDE, 2, quarter, cols), x.dtype),
            pltpu.VMEM((2, SIDE, 2, half_rows, cols), x.dtype),
            pltpu.VMEM((2, SIDE, 2, half_rows, cols), x.dtype),
            pltpu.VMEM((2, SIDE, half_rows, cols), F32),
            pltpu.VMEM((2, 2, quarter, cols), x.dtype),
            pltpu.VMEM((2, 2, half_rows, cols), x.dtype),
            pltpu.VMEM((2, 3, half_rows, cols), x.dtype),
            pltpu.SemaphoreType.DMA((40,)), pltpu.SemaphoreType.DMA((40,)),
        ],
        compiler_params=pltpu.CompilerParams(
            collective_id=call_id, has_side_effects=True, vmem_limit_bytes=VMEM_ASK
        ),
        name="collect",
    )(x)


def greet(axis_steps):
    barrier = pltpu.get_barrier_semaphore()
    for target in axis_steps:
        pl.semaphore_signal(barrier, inc=1, device_id=target, device_id_type=MESH)
    pl.semaphore_wait(barrier, len(axis_steps))


def ring_neighbours(axis, x, y):
    steps = ((1, 0), (3, 0), (0, 1), (0, 3))
    return [{axis: place_of(0, x + dx, y + dy)} for dx, dy in steps]


def plane_neighbours():
    z = lax.axis_index("wshard")
    return [{"wshard": lax.rem(z + 1, SIDE)}, {"wshard": lax.rem(z + 3, SIDE)}]


def other_core():
    return {"section": 1 - lax.axis_index("section")}


class Sender:
    def __init__(self, send, recv):
        self.send, self.recv, self.used, self.copies = send, recv, 0, {}

    def make(self, name, source, target, to):
        copy = pltpu.make_async_remote_copy(
            src_ref=source, dst_ref=target, send_sem=self.send.at[self.used],
            recv_sem=self.recv.at[self.used], device_id=to, device_id_type=MESH,
        )
        self.used += 1
        self.copies[name] = copy
        return copy

    def go(self, name, source, target, to):
        self.make(name, source, target, to).start()

    def arrived(self, name):
        self.copies[name].wait_recv()

    def sent(self):
        for copy in self.copies.values():
            copy.wait_send()


def opening_kernel(
    axis, x_ref, w_ref, wo_ref, o_ref, wall_ref, woall_ref,
    send, recv, own, send2, recv2, own2,
):
    x, y = ring_places(axis)
    part, z = lax.axis_index("section"), lax.axis_index("wshard")
    up, down = plane_neighbours()
    greet(ring_neighbours(axis, x, y) + [up, down, other_core()])
    rows = w_ref.shape[0]
    half = rows // 2
    half_wo = wo_ref.shape[0] // 2
    planes = Sender(send2, recv2)

    def held(at, offset=0, size=rows):
        return wall_ref.at[part, pl.ds(pl.multiple_of(lax.rem(at, SIDE) * rows + offset, 16), size)]

    mine = pltpu.make_async_copy(w_ref, held(z), own2.at[0])
    mine.start()
    planes.go("up", w_ref, held(z), up)
    planes.go("down", w_ref, held(z), down)
    role = lax.rem(z - y + SIDE, SIDE)
    woown = woall_ref.at[part]
    first, second = woown.at[pl.ds(0, half_wo)], woown.at[pl.ds(half_wo, half_wo)]
    rows_mine = pltpu.make_async_copy(wo_ref, woown, own2.at[1])
    rows_up = planes.make("wo_up", wo_ref, woown, up)
    rows_down = planes.make("wo_down", wo_ref, woown, down)
    on_up = planes.make("wo_on_up", first, first, up)
    on_down = planes.make("wo_on_down", second, second, down)
    swap_wo = planes.make("swap_wo", woown, woown, other_core())

    @pl.when(role == 0)
    def _():
        rows_mine.start()
        rows_up.start()
        rows_down.start()

    spread_steps(axis, x_ref, o_ref, send, recv, own)

    planes.arrived("up")
    planes.go("on_up", held(z + 3, 0, half), held(z + 3, 0, half), up)
    planes.arrived("down")
    planes.go("on_down", held(z + 1, half, half), held(z + 1, half, half), down)

    @pl.when(role == 1)
    def _():
        rows_up.wait_recv()
        on_up.start()

    @pl.when(role == 3)
    def _():
        rows_down.wait_recv()
        on_down.start()

    mine.wait()
    for k, at in enumerate((z, z + 3, z + 1)):
        planes.go(("swap", k), held(at), held(at), other_core())

    @pl.when(role == 0)
    def _():
        rows_mine.wait()

    @pl.when(role == 2)
    def _():
        on_up.wait_recv()
        on_down.wait_recv()

    swap_wo.start()
    planes.arrived("on_up")
    planes.arrived("on_down")
    planes.go(("swap", 3), held(z + 2), held(z + 2), other_core())
    for k in range(SIDE):
        planes.arrived(("swap", k))
    swap_wo.wait_recv()

    @pl.when(role == 0)
    def _():
        rows_up.wait_send()
        rows_down.wait_send()

    @pl.when(role == 1)
    def _():
        on_up.wait_send()

    @pl.when(role == 3)
    def _():
        on_down.wait_send()

    for name, copy in planes.copies.items():
        if name not in ("wo_up", "wo_down", "wo_on_up", "wo_on_down"):
            copy.wait_send()


def opening(x, w, wo, axis, call_id):
    count = lax.axis_size(axis)
    vmem = pl.BlockSpec(memory_space=pltpu.VMEM)
    return pl.pallas_call(
        lambda *refs: opening_kernel(axis, *refs),
        in_specs=[vmem] * 3,
        out_specs=[vmem] * 3,
        out_shape=[
            jax.ShapeDtypeStruct((count * x.shape[0], x.shape[1]), x.dtype),
            jax.ShapeDtypeStruct((2, SIDE * w.shape[0], w.shape[1]), w.dtype),
            jax.ShapeDtypeStruct((2,) + wo.shape, wo.dtype),
        ],
        scratch_shapes=[
            pltpu.SemaphoreType.DMA((40,)), pltpu.SemaphoreType.DMA((40,)),
            pltpu.SemaphoreType.DMA,
            pltpu.SemaphoreType.DMA((16,)), pltpu.SemaphoreType.DMA((16,)),
            pltpu.SemaphoreType.DMA((2,)),
        ],
        compiler_params=pltpu.CompilerParams(
            collective_id=call_id, has_side_effects=True, vmem_limit_bytes=VMEM_ASK
        ),
        name="opening",
    )(x, w, wo)


def fold_kernel(
    gin_ref, gout_ref, small_ref, gin2_ref, gout2_ref, small2_ref,
    fin_ref, fout_ref, fsmall_ref,
    land_in, land_out, land_small, sum_in, sum_out, sum_small,
    far_in, far_out, near_in, near_out, all_small, send, recv,
):
    z = lax.axis_index("wshard")
    up, down = plane_neighbours()
    across = {"wshard": lax.rem(z + 2, SIDE)}
    greet([up, down, across, other_core()])
    out = Sender(send, recv)
    arrays = (
        (gin_ref, gin2_ref, land_in, sum_in, far_in, near_in, fin_ref),
        (gout_ref, gout2_ref, land_out, sum_out, far_out, near_out, fout_ref),
    )

    def block(ref, d, offset=0, size=None):
        rows = ref.shape[0] // SIDE
        start = lax.rem(z + d, SIDE) * rows + offset
        return pl.ds(pl.multiple_of(start, 16), rows if size is None else size)

    for d in (2, 1, 3, 0):
        for k, (_, theirs, land, *_) in enumerate(arrays):
            out.go(("swap", k, d), theirs.at[block(theirs, d)], land.at[block(theirs, d)], other_core())
    out.go("small", small2_ref, land_small, other_core())

    def add_cores(d):
        for k, (ours, _, land, total, *_) in enumerate(arrays):
            out.arrived(("swap", k, d))
            at = block(ours, d)
            total[at, :] = (ours[at, :].astype(F32) + land[at, :].astype(F32)).astype(BF16)

    add_cores(2)
    for k, (_, _, _, total, far, _, _) in enumerate(arrays):
        half = total.shape[0] // SIDE // 2
        out.go(("far1", k), total.at[block(total, 2, 0, half)], far.at[0], up)
        out.go(("far2", k), total.at[block(total, 2, half, half)], far.at[1], down)
    out.arrived("small")
    sum_small[...] = small_ref[...] + land_small[...]
    out.go("small1", sum_small, all_small.at[0], up)
    out.go("small2", sum_small, all_small.at[1], down)
    out.go("small3", sum_small, all_small.at[2], across)
    for side, (d, to) in enumerate(((1, up), (3, down))):
        add_cores(d)
        for k, (_, _, _, total, far, near, _) in enumerate(arrays):
            half = total.shape[0] // SIDE // 2
            out.arrived((("far1", "far2")[side], k))
            at = block(total, d, half * side, half)
            total[at, :] = (total[at, :].astype(F32) + far[side].astype(F32)).astype(BF16)
            out.go((("near1", "near2")[side], k), total.at[block(total, d)], near.at[side], to)
    add_cores(0)
    for k, (_, _, _, total, _, near, done) in enumerate(arrays):
        out.arrived(("near1", k))
        out.arrived(("near2", k))
        done[...] = (
            total[block(total, 0), :].astype(F32) + near[0].astype(F32) + near[1].astype(F32)
        ).astype(BF16)
    for name in ("small1", "small2", "small3"):
        out.arrived(name)
    fsmall_ref[...] = sum_small[...] + all_small[0] + all_small[1] + all_small[2]
    out.sent()


def fold(gin, gout, small, gin2, gout2, small2, call_id):
    vmem = pl.BlockSpec(memory_space=pltpu.VMEM)
    (a, b), (c, d) = gin.shape, gout.shape
    return pl.pallas_call(
        fold_kernel,
        in_specs=[vmem] * 6,
        out_specs=[vmem] * 3,
        out_shape=[
            jax.ShapeDtypeStruct((a // SIDE, b), BF16),
            jax.ShapeDtypeStruct((c // SIDE, d), BF16),
            jax.ShapeDtypeStruct(small.shape, F32),
        ],
        scratch_shapes=[
            pltpu.VMEM((a, b), BF16), pltpu.VMEM((c, d), BF16), pltpu.VMEM(small.shape, F32),
            pltpu.VMEM((a, b), BF16), pltpu.VMEM((c, d), BF16), pltpu.VMEM(small.shape, F32),
            pltpu.VMEM((2, a // SIDE // 2, b), BF16), pltpu.VMEM((2, c // SIDE // 2, d), BF16),
            pltpu.VMEM((2, a // SIDE, b), BF16), pltpu.VMEM((2, c // SIDE, d), BF16),
            pltpu.VMEM((3,) + small.shape, F32),
            pltpu.SemaphoreType.DMA((24,)), pltpu.SemaphoreType.DMA((24,)),
        ],
        compiler_params=pltpu.CompilerParams(
            collective_id=call_id, has_side_effects=True, vmem_limit_bytes=VMEM_ASK
        ),
        name="fold",
    )(gin, gout, small, gin2, gout2, small2)


def exchange_kernel(axis, count, x_ref, o_ref, landing, send, recv):
    me = lax.axis_index(axis)
    rows = o_ref.shape[0]
    greet([{axis: lax.rem(me + d, count)} for d in range(1, count)])
    out = Sender(send, recv)

    def block(j):
        return pl.ds(pl.multiple_of(j * rows, 16), rows)

    for d in range(1, count):
        to = lax.rem(me + d, count)
        out.go(d, x_ref.at[block(to)], landing.at[d], {axis: to})
    total = x_ref[block(me), :].astype(F32)
    for d in range(1, count):
        out.arrived(d)
        total = total + landing[d].astype(F32)
    o_ref[...] = total.astype(BF16)
    out.sent()


def exchange(x, axis, call_id):
    count = lax.axis_size(axis)
    rows = x.shape[0] // count
    vmem = pl.BlockSpec(memory_space=pltpu.VMEM)
    return pl.pallas_call(
        lambda *refs: exchange_kernel(axis, count, *refs),
        in_specs=[vmem],
        out_specs=vmem,
        out_shape=jax.ShapeDtypeStruct((rows, x.shape[1]), BF16),
        scratch_shapes=[
            pltpu.VMEM((count, rows, x.shape[1]), x.dtype),
            pltpu.SemaphoreType.DMA((count,)), pltpu.SemaphoreType.DMA((count,)),
        ],
        compiler_params=pltpu.CompilerParams(
            collective_id=call_id, has_side_effects=True, vmem_limit_bytes=VMEM_ASK
        ),
        name="exchange",
    )(x)


def assemble_kernel(inner, all_ref, gin_ref, gout_ref, steps):
    count = all_ref.shape[0]
    for j in range(count):
        gin_ref[:, j * HC : (j + 1) * HC] = all_ref[j, 0:256, 0:HC].astype(F32)
        gin_ref[:, inner + j * HC : inner + (j + 1) * HC] = all_ref[j, 0:256, HC:].astype(F32)
        gin_ref[j * 16 : (j + 1) * 16, 2 * inner : 2 * inner + 2 * NS] = all_ref[
            j, 256:272, :
        ].astype(F32)
        steps[2 * j : 2 * j + 2, :] = all_ref[j, 272:288, :].astype(F32)[0:2, :]
        big, small = j % SIDE, j // SIDE
        for c in range(4):
            gout_ref[big * HC + small * 32 : big * HC + small * 32 + 32, c * 256 : (c + 1) * 256] = (
                all_ref[j, 288 + 32 * c : 320 + 32 * c, :].astype(F32)
            )
    gin_ref[:, 2 * inner + 2 * NS :] = steps[...].T


def assemble(everyone, inner, columns, width):
    return pl.pallas_call(
        lambda *refs: assemble_kernel(inner, *refs),
        in_specs=[pl.BlockSpec(memory_space=pltpu.VMEM)],
        out_specs=[pl.BlockSpec(memory_space=pltpu.VMEM)] * 2,
        out_shape=[
            jax.ShapeDtypeStruct((256, columns), F32), jax.ShapeDtypeStruct((512, width), F32)
        ],
        scratch_shapes=[pltpu.VMEM((2 * everyone.shape[0], 256), F32)],
        compiler_params=pltpu.CompilerParams(vmem_limit_bytes=VMEM_ASK),
        name="assemble",
    )(everyone)


def rms_scale(values, gain):
    return values * lax.rsqrt(jnp.mean(values * values, axis=-1, keepdims=True) + EPS) * gain


def document_masks(doc):
    length = doc.shape[0]
    cols = []
    for k in (1, 2, 3):
        before = jnp.pad(doc, (k, 0), constant_values=-1)[:length]
        cols.append(before == doc)
    for k in (1, 2, 3):
        after = jnp.pad(doc, (0, k), constant_values=-1)[k:]
        cols.append(after == doc)
    blocks = doc.reshape(-1, SPAN)
    previous = jnp.concatenate([doc[:1], blocks[:-1, -1]])
    cols.append((blocks == previous[:, None]).reshape(-1))
    cols.append((blocks == blocks[:, -1:]).reshape(-1))
    cols.append(doc)
    cols = [c.astype(F32) for c in cols]
    cols += [jnp.zeros_like(cols[0])] * (16 - len(cols))
    return jnp.stack(cols, axis=1), doc.astype(F32)[None, :]


def forward_layer(u, n, layer, mask, docr, inner, reduce_rows):
    w, wo, cw, vec, _ = layer
    out = forward_core(n, w, wo, cw, vec, mask, docr)
    summed = reduce_rows(out[0])
    width = u.shape[1]
    square = summed[:, width] + summed[:, width + 1] + summed[:, width + 2]
    r = lax.rsqrt(square / inner + EPS)[:, None]
    branch = summed[:, :width] * r
    return u + branch, (branch, r, out[1:])


def backward_payload(c, branch, r, inner):
    low = c.astype(BF16)
    pull = r * r * jnp.sum(low.astype(F32) * branch, axis=1, keepdims=True) / inner
    hi, mid, lo = three(r)
    phi, pmid, _ = three(pull)
    pad = jnp.zeros((c.shape[0], AUX - 5), BF16)
    return jnp.concatenate([low, hi, mid, lo, phi, pmid, pad], axis=1)


def layer_weights(in_proj, out_proj, conv_weight, conv_bias, dt_bias, a_log, skip_scale, pre_gain, norm_gain, inner, q):
    heads = dt_bias.shape[0]
    def cols(a, start, size):
        return lax.dynamic_slice_in_dim(a, start, size, a.ndim - 1)
    bc = 2 * inner
    wdt = jnp.repeat(cols(in_proj, bc + 2 * NS + 2 * q, 2), HEAD, axis=1)
    w = jnp.concatenate(
        [cols(in_proj, q * HC, HC), cols(in_proj, inner + q * HC, HC),
         in_proj[:, bc : bc + 2 * NS], wdt], axis=1,
    )
    cw = jnp.concatenate([cols(conv_weight, q * HC, HC), conv_weight[:, inner:]], axis=1)
    cb = jnp.concatenate([cols(conv_bias, q * HC, HC), conv_bias[inner:]])
    def lanes(a):
        return jnp.repeat(cols(a, 2 * q, 2), HEAD)
    vec = jnp.stack(
        [lanes(dt_bias), jnp.exp(lanes(a_log)), lanes(skip_scale), cols(norm_gain, q * HC, HC)]
    )
    return w, cw, cb, vec, pre_gain


def body(
    block_input, doc_ids, out_grad, in_proj, out_proj, conv_weight, conv_bias,
    dt_bias, a_log, skip_scale, pre_gain, norm_gain,
):
    part = lax.axis_index("section")
    q = lax.axis_index("seq")
    n_seq = lax.axis_size("seq")
    n_z = lax.axis_size("wshard")
    inner = norm_gain.shape[1]
    width = block_input.shape[3]
    heads = dt_bias.shape[1]

    w, cw, cb, vec, pre = layer_weights(
        in_proj[0], None, conv_weight[0], conv_bias[0], dt_bias[0], a_log[0], skip_scale[0],
        pre_gain[0], norm_gain[0], inner, q,
    )
    out_rows = out_proj.shape[1]
    per_plane = out_rows // HC
    wo = lax.dynamic_slice_in_dim(out_proj[0], lax.rem(q, per_plane) * HC, HC, 0)
    small = jnp.concatenate([cw.ravel(), cb, vec.ravel(), pre])
    small_all = lax.all_gather(small, "section", axis=0)
    doc = lax.dynamic_index_in_dim(doc_ids[:, 0], part, 0, keepdims=False)
    mask, docr = document_masks(doc)
    u = lax.dynamic_index_in_dim(block_input[:, 0], part, 0, keepdims=False).astype(F32)
    cot = lax.dynamic_index_in_dim(out_grad[:, 0], part, 0, keepdims=False).astype(F32)

    n, w_all, wo_all = opening(
        rms_scale(u, small_all[0][-width:]).astype(BF16), w, wo, "seq", 1
    )
    layers = []
    for l in (0, 1):
        s = small_all[l]
        cwl = jnp.concatenate([s[: 5 * 3 * HC].reshape(5, 3 * HC), jnp.zeros((3, 3 * HC), F32)])
        at = 5 * 3 * HC
        vecl = jnp.concatenate([s[at : at + 4 * HC].reshape(4, HC), jnp.zeros((4, HC), F32)])
        layers.append((w_all[l], wo_all[l], cwl, vecl, s[at + 4 * HC :]))

    inputs, normed, saved, hidden = [], [], [], []
    for l in (0, 1):
        inputs.append(u)
        if l == 1:
            n = spread(rms_scale(u, layers[l][4]).astype(BF16), "seq", 5)
        normed.append(n)
        u, s = forward_layer(
            u, n, layers[l], mask, docr, inner, lambda x: collect(x, "seq", 2)
        )
        hidden.append(u)
        saved.append(s)

    grads_in, grads = [None, None], [None, None]
    for l in (1, 0):
        branch, r, kept = saved[l]
        w, wo, cwl, vecl, gain = layers[l]
        payload = spread(backward_payload(cot, branch, r, inner), "seq", 3)
        gpart, gin, gout, gsmall = backward_core(
            payload, normed[l], w, wo, cwl, vecl, mask, docr, kept
        )
        g_normed = collect(gpart, "seq", 4)
        _, pull = jax.vjp(rms_scale, inputs[l], gain)
        path, g_pre = pull(g_normed)
        cot = cot + path
        grads_in[l] = cot
        grads[l] = (gin, gout, gsmall, g_pre)

    def swap(a):
        return lax.ppermute(a, "section", [(0, 1), (1, 0)])

    def by_layer(pair):
        mine = jnp.where(part == 0, pair[0], pair[1])
        other = swap(jnp.where(part == 0, pair[1], pair[0]))
        return jnp.where(part == 0, jnp.stack([mine, other]), jnp.stack([other, mine]))

    hidden_out = by_layer(hidden)
    grads_out = by_layer(grads_in)

    def packed(g):
        gin, gout, gsmall, g_pre = g
        pre_rows = jnp.pad(g_pre, (0, 8 * 3 * HC - width)).reshape(8, 3 * HC)
        return gin.astype(BF16), gout.astype(BF16), jnp.concatenate([gsmall, pre_rows])

    pair = [packed(g) for g in grads]
    mine = [jnp.where(part == 0, a, b) for a, b in zip(*pair)]
    other = [jnp.where(part == 0, b, a) for a, b in zip(*pair)]
    gin, gout, gsmall = fold(*mine, *other, 6)
    n_rows = width // n_z
    route = []
    for y in range(SIDE):
        for x in range(SIDE):
            for z in range(SIDE):
                route.append(((y * SIDE + x) * n_z + z, (z * SIDE + x) * n_z + y))
    gout = lax.ppermute(gout, ("seq", "wshard"), route)
    g_bc = exchange(gin[:, 2 * HC : 4 * HC], "seq", 7)
    g_dt = jnp.pad(gin[:, 4 * HC :: HEAD].T, ((0, 14), (0, 0)))
    smalls = [t.reshape(-1, 256) for t in three(gsmall)]
    block = [gin[:, : 2 * HC], g_bc, g_dt] + [gout[:, c : c + 256] for c in range(0, width, 256)]
    block = jnp.concatenate(block + smalls)
    used = block.shape[0]
    size = -(-used // 64) * 64
    everyone = spread(jnp.pad(block, ((0, size - used), (0, 0))), "seq", 8)
    everyone = everyone.reshape(n_seq, size, 256)
    shard_in, shard_out = assemble(everyone, inner, in_proj.shape[2], width)

    third = smalls[0].shape[0]
    small = sum(
        everyone[:, used - third * (3 - k) : used - third * (2 - k)].astype(F32) for k in range(3)
    ).reshape(n_seq, 16, 3 * HC)
    conv_x = jnp.moveaxis(small[:, :5, :HC], 0, 1).reshape(5, inner)
    conv = jnp.concatenate([conv_x, small[:, :5, HC:].sum(axis=0)], axis=1)
    pieces = [
        conv[:4], conv[4],
        small[:, 6, 0:HC:HEAD].reshape(heads),
        small[:, 6, HC : 2 * HC : HEAD].reshape(heads),
        small[:, 5, HC : 2 * HC].reshape(heads, HEAD).sum(axis=1),
        small[:, 8:].sum(axis=0).reshape(-1)[:width],
        small[:, 5, :HC].reshape(inner),
    ]
    return (
        hidden_out[None, :, None], grads_out[None, :, None], shard_in[None], shard_out[None],
        *[p[None] for p in pieces],
    )


def solution(mesh):
    specs = (
        P(None, "wshard", "seq", None),
        P(None, "wshard", None),
        P(None, "wshard", "seq", None),
        P("section", "wshard", None),
        P("section", "wshard", None),
        P("section", None, None),
        P("section", None),
        P("section", None),
        P("section", None),
        P("section", None),
        P("section", None),
        P("section", None),
    )
    outs = (
        P("section", None, "wshard", "seq", None),
        P("section", None, "wshard", "seq", None),
        P("section", "wshard", None),
        P("section", "wshard", None),
        P("section", None, None),
    ) + (P("section", None),) * 6
    return jax.shard_map(body, mesh=mesh, in_specs=specs, out_specs=outs, check_vma=False)
```

```python
import jax
import jax.numpy as jnp
from jax import lax
from jax.experimental import pallas as pl
from jax.experimental.pallas import tpu as pltpu
from jax.sharding import PartitionSpec as P

SPAN = 256
EPS = 1e-05
F32 = jnp.float32
BF16 = jnp.bfloat16
MESH = pl.DeviceIdType.MESH
VMEM_ASK = 48 * 1024 * 1024

HC = 128
NS = 128
WR = 528
AUX = 128
HEAD = 64
SIDE = 4
AXIS = "seq"


def dot_nn(a, b):
    return lax.dot_general(a, b, (((1,), (0,)), ((), ())), preferred_element_type=F32)


def dot_nt(a, b):
    return lax.dot_general(a, b, (((1,), (1,)), ((), ())), preferred_element_type=F32)


def dot_tn(a, b):
    return lax.dot_general(a, b, (((0,), (0,)), ((), ())), preferred_element_type=F32)


def three(x):
    hi = x.astype(BF16)
    rest = x - hi.astype(F32)
    mid = rest.astype(BF16)
    low = (rest - mid.astype(F32)).astype(BF16)
    return hi, mid, low


def exact_left(ones, x):
    hi, mid, low = three(x)
    return dot_nn(ones, hi) + dot_nn(ones, mid) + dot_nn(ones, low)


def exact_right(x, ones):
    hi, mid, low = three(x)
    return dot_nn(hi, ones) + dot_nn(mid, ones) + dot_nn(low, ones)


def iota(shape, dim):
    return lax.broadcasted_iota(jnp.int32, shape, dim)


def sigmoid(x):
    return 1.0 / (1.0 + jnp.exp(-x))


def softplus(x):
    return jnp.maximum(x, 0.0) + jnp.log1p(jnp.exp(-jnp.abs(x)))


def conv_rows(vbuf, con, mask):
    z = vbuf[pl.ds(8, SPAN), :] * con[3:4, :] + con[4:5, :]
    for k in (1, 2, 3):
        z = z + vbuf[pl.ds(8 - k, SPAN), :] * con[3 - k : 4 - k, :] * mask[:, k - 1 : k]
    return z


def block_terms(dt, vec, mask, docr):
    step = softplus(dt + vec[0])
    log_decay = -step * vec[1]
    rows, cols = iota((SPAN, SPAN), 0), iota((SPAN, SPAN), 1)
    lower = rows >= cols
    running = exact_left(lower.astype(F32).astype(BF16), log_decay)
    turned = running.T
    allowed = lower & (mask[:, 8:9] == docr)
    decays = []
    for h in (0, 1):
        gaps = running[:, h * HEAD : h * HEAD + 1] - turned[h * HEAD : h * HEAD + 1, :]
        decays.append(jnp.exp(jnp.where(allowed, gaps, -1e30)))
    reach = jnp.exp(running) * mask[:, 6:7]
    total = running[SPAN - 1 :, :]
    tail = jnp.exp(total - running) * mask[:, 7:8]
    carry = jnp.exp(total) * mask[SPAN - 1 :, 6:7]
    return step, log_decay, decays, reach, tail, carry


def layer_constants(con):
    return con[5:6, :HC], con[5:6, HC : 2 * HC], con[5:6, 2 * HC : 3 * HC], con[6:7, :HC]


def pre_gain_of(con):
    return jnp.concatenate([con[k : k + 1, 3 * HC : 4 * HC] for k in range(8)], axis=1)


def head_ones():
    return (iota((16, HC), 0) == iota((16, HC), 1) // HEAD).astype(F32).astype(BF16)


def head_firsts():
    return (iota((HC, 16), 0) == iota((HC, 16), 1) * HEAD).astype(F32).astype(BF16)


def lanes_of(columns, rows):
    lane = iota((rows, AUX), 1)
    out = jnp.zeros((rows, AUX), F32)
    for k, column in enumerate(columns):
        out = jnp.where(lane == k, column.astype(F32), out)
    return out.astype(BF16)


def fwd_step(i, n_ref, wt_ref, wo_ref, con_ref, mask_ref, docr_ref, kept, part, vbuf, state):
    vh_ref, gate_ref, dt_ref, mix_ref, scan_ref, st_ref = kept

    @pl.when(i == 0)
    def _():
        vbuf[0:8, :] = jnp.zeros((8, 3 * HC), F32)
        state[...] = jnp.zeros_like(state)

    width = wo_ref.shape[2]
    chunk = wt_ref.shape[3]
    mask = mask_ref[...]
    con = con_ref[0]
    vec = layer_constants(con)
    conv = con[:, : 3 * HC]
    proj = dot_nt(n_ref[:, 0:chunk], wt_ref[0, 0])
    for k in range(1, wt_ref.shape[1]):
        proj = proj + dot_nt(n_ref[:, k * chunk : (k + 1) * chunk], wt_ref[0, k])
    gate = proj[:, :HC]
    v = proj[:, HC : 4 * HC].astype(BF16).astype(F32)
    dt = dot_nn(proj[:, 4 * HC :].astype(BF16), head_ones())
    vbuf[8:, :] = v
    z = conv_rows(vbuf, conv, mask)
    vh_ref[0] = vbuf[...]
    vbuf[0:8, :] = v[SPAN - 8 :, :]
    act = z * sigmoid(z)
    xc = act[:, :HC]
    b16 = act[:, HC : 2 * HC].astype(BF16)
    c16 = act[:, 2 * HC :].astype(BF16)
    step, _, decays, reach, tail, carry = block_terms(dt, vec, mask, docr_ref[0:1, :])
    xs = xc * step
    xs16 = xs.astype(BF16)
    scores = dot_nt(c16, b16)
    within = [dot_nn((scores * d).astype(BF16), xs16) for d in decays]
    first = iota((SPAN, HC), 1) < HEAD
    st = state[...]
    st_ref[0] = st
    scan = jnp.where(first, within[0], within[1]) + dot_nn(c16, st.astype(BF16)) * reach
    state[...] = st * carry + dot_tn(b16, (xs * tail).astype(BF16))
    mixed = (scan + xc * vec[2]).astype(BF16)
    g = mixed.astype(F32) * (gate * sigmoid(gate))
    place = pl.ds(pl.multiple_of(i * SPAN, SPAN), SPAN)
    part[place, :width] = dot_nn((g * vec[3]).astype(BF16), wo_ref[0]).astype(BF16)
    part[place, width:] = lanes_of(three(jnp.sum(g * g, axis=1, keepdims=True)), SPAN)
    gate_ref[...] = gate
    dt_ref[...] = dt
    mix_ref[...] = mixed
    scan_ref[...] = scan


def bwd_step(
    i, c_ref, n_ref, wt_ref, wo_ref, con_ref, mask_ref, docr_ref, kept,
    part, gin, gout, small, dzbuf, dstate,
):
    vh_ref, gate_ref, dt_ref, mix_ref, scan_ref, st_ref = kept

    @pl.when(i == 0)
    def _():
        dzbuf[SPAN:, :] = jnp.zeros((8, 3 * HC), F32)
        dstate[...] = jnp.zeros_like(dstate)
        gin[...] = jnp.zeros_like(gin)
        gout[...] = jnp.zeros_like(gout)
        small[...] = jnp.zeros_like(small)

    width = wo_ref.shape[2]
    chunk = wt_ref.shape[3]
    mask = mask_ref[...]
    con = con_ref[0]
    vec = layer_constants(con)
    conv = con[:, : 3 * HC]
    cot = c_ref[:, :width]
    aux = c_ref[:, width:].astype(F32)
    r = aux[:, 0:1] + aux[:, 1:2] + aux[:, 2:3]
    pull = aux[:, 3:4] + aux[:, 4:5]
    gate = gate_ref[...]
    sg = sigmoid(gate)
    silu = gate * sg
    mixed = mix_ref[...].astype(F32)
    g = mixed * silu
    gain = vec[3]
    dy = dot_nt(cot, wo_ref[0])
    gr = g * r
    gout[...] += dot_tn((gr * gain).astype(BF16), cot)
    d_gain = jnp.sum(dy * gr, axis=0, keepdims=True)
    dg = dy * (r * gain) - g * pull
    dm16 = (dg * silu).astype(BF16)
    dm = dm16.astype(F32)
    dgate = dg * mixed * (sg * (1.0 + gate * (1.0 - sg)))

    vbuf = vh_ref.at[0]
    z = conv_rows(vbuf, conv, mask)
    sz = sigmoid(z)
    act = z * sz
    xc = act[:, :HC]
    b16 = act[:, HC : 2 * HC].astype(BF16)
    c16 = act[:, 2 * HC :].astype(BF16)
    dt = dt_ref[...]
    step, log_decay, decays, reach, tail, carry = block_terms(dt, vec, mask, docr_ref[0:1, :])
    xs16 = (xc * step).astype(BF16)
    xs = xs16.astype(F32)
    scores = dot_nt(c16, b16)
    first = iota((SPAN, HC), 1) < HEAD
    zero16 = jnp.zeros((SPAN, HC), BF16)
    dscores = jnp.zeros((SPAN, SPAN), F32)
    dxs = []
    for h in (0, 1):
        own = jnp.where(first, dm16, zero16) if h == 0 else jnp.where(first, zero16, dm16)
        dp = dot_nt(own, xs16)
        dscores = dscores + dp * decays[h]
        dxs.append(dot_tn((scores * decays[h]).astype(BF16), dm16))
    ds16 = dscores.astype(BF16)
    st = st_ref[0]
    dst = dstate[...]
    dst16 = dst.astype(BF16)
    dcs16 = (dm * reach).astype(BF16)
    dc = dot_nn(ds16, b16) + dot_nt(dcs16, st.astype(BF16))
    db = dot_tn(ds16, c16) + dot_nt((xs * tail).astype(BF16), dst16)
    dxs_tail = dot_nn(b16, dst16) * tail
    dxs_all = jnp.where(first, dxs[0], dxs[1]) + dxs_tail
    dstate[...] = dst * carry + dot_tn(c16, dcs16)

    d_total = jnp.sum(xs * dxs_tail, axis=0, keepdims=True) + carry * jnp.sum(
        dst * st, axis=0, keepdims=True
    )
    flow = dm * scan_ref[...] - xs * dxs_all
    rows, cols = iota((SPAN, SPAN), 0), iota((SPAN, SPAN), 1)
    upper = (cols >= rows).astype(F32).astype(BF16)
    flow = exact_left(upper, flow) + d_total
    same_head = ((iota((HC, HC), 0) < HEAD) == (iota((HC, HC), 1) < HEAD)).astype(F32).astype(BF16)
    d_log = exact_right(flow, same_head)
    d_step = exact_right(dxs_all * xc, same_head) - d_log * vec[1]
    d_alog = jnp.sum(d_log * log_decay, axis=0, keepdims=True)
    d_dt = d_step * sigmoid(dt + vec[0])
    d_skip = jnp.sum(dm * xc, axis=0, keepdims=True)
    d_xc = dm * vec[2] + dxs_all * step

    dact = sz * (1.0 + z * (1.0 - sz))
    dzbuf[:SPAN, 0:HC] = d_xc * dact[:, :HC]
    dzbuf[:SPAN, HC : 2 * HC] = db * dact[:, HC : 2 * HC]
    dzbuf[:SPAN, 2 * HC :] = dc * dact[:, 2 * HC :]
    dz = dzbuf[:SPAN, :]
    dv = dz * conv[3:4, :]
    small[3:4, : 3 * HC] += jnp.sum(dz * vbuf[pl.ds(8, SPAN), :], axis=0, keepdims=True)
    small[4:5, : 3 * HC] += jnp.sum(dz, axis=0, keepdims=True)
    for k in (1, 2, 3):
        dv = dv + dzbuf[pl.ds(k, SPAN), :] * conv[3 - k : 4 - k, :] * mask[:, 2 + k : 3 + k]
        small[3 - k : 4 - k, : 3 * HC] += jnp.sum(
            dz * vbuf[pl.ds(8 - k, SPAN), :] * mask[:, k - 1 : k], axis=0, keepdims=True
        )
    dzbuf[SPAN:, :] = dz[:8, :]
    small[5:6, 0:HC] += d_gain
    small[5:6, HC : 2 * HC] += d_skip
    small[6:7, 0:HC] += jnp.sum(d_dt, axis=0, keepdims=True)
    small[6:7, HC : 2 * HC] += d_alog

    gp = jnp.concatenate([dgate.astype(BF16), dv.astype(BF16)], axis=1)
    gdt = dot_nn(d_dt.astype(BF16), head_firsts()).astype(BF16)
    wide = 4 * HC
    place = pl.ds(pl.multiple_of((pl.num_programs(0) - 1 - i) * SPAN, SPAN), SPAN)
    for k in range(wt_ref.shape[1]):
        cols_k = slice(k * chunk, (k + 1) * chunk)
        part[place, cols_k] = (
            dot_nn(gp, wt_ref[0, k, :wide]) + dot_nn(gdt, wt_ref[0, k, wide:])
        ).astype(BF16)
        gin[k, :wide] += dot_tn(gp, n_ref[:, cols_k])
        gin[k, wide:] += dot_tn(gdt, n_ref[:, cols_k])


def place_of(half, f, s):
    f, s = lax.rem(f, SIDE), lax.rem(s, SIDE)
    return s * SIDE + f if half == 0 else f * SIDE + s


def ring_places():
    me = lax.axis_index(AXIS)
    return me % SIDE, me // SIDE


def ring_neighbours():
    x, y = ring_places()
    steps = ((1, 0), (3, 0), (0, 1), (0, 3))
    return [{AXIS: place_of(0, x + dx, y + dy)} for dx, dy in steps]


def plane_neighbours():
    z = lax.axis_index("wshard")
    return [{"wshard": lax.rem(z + 1, SIDE)}, {"wshard": lax.rem(z + 3, SIDE)}]


def plane_across():
    return {"wshard": lax.rem(lax.axis_index("wshard") + 2, SIDE)}


def other_core():
    return {"section": 1 - lax.axis_index("section")}


def greet(targets):
    barrier = pltpu.get_barrier_semaphore()
    for target in targets:
        pl.semaphore_signal(barrier, inc=1, device_id=target, device_id_type=MESH)


def greeted(count):
    pl.semaphore_wait(pltpu.get_barrier_semaphore(), count)


def run(*parts):
    live = list(parts)
    while live:
        for part in list(live):
            try:
                next(part)
            except StopIteration:
                live.remove(part)


class Sender:
    def __init__(self, send, recv):
        self.send, self.recv, self.used, self.copies, self.free = send, recv, 0, {}, set()

    def make(self, name, source, target, to):
        copy = pltpu.make_async_remote_copy(
            src_ref=source, dst_ref=target, send_sem=self.send.at[self.used],
            recv_sem=self.recv.at[self.used], device_id=to, device_id_type=MESH,
        )
        self.used += 1
        self.copies[name] = copy
        return copy

    def go(self, name, source, target, to):
        self.make(name, source, target, to).start()
        self.free.add(name)

    def arrived(self, name):
        self.copies[name].wait_recv()

    def sent(self):
        for name in self.copies:
            if name in self.free:
                self.copies[name].wait_send()


def rows_at(ref, start, size):
    return ref.at[pl.ds(pl.multiple_of(start, 16), size)]


def spread_steps(x_ref, o_ref, out, own):
    x, y = ring_places()
    rows = x_ref.shape[0]
    half_rows, quarter = rows // 2, rows // 4
    mine = pltpu.make_async_copy(x_ref, rows_at(o_ref, place_of(0, x, y) * rows, rows), own)
    mine.start()
    firsts = ((x, y), (y, x))

    def go(name, half, block, offset, size, to, source=None):
        place = rows_at(o_ref, block * rows + half * half_rows + offset, size)
        out.go((half, name), place if source is None else source, place, {AXIS: to})

    def across(half, d):
        f, s = firsts[half]
        block = place_of(half, f + d, s)
        source = x_ref.at[pl.ds(half * half_rows, half_rows)] if d == 0 else None
        go(("t1", d), half, block, 0, half_rows, place_of(half, f, s + 1), source)
        go(("t2", d), half, block, 0, half_rows, place_of(half, f, s + 3), source)

    def onward(half, d):
        f, s = firsts[half]
        out.arrived((half, ("t1", d)))
        go(("u1", d), half, place_of(half, f + d, s + 3), 0, quarter, place_of(half, f, s + 1))
        out.arrived((half, ("t2", d)))
        go(("u2", d), half, place_of(half, f + d, s + 1), quarter, quarter, place_of(half, f, s + 3))

    for half in (0, 1):
        f, s = firsts[half]
        source = x_ref.at[pl.ds(half * half_rows, half_rows)]
        block = place_of(half, f, s)
        go("s1", half, block, 0, half_rows, place_of(half, f + 1, s), source)
        go("s2", half, block, 0, half_rows, place_of(half, f + 3, s), source)
    for half in (0, 1):
        across(half, 0)
    yield
    for half in (0, 1):
        f, s = firsts[half]
        out.arrived((half, "s1"))
        go("s3", half, place_of(half, f + 3, s), 0, quarter, place_of(half, f + 1, s))
        out.arrived((half, "s2"))
        go("s4", half, place_of(half, f + 1, s), quarter, quarter, place_of(half, f + 3, s))
    for half in (0, 1):
        across(half, 3)
        across(half, 1)
    yield
    for half in (0, 1):
        onward(half, 0)
    for half in (0, 1):
        out.arrived((half, "s3"))
        out.arrived((half, "s4"))
        across(half, 2)
    yield
    for d in (3, 1, 2):
        for half in (0, 1):
            onward(half, d)
        yield
    for half in (0, 1):
        for d in range(SIDE):
            out.arrived((half, ("u1", d)))
            out.arrived((half, ("u2", d)))
    mine.wait()


def collect_scratch(rows, cols):
    half_rows, quarter = rows // 2, rows // 4
    return [
        pltpu.VMEM((2, SIDE, 2, quarter, cols), BF16),
        pltpu.VMEM((2, SIDE, 2, half_rows, cols), BF16),
        pltpu.VMEM((2, SIDE, 2, half_rows, cols), BF16),
        pltpu.VMEM((2, SIDE, half_rows, cols), F32),
        pltpu.VMEM((2, 2, quarter, cols), BF16),
        pltpu.VMEM((2, 2, half_rows, cols), BF16),
        pltpu.VMEM((2, 3, half_rows, cols), BF16),
        pltpu.VMEM((rows, cols), F32),
    ]


def collect_steps(x_ref, buffers, out):
    far, near, stage, reduced, far2, near2, stage2, o_ref = buffers
    x, y = ring_places()
    rows = o_ref.shape[0]
    half_rows, quarter = rows // 2, rows // 4
    firsts = ((x, y), (y, x))
    order = (2, 1, 3, 0)

    def go(name, half, source, target, to):
        out.go((half, name), source, target, {AXIS: to})

    def start_of(half, f, s):
        return pl.multiple_of(place_of(half, f, s) * rows + half * half_rows, 16)

    for d in order:
        for half in (0, 1):
            f, s = firsts[half]
            start = start_of(half, f + d, s + 2)
            go(("a1", d), half, rows_at(x_ref, start, quarter), far.at[half, d, 0],
               place_of(half, f, s + 1))
            go(("a2", d), half, rows_at(x_ref, start + quarter, quarter), far.at[half, d, 1],
               place_of(half, f, s + 3))
    yield
    for d in order:
        for half in (0, 1):
            f, s = firsts[half]
            for side, step in enumerate((1, 3)):
                start = start_of(half, f + d, s + step)
                plain, through = quarter * (1 - side), quarter * side
                stage[half, d, side, pl.ds(plain, quarter)] = x_ref[
                    pl.ds(pl.multiple_of(start + plain, 16), quarter), :
                ]
                out.arrived((half, (("a1", "a2")[side], d)))
                stage[half, d, side, pl.ds(through, quarter)] = (
                    x_ref[pl.ds(pl.multiple_of(start + through, 16), quarter), :].astype(F32)
                    + far[half, d, side].astype(F32)
                ).astype(BF16)
                go((("b1", "b2")[side], d), half, stage.at[half, d, side], near.at[half, d, side],
                   place_of(half, f, s + step))
        if d in (1, 0):
            yield

    def reduce_second(half, d):
        f, s = firsts[half]
        out.arrived((half, ("b1", d)))
        out.arrived((half, ("b2", d)))
        reduced[half, d] = (
            x_ref[pl.ds(start_of(half, f + d, s), half_rows), :].astype(F32)
            + near[half, d, 0].astype(F32) + near[half, d, 1].astype(F32)
        )

    for half in (0, 1):
        f, s = firsts[half]
        reduce_second(half, 2)
        stage2[half, 2] = reduced[half, 2].astype(BF16)
        go("c1", half, stage2.at[half, 2, pl.ds(0, quarter)], far2.at[half, 0],
           place_of(half, f + 1, s))
        go("c2", half, stage2.at[half, 2, pl.ds(quarter, quarter)], far2.at[half, 1],
           place_of(half, f + 3, s))
    yield
    for d, side in ((1, 0), (3, 1)):
        for half in (0, 1):
            f, s = firsts[half]
            reduce_second(half, d)
            plain, through = quarter * (1 - side), quarter * side
            out.arrived((half, ("c1", "c2")[side]))
            stage2[half, side, pl.ds(plain, quarter)] = reduced[
                half, d, pl.ds(plain, quarter)
            ].astype(BF16)
            stage2[half, side, pl.ds(through, quarter)] = (
                reduced[half, d, pl.ds(through, quarter)] + far2[half, side].astype(F32)
            ).astype(BF16)
            go(("d1", "d2")[side], half, stage2.at[half, side], near2.at[half, side],
               place_of(half, f + d, s))
    yield
    for half in (0, 1):
        reduce_second(half, 0)
    for half in (0, 1):
        out.arrived((half, "d1"))
        out.arrived((half, "d2"))
        o_ref[pl.ds(half * half_rows, half_rows), :] = (
            reduced[half, 0] + near2[half, 0].astype(F32) + near2[half, 1].astype(F32)
        )


def half_of(rows):
    return rows // 32 * 16


def fold_scratch():
    scratch = [pltpu.VMEM((8, 4 * HC), F32)] * 3 + [pltpu.VMEM((3, 8, 4 * HC), F32)]
    for rows, cols in ((WR, 256), (HC // SIDE, 1024)):
        scratch += [pltpu.VMEM((SIDE, rows, cols), BF16)] * 3
        scratch += [pltpu.VMEM((2, rows - half_of(rows), cols), BF16)]
        scratch += [pltpu.VMEM((2, rows, cols), BF16)]
    return scratch


def fold_steps(layer, gin, gout, fin_ref, fout_ref, buffers, out):
    z = lax.axis_index("wshard")
    up, down = plane_neighbours()
    owner = lax.axis_index("section") == layer
    ours_in, land_in, total_in, far_in, near_in = buffers[4:9]
    ours_out, land_out, total_out, far_out, near_out = buffers[9:14]
    ours_in[...] = gin[...].astype(BF16)
    piece = HC // SIDE
    for k in range(SIDE):
        ours_out[k] = gout[k * piece : (k + 1) * piece, :].astype(BF16)
    arrays = (
        (ours_in, land_in, total_in, far_in, near_in, fin_ref),
        (ours_out, land_out, total_out, far_out, near_out, fout_ref),
    )

    def at(d):
        return lax.rem(z + d, SIDE)

    swaps, legs = {}, {}
    parts = []
    for ours in (ours_in, ours_out):
        half = half_of(ours.shape[1])
        parts.append((pl.ds(0, half), pl.ds(half, ours.shape[1] - half)))
    for d in (2, 1, 3, 0):
        for k, (ours, land, *_) in enumerate(arrays):
            swaps[k, d] = out.make(("swap", k, d), ours.at[at(d)], land.at[at(d)], other_core())
    for k, (_, _, total, far, near, _) in enumerate(arrays):
        for side, to in enumerate((up, down)):
            some = parts[k][side]
            legs[k, "far", side] = out.make(
                ("far", k, side), total.at[at(2), some], far.at[side, pl.ds(0, some.size)], to
            )
        legs[k, "near", 0] = out.make(("near", k, 0), total.at[at(1)], near.at[0], up)
        legs[k, "near", 1] = out.make(("near", k, 1), total.at[at(3)], near.at[1], down)

    @pl.when(jnp.logical_not(owner))
    def _():
        for copy in swaps.values():
            copy.start()

    yield

    def add_cores(d):
        for k, (ours, land, total, *_) in enumerate(arrays):
            swaps[k, d].wait_recv()
            total[at(d)] = (ours[at(d)].astype(F32) + land[at(d)].astype(F32)).astype(BF16)

    @pl.when(owner)
    def _():
        add_cores(2)
        for k in (0, 1):
            legs[k, "far", 0].start()
            legs[k, "far", 1].start()

    yield
    for side, d in ((0, 1), (1, 3)):
        @pl.when(owner)
        def _():
            add_cores(d)
            for k, (_, _, total, far, _, _) in enumerate(arrays):
                legs[k, "far", side].wait_recv()
                some = parts[k][side]
                total[at(d), some] = (
                    total[at(d), some].astype(F32) + far[side, pl.ds(0, some.size)].astype(F32)
                ).astype(BF16)
                legs[k, "near", side].start()

        yield

    @pl.when(owner)
    def _():
        add_cores(0)
        for k, (_, _, total, _, near, done) in enumerate(arrays):
            legs[k, "near", 0].wait_recv()
            legs[k, "near", 1].wait_recv()
            done[...] = (
                total[at(0)].astype(F32) + near[0].astype(F32) + near[1].astype(F32)
            ).astype(BF16)
        for leg in legs.values():
            leg.wait_send()

    @pl.when(jnp.logical_not(owner))
    def _():
        for copy in swaps.values():
            copy.wait_send()


def fold_small(layer, small, done_ref, buffers, out):
    owner = lax.axis_index("section") == layer
    land, total, _, planes = buffers[:4]
    up, down = plane_neighbours()
    swap = out.make("small", small, land, other_core())
    legs = [
        out.make(("small", k), total, planes.at[k], to)
        for k, to in enumerate((up, down, plane_across()))
    ]

    @pl.when(jnp.logical_not(owner))
    def _():
        swap.start()

    @pl.when(owner)
    def _():
        swap.wait_recv()
        total[...] = small[...] + land[...]
        for leg in legs:
            leg.start()

    yield

    @pl.when(owner)
    def _():
        for leg in legs:
            leg.wait_recv()
        done_ref[...] = total[...] + planes[0] + planes[1] + planes[2]
        for leg in legs:
            leg.wait_send()

    @pl.when(jnp.logical_not(owner))
    def _():
        swap.wait_send()


def norm_rows(u):
    return u * lax.rsqrt(jnp.mean(u * u, axis=1, keepdims=True) + EPS)


def payload_into(ref, c, branch, r, inner):
    width = c.shape[1]
    low = c.astype(BF16)
    pull = r * r * jnp.sum(low.astype(F32) * branch, axis=1, keepdims=True) / inner
    ref[:, :width] = low
    ref[:, width:] = lanes_of(list(three(r)) + list(three(pull))[:2], c.shape[0])


def forward_kernel(
    layer, inner, n_ref, wt_ref, wo_ref, con_ref, cons_ref, mask_ref, docr_ref, u_ref, cot_ref,
    vh_ref, gate_ref, dt_ref, mix_ref, scan_ref, st_ref, h_ref, branch_ref, r_ref, next_ref,
    vbuf, state, part, own_rows, landing, send, recv, send2, recv2, own, *buffers,
):
    i = pl.program_id(0)
    last = pl.num_programs(0) - 1

    @pl.when(i == 0)
    def _():
        greet(ring_neighbours())

    kept = (vh_ref, gate_ref, dt_ref, mix_ref, scan_ref, st_ref)
    fwd_step(i, n_ref, wt_ref, wo_ref, con_ref, mask_ref, docr_ref, kept, part, vbuf, state)

    @pl.when(i == last)
    def _():
        greeted(4)
        out = Sender(send, recv)
        run(collect_steps(part, buffers, out))
        width = u_ref.shape[1]
        total = buffers[-1]
        square = total[:, width : width + 1] + total[:, width + 1 : width + 2]
        square = square + total[:, width + 2 : width + 3]
        r = lax.rsqrt(square / inner + EPS)
        branch = total[:, :width] * r
        h = u_ref[...] + branch
        h_ref[...] = h
        branch_ref[...] = branch
        r_ref[...] = jnp.broadcast_to(r, r_ref.shape)
        if layer == 0:
            own_rows[...] = (norm_rows(h) * pre_gain_of(cons_ref[1])).astype(BF16)
        else:
            payload_into(own_rows, cot_ref[...], branch, r, inner)
        more = Sender(send2, recv2)
        run(spread_steps(own_rows, landing, more, own.at[0]))
        copy = pltpu.make_async_copy(landing, next_ref, own.at[1])
        copy.start()
        out.sent()
        more.sent()
        copy.wait()


def whole(shape):
    return pl.BlockSpec(shape, lambda i: (0,) * len(shape))


def of_layer(a, layer):
    rest = (0,) * (a.ndim - 1)
    return pl.BlockSpec((1,) + a.shape[1:], lambda i: (layer,) + rest)


def sems(count):
    return [pltpu.SemaphoreType.DMA((count,)), pltpu.SemaphoreType.DMA((count,))]


def forward_layer(layer, inner, n, wt, wo, cons, mask, docr, u, cot):
    length, width = n.shape
    blocks = length // SPAN
    mine = u.shape[0]
    wide = width + AUX
    out_cols = width if layer == 0 else wide

    def rows(cols):
        return pl.BlockSpec((SPAN, cols), lambda i: (i, 0))

    def shape(dims, dtype=F32):
        return jax.ShapeDtypeStruct(dims, dtype)

    return pl.pallas_call(
        lambda *refs: forward_kernel(layer, inner, *refs),
        grid=(blocks,),
        in_specs=[
            rows(width), of_layer(wt, layer), of_layer(wo, layer), of_layer(cons, layer),
            whole(cons.shape), rows(mask.shape[1]), pl.BlockSpec((8, SPAN), lambda i: (0, i)),
            whole(u.shape), whole(cot.shape),
        ],
        out_specs=[
            pl.BlockSpec((1, SPAN + 8, 3 * HC), lambda i: (i, 0, 0)),
            rows(HC), rows(HC), rows(HC), rows(HC),
            pl.BlockSpec((1, NS, HC), lambda i: (i, 0, 0)),
            whole(u.shape), whole(u.shape), whole((mine, HC)), pl.BlockSpec(memory_space=pl.ANY),
        ],
        out_shape=[
            shape((blocks, SPAN + 8, 3 * HC)), shape((length, HC)), shape((length, HC)),
            shape((length, HC), BF16), shape((length, HC)), shape((blocks, NS, HC)),
            shape(u.shape), shape(u.shape), shape((mine, HC)), shape((length, out_cols), BF16),
        ],
        scratch_shapes=[
            pltpu.VMEM((SPAN + 8, 3 * HC), F32), pltpu.VMEM((NS, HC), F32),
            pltpu.VMEM((length, wide), BF16), pltpu.VMEM((mine, out_cols), BF16),
            pltpu.VMEM((length, out_cols), BF16), *sems(40), *sems(40),
            pltpu.SemaphoreType.DMA((2,)), *collect_scratch(mine, wide),
        ],
        compiler_params=pltpu.CompilerParams(
            vmem_limit_bytes=VMEM_ASK, collective_id=1 + layer, has_side_effects=True
        ),
        name="forward_layer",
    )(n, wt, wo, cons, cons, mask, docr, u, cot)


def backward_kernel(
    layer, inner, c_ref, n_ref, wt_ref, wo_ref, con_ref, mask_ref, docr_ref,
    vh_ref, gate_ref, dt_ref, mix_ref, scan_ref, st_ref, u_ref, cot_ref, branch_ref, r_ref,
    cotout_ref, fin_ref, fout_ref, fsmall_ref, next_ref,
    dzbuf, dstate, part, gin, gout, small, own_rows, landing,
    send, recv, send2, recv2, send3, recv3, own, *buffers,
):
    i = pl.program_id(0)
    last = pl.num_programs(0) - 1
    targets = ring_neighbours() + plane_neighbours() + [plane_across(), other_core()]

    @pl.when(i == 0)
    def _():
        greet(targets)

    kept = (vh_ref, gate_ref, dt_ref, mix_ref, scan_ref, st_ref)
    bwd_step(
        i, c_ref, n_ref, wt_ref, wo_ref, con_ref, mask_ref, docr_ref, kept,
        part, gin, gout, small, dzbuf, dstate,
    )

    @pl.when(i == last)
    def _():
        greeted(len(targets))
        collecting, folding = buffers[:8], buffers[8:]
        out, folds, more = Sender(send, recv), Sender(send2, recv2), Sender(send3, recv3)
        run(
            collect_steps(part, collecting, out),
            fold_steps(layer, gin, gout, fin_ref, fout_ref, folding, folds),
        )
        g = collecting[-1][...]
        u = u_ref[...]
        gain = pre_gain_of(con_ref[0])
        width = u.shape[1]
        ri = lax.rsqrt(jnp.mean(u * u, axis=1, keepdims=True) + EPS)
        gg = g * gain
        dot = jnp.sum(gg * u, axis=1, keepdims=True) / width
        c = cot_ref[...] + gg * ri - u * (ri * ri * ri * dot)
        cotout_ref[...] = c
        d_pre = jnp.sum(g * u * ri, axis=0, keepdims=True)
        for k in range(8):
            small[k : k + 1, 3 * HC :] = d_pre[:, k * HC : (k + 1) * HC]
        ending = fold_small(layer, small, fsmall_ref, folding, folds)
        if layer == 1:
            payload_into(own_rows, c, branch_ref[...], r_ref[:, 0:1], inner)
            run(spread_steps(own_rows, landing, more, own.at[0]), ending)
            copy = pltpu.make_async_copy(landing, next_ref, own.at[1])
            copy.start()
            out.sent()
            more.sent()
            copy.wait()
        else:
            run(ending)
            next_ref[...] = jnp.zeros_like(next_ref)
            out.sent()


def backward_layer(layer, inner, c, n, wt, wo, cons, mask, docr, kept, u, cot, branch, r):
    length, width = n.shape
    blocks = length // SPAN
    last = blocks - 1
    mine = u.shape[0]
    wide = width + AUX

    def rows(cols):
        return pl.BlockSpec((SPAN, cols), lambda i: (last - i, 0))

    def stack(a):
        return pl.BlockSpec((1,) + a.shape[1:], lambda i: (last - i, 0, 0))

    def shape(dims, dtype=F32):
        return jax.ShapeDtypeStruct(dims, dtype)

    more = (length, wide) if layer == 1 else (16, HC)
    return pl.pallas_call(
        lambda *refs: backward_kernel(layer, inner, *refs),
        grid=(blocks,),
        in_specs=[
            rows(wide), rows(width), of_layer(wt, layer), of_layer(wo, layer),
            of_layer(cons, layer), rows(mask.shape[1]),
            pl.BlockSpec((8, SPAN), lambda i: (0, last - i)),
            stack(kept[0]), rows(HC), rows(HC), rows(HC), rows(HC), stack(kept[5]),
            whole(u.shape), whole(u.shape), whole(u.shape), whole(r.shape),
        ],
        out_specs=[
            whole(u.shape), whole((WR, 256)), whole((HC // SIDE, width)), whole((8, 4 * HC)),
            pl.BlockSpec(memory_space=pl.ANY) if layer == 1 else whole(more),
        ],
        out_shape=[
            shape(u.shape), shape((WR, 256), BF16), shape((HC // SIDE, width), BF16),
            shape((8, 4 * HC)), shape(more, BF16),
        ],
        scratch_shapes=[
            pltpu.VMEM((SPAN + 8, 3 * HC), F32), pltpu.VMEM((NS, HC), F32),
            pltpu.VMEM((length, width), BF16), pltpu.VMEM((SIDE, WR, 256), F32),
            pltpu.VMEM((HC, width), F32), pltpu.VMEM((8, 4 * HC), F32),
            pltpu.VMEM((mine, wide), BF16), pltpu.VMEM(more, BF16),
            *sems(40), *sems(24), *sems(40), pltpu.SemaphoreType.DMA((2,)),
            *collect_scratch(mine, width), *fold_scratch(),
        ],
        compiler_params=pltpu.CompilerParams(
            vmem_limit_bytes=VMEM_ASK, collective_id=3 + layer, has_side_effects=True
        ),
        name="backward_layer",
    )(c, n, wt, wo, cons, mask, docr, *kept, u, cot, branch, r)


def prepare_kernel(
    doc_ref, cw_ref, cb_ref, dtb_ref, alog_ref, skip_ref, pre_ref, gain_ref,
    con_ref, mask_ref, docr_ref,
):
    q = lax.axis_index(AXIS)
    part = lax.axis_index("section")
    inner = gain_ref.shape[1]
    own = pl.ds(pl.multiple_of(q * HC, HC), HC)
    con_ref[...] = jnp.zeros_like(con_ref)
    con_ref[0:4, :HC] = cw_ref[0, :, own]
    con_ref[0:4, HC : 3 * HC] = cw_ref[0, :, inner:]
    con_ref[4:5, :HC] = cb_ref[:, own]
    con_ref[4:5, HC : 3 * HC] = cb_ref[:, inner:]

    def lanes(ref):
        value = ref[...]
        lane = iota(value.shape, 1)
        two = [
            jnp.sum(jnp.where(lane == 2 * q + h, value, 0.0), axis=1, keepdims=True) for h in (0, 1)
        ]
        return jnp.where(iota((1, HC), 1) < HEAD, two[0], two[1])

    con_ref[5:6, :HC] = lanes(dtb_ref)
    con_ref[5:6, HC : 2 * HC] = jnp.exp(lanes(alog_ref))
    con_ref[5:6, 2 * HC : 3 * HC] = lanes(skip_ref)
    con_ref[6:7, :HC] = gain_ref[:, own]
    for k in range(8):
        con_ref[k : k + 1, 3 * HC :] = pre_ref[:, k * HC : (k + 1) * HC]

    doc = doc_ref[part].astype(F32)
    length = doc.shape[1]
    doc8 = jnp.broadcast_to(doc, (8, length))
    docr_ref[...] = doc8
    at = iota((8, length), 1)
    rows = []
    for k in (1, 2, 3):
        rows.append((pltpu.roll(doc8, k, 1) == doc8) & (at >= k))
    for k in (1, 2, 3):
        rows.append((pltpu.roll(doc8, length - k, 1) == doc8) & (at < length - k))
    before, final = doc8, doc8
    for b in range(length // SPAN):
        inside = (at >= b * SPAN) & (at < (b + 1) * SPAN)
        start = max(b * SPAN - 1, 0)
        end = (b + 1) * SPAN - 1
        before = jnp.where(inside, doc[:, start : start + 1], before)
        final = jnp.where(inside, doc[:, end : end + 1], final)
    rows += [before == doc8, final == doc8]
    sub = iota((8, length), 0)
    first = jnp.zeros((8, length), F32)
    for k, row in enumerate(rows):
        first = jnp.where((sub == k) & row, 1.0, first)
    both = jnp.concatenate([first, doc8, jnp.zeros((HC - 16, length), F32)])
    mask_ref[...] = both.T


def prepare(doc_ids, *params):
    length = doc_ids.shape[2]
    vmem = pl.BlockSpec(memory_space=pltpu.VMEM)
    return pl.pallas_call(
        prepare_kernel,
        in_specs=[vmem] * (1 + len(params)),
        out_specs=[vmem] * 3,
        out_shape=[
            jax.ShapeDtypeStruct((8, 4 * HC), F32), jax.ShapeDtypeStruct((length, HC), F32),
            jax.ShapeDtypeStruct((8, length), F32),
        ],
        compiler_params=pltpu.CompilerParams(vmem_limit_bytes=VMEM_ASK),
        name="prepare",
    )(doc_ids, *params)


def weights_steps(w_ref, wo_ref, wall_ref, woall_ref, own_w, dts, out, own):
    x, y = ring_places()
    q = lax.axis_index(AXIS)
    part, z = lax.axis_index("section"), lax.axis_index("wshard")
    up, down = plane_neighbours()
    half, half_wo = 256, HC // 2

    def at(d):
        return lax.rem(z + d, SIDE)

    mine = pltpu.make_async_copy(own_w, wall_ref.at[part, z], own.at[4])
    mine.start()
    out.go("up", own_w, wall_ref.at[part, z], up)
    out.go("down", own_w, wall_ref.at[part, z], down)
    role = at(SIDE - y)
    woown = woall_ref.at[part]
    wo_mine = wo_ref.at[0, pl.ds(pl.multiple_of(x * HC, HC), HC)]
    first, second = woown.at[pl.ds(0, half_wo)], woown.at[pl.ds(half_wo, half_wo)]
    rows_mine = pltpu.make_async_copy(wo_mine, woown, own.at[5])
    rows_up = out.make("wo_up", wo_mine, woown, up)
    rows_down = out.make("wo_down", wo_mine, woown, down)
    on_up = out.make("wo_on_up", first, first, up)
    on_down = out.make("wo_on_down", second, second, down)

    @pl.when(role == 0)
    def _():
        rows_mine.start()
        rows_up.start()
        rows_down.start()

    yield
    out.arrived("up")
    before, after = wall_ref.at[part, at(3)], wall_ref.at[part, at(1)]
    out.go("on_up", before.at[pl.ds(0, half)], before.at[pl.ds(0, half)], up)
    out.arrived("down")
    out.go("on_down", after.at[pl.ds(half, WR - half)], after.at[pl.ds(half, WR - half)], down)
    mine.wait()
    for k, d in enumerate((0, 3, 1)):
        out.go(("swap", k), wall_ref.at[part, at(d)], wall_ref.at[part, at(d)], other_core())

    yield

    @pl.when(role == 1)
    def _():
        rows_up.wait_recv()
        on_up.start()

    @pl.when(role == 3)
    def _():
        rows_down.wait_recv()
        on_down.start()

    @pl.when(role == 0)
    def _():
        rows_mine.wait()

    @pl.when(role == 2)
    def _():
        on_up.wait_recv()
        on_down.wait_recv()

    out.go("swap_wo", woown, woown, other_core())
    yield
    out.arrived("on_up")
    out.arrived("on_down")
    out.go(("swap", 3), wall_ref.at[part, at(2)], wall_ref.at[part, at(2)], other_core())
    yield
    for k in range(SIDE):
        out.arrived(("swap", k))
    out.arrived("swap_wo")

    @pl.when(role == 0)
    def _():
        rows_up.wait_send()
        rows_down.wait_send()

    @pl.when(role == 1)
    def _():
        on_up.wait_send()

    @pl.when(role == 3)
    def _():
        on_down.wait_send()


def opening_kernel(
    x_ref, og_ref, cons_ref, w_ref, wo_ref, o_ref, u_ref, cot_ref, wall_ref, woall_ref,
    own_rows, own_w, dts, send, recv, send2, recv2, own,
):
    targets = ring_neighbours() + plane_neighbours() + [other_core()]
    greet(targets)
    q = lax.axis_index(AXIS)
    part = lax.axis_index("section")
    inner = (w_ref.shape[0] - 2 * NS) // 2 // HC * HC
    pieces = [
        (pl.ds(pl.multiple_of(q * HC, HC), HC), own_w.at[pl.ds(0, HC)]),
        (pl.ds(pl.multiple_of(inner + q * HC, HC), HC), own_w.at[pl.ds(HC, HC)]),
        (pl.ds(2 * inner, 2 * NS), own_w.at[pl.ds(2 * HC, 2 * NS)]),
        (pl.ds(2 * inner + 2 * NS, dts.shape[0]), dts),
    ]
    copies = [
        pltpu.make_async_copy(w_ref.at[rows], target, own.at[k])
        for k, (rows, target) in enumerate(pieces)
    ]
    for copy in copies:
        copy.start()
    u = x_ref[part, 0].astype(F32)
    u_ref[...] = u
    cot_ref[...] = og_ref[part, 0].astype(F32)
    own_rows[...] = (norm_rows(u) * pre_gain_of(cons_ref[0])).astype(BF16)
    for copy in copies:
        copy.wait()
    heads = dts.shape[0]
    pick = (iota((16, heads), 1) == 2 * q + iota((16, heads), 0)) & (iota((16, heads), 0) < 2)
    own_w[4 * HC :, :] = dot_nn(pick.astype(F32).astype(BF16), dts[...]).astype(BF16)
    greeted(len(targets))
    out, planes = Sender(send, recv), Sender(send2, recv2)
    run(
        weights_steps(w_ref, wo_ref, wall_ref, woall_ref, own_w, dts, planes, own),
        spread_steps(own_rows, o_ref, out, own.at[6]),
    )
    out.sent()
    planes.sent()


def opening(block_input, out_grad, cons, w, wo, heads):
    vmem, hbm = pl.BlockSpec(memory_space=pltpu.VMEM), pl.BlockSpec(memory_space=pl.ANY)
    rows, width = block_input.shape[2:]
    count = lax.axis_size(AXIS)

    def shape(dims, dtype=F32):
        return jax.ShapeDtypeStruct(dims, dtype)

    return pl.pallas_call(
        opening_kernel,
        in_specs=[vmem, vmem, vmem, hbm, hbm],
        out_specs=[vmem] * 5,
        out_shape=[
            shape((count * rows, width), BF16), shape((rows, width)), shape((rows, width)),
            shape((2, SIDE, WR, w.shape[1]), BF16), shape((2, HC, width), BF16),
        ],
        scratch_shapes=[
            pltpu.VMEM((rows, width), BF16), pltpu.VMEM((WR, w.shape[1]), BF16),
            pltpu.VMEM((heads, w.shape[1]), BF16), *sems(40), *sems(16),
            pltpu.SemaphoreType.DMA((7,)),
        ],
        compiler_params=pltpu.CompilerParams(
            collective_id=5, has_side_effects=True, vmem_limit_bytes=VMEM_ASK
        ),
        name="opening",
    )(block_input, out_grad, cons, w, wo)


END_ROWS = 448


def closing_kernel(
    fin0, fout0, fs0, fin1, fout1, fs1, o_ref,
    mixed_in, mixed_out, came, block, landing, send, recv, send2, recv2, own,
):
    me = lax.axis_index(AXIS)
    count = lax.axis_size(AXIS)
    x, y = ring_places()
    z = lax.axis_index("wshard")
    part = lax.axis_index("section")
    others = [{AXIS: lax.rem(me + d, count)} for d in range(1, count)]
    turned = {AXIS: place_of(0, x, z), "wshard": y}

    greet(others)

    @pl.when(z != y)
    def _():
        pl.semaphore_signal(
            pltpu.get_barrier_semaphore(), inc=1, device_id=turned, device_id_type=MESH
        )

    zero = part == 0
    mixed_in[...] = jnp.where(zero, fin0[...], fin1[...])
    mixed_out[...] = jnp.where(zero, fout0[...], fout1[...])
    small = jnp.where(zero, fs0[...], fs1[...])
    greeted(len(others) + (z != y).astype(jnp.int32))
    out, more = Sender(send, recv), Sender(send2, recv2)
    def bc(j):
        return rows_at(mixed_in, 2 * HC + j * 16, 16)

    for d in range(1, count):
        to = lax.rem(me + d, count)
        out.go(d, bc(to), landing.at[d], {AXIS: to})
    turn = out.make("turn", mixed_out, came, turned)

    @pl.when(z != y)
    def _():
        turn.start()

    block[0 : 2 * HC, :] = mixed_in[0 : 2 * HC, :]
    block[2 * HC + 16 : 2 * HC + 32, :] = mixed_in[4 * HC :, :]
    chunks = jnp.concatenate([small[:, :256], small[:, 256:]])
    hi, mid, _ = three(chunks)
    block[END_ROWS - 32 : END_ROWS - 16, :] = hi
    block[END_ROWS - 16 :, :] = mid
    total = mixed_in[pl.ds(pl.multiple_of(2 * HC + me * 16, 16), 16), :].astype(F32)
    for d in range(1, count):
        out.arrived(d)
        total = total + landing[d].astype(F32)
    block[2 * HC : 2 * HC + 16, :] = total.astype(BF16)

    @pl.when(z != y)
    def _():
        turn.wait_recv()

    @pl.when(z == y)
    def _():
        came[...] = mixed_out[...]

    at = 2 * HC + 32
    for c in range(4):
        block[at + 32 * c : at + 32 * (c + 1), :] = came[:, c * 256 : (c + 1) * 256]
    run(spread_steps(block, o_ref, more, own))
    out.sent()
    more.sent()

    @pl.when(z != y)
    def _():
        turn.wait_send()


def closing(*sums):
    vmem = pl.BlockSpec(memory_space=pltpu.VMEM)
    count = lax.axis_size(AXIS)
    width = sums[1].shape[1]
    return pl.pallas_call(
        closing_kernel,
        in_specs=[vmem] * 6,
        out_specs=vmem,
        out_shape=jax.ShapeDtypeStruct((count * END_ROWS, 256), BF16),
        scratch_shapes=[
            pltpu.VMEM((WR, 256), BF16), pltpu.VMEM((HC // SIDE, width), BF16),
            pltpu.VMEM((HC // SIDE, width), BF16), pltpu.VMEM((END_ROWS, 256), BF16),
            pltpu.VMEM((count, 16, 256), BF16), *sems(17), *sems(40), pltpu.SemaphoreType.DMA,
        ],
        compiler_params=pltpu.CompilerParams(
            collective_id=6, has_side_effects=True, vmem_limit_bytes=VMEM_ASK
        ),
        name="closing",
    )(*sums)


def assemble_kernel(
    inner, all_ref, gin_ref, gout_ref, convw_ref, convb_ref, pre_ref, gain_ref, heads_ref
):
    count = all_ref.shape[0]
    lane = iota((1, HC), 1)
    bc = jnp.zeros((5, 2 * HC), F32)
    pre = jnp.zeros((8, HC), F32)
    per_head = [jnp.zeros((1, HC), F32)] * 3
    for j in range(count):
        own = slice(j * HC, (j + 1) * HC)
        gin_ref[own, :] = all_ref[j, 0:HC, :].astype(F32)
        gin_ref[inner + j * HC : inner + (j + 1) * HC, :] = all_ref[j, HC : 2 * HC, :].astype(F32)
        at = 2 * inner + j * 16
        gin_ref[at : at + 16, :] = all_ref[j, 256:272, :].astype(F32)
        at = 2 * inner + 2 * NS + 2 * j
        gin_ref[at : at + 2, :] = all_ref[j, 272:288, :].astype(F32)[0:2, :]
        big, piece = j % SIDE, j // SIDE
        at = big * HC + piece * 32
        for c in range(4):
            gout_ref[at : at + 32, c * 256 : (c + 1) * 256] = (
                all_ref[j, 288 + 32 * c : 320 + 32 * c, :].astype(F32)
            )
        small = all_ref[j, END_ROWS - 32 : END_ROWS - 16, :].astype(F32)
        small = small + all_ref[j, END_ROWS - 16 :, :].astype(F32)
        convw_ref[:, own] = small[0:4, :HC]
        convb_ref[:, own] = small[4:5, :HC]
        gain_ref[:, own] = small[5:6, :HC]
        bc = bc + jnp.concatenate([small[0:5, HC:], small[8:13, :HC]], axis=1)
        pre = pre + small[8:16, HC:]
        skip = small[5:6, HC:]
        for h in (0, 1):
            here = lane == 2 * j + h
            mine = (lane >= h * HEAD) & (lane < (h + 1) * HEAD)
            values = (
                small[6:7, h * HEAD : h * HEAD + 1],
                small[6:7, HC + h * HEAD : HC + h * HEAD + 1],
                jnp.sum(jnp.where(mine, skip, 0.0), axis=1, keepdims=True),
            )
            per_head = [jnp.where(here, v, p) for v, p in zip(values, per_head)]
    convw_ref[:, inner:] = bc[0:4]
    convb_ref[:, inner:] = bc[4:5]
    for k in range(8):
        pre_ref[:, k * HC : (k + 1) * HC] = pre[k : k + 1]
    heads_ref[...] = jnp.concatenate(per_head + [jnp.zeros((5, HC), F32)])


def assemble(everyone, inner, columns, width, channels):
    def shape(*dims):
        return jax.ShapeDtypeStruct(dims, F32)

    vmem = pl.BlockSpec(memory_space=pltpu.VMEM)
    return pl.pallas_call(
        lambda *refs: assemble_kernel(inner, *refs),
        in_specs=[vmem],
        out_specs=[vmem] * 7,
        out_shape=[
            shape(columns, 256), shape(512, width), shape(4, channels), shape(1, channels),
            shape(1, width), shape(1, inner), shape(8, HC),
        ],
        compiler_params=pltpu.CompilerParams(vmem_limit_bytes=VMEM_ASK),
        name="assemble",
    )(everyone)


def body(
    block_input, doc_ids, out_grad, in_proj, out_proj, conv_weight, conv_bias,
    dt_bias, a_log, skip_scale, pre_gain, norm_gain,
):
    part = lax.axis_index("section")
    inner = norm_gain.shape[1]
    width = block_input.shape[3]
    heads = dt_bias.shape[1]
    con, mask, docr = prepare(
        doc_ids, conv_weight, conv_bias, dt_bias, a_log, skip_scale, pre_gain, norm_gain
    )
    cons = lax.all_gather(con, "section", axis=0)
    n0, u0, cot, wt, wo = opening(
        block_input, out_grad, cons, jnp.swapaxes(in_proj[0], 0, 1), out_proj, heads
    )
    shared = (wt, wo, cons, mask, docr)
    *kept0, h0, branch0, r0, n1 = forward_layer(0, inner, n0, *shared, u0, cot)
    *kept1, h1, _, r1, c1 = forward_layer(1, inner, n1, *shared, h0, cot)
    g1, *sums1, c0 = backward_layer(1, inner, c1, n1, *shared, kept1, h0, cot, branch0, r0)
    g0, *sums0, _ = backward_layer(0, inner, c0, n0, *shared, kept0, u0, g1, branch0, r0)

    def by_layer(first, second):
        mine = jnp.where(part == 0, first, second)
        other = lax.ppermute(jnp.where(part == 0, second, first), "section", [(0, 1), (1, 0)])
        pair = jnp.where(part == 0, jnp.stack([mine, other]), jnp.stack([other, mine]))
        return pair[None, :, None]

    hidden = by_layer(h0, h1)
    input_grads = by_layer(g0, g1)
    everyone = closing(*sums0, *sums1).reshape(-1, END_ROWS, 256)
    gin, gout, convw, convb, pre, gain, per_head = assemble(
        everyone, inner, in_proj.shape[2], width, conv_weight.shape[2]
    )
    return (
        hidden, input_grads, jnp.swapaxes(gin, 0, 1)[None], gout[None], convw[None], convb,
        per_head[0:1, :heads], per_head[1:2, :heads], per_head[2:3, :heads], pre, gain,
    )


def solution(mesh):
    specs = (
        P(None, "wshard", "seq", None),
        P(None, "wshard", None),
        P(None, "wshard", "seq", None),
        P("section", "wshard", None),
        P("section", "wshard", None),
        P("section", None, None),
        P("section", None),
        P("section", None),
        P("section", None),
        P("section", None),
        P("section", None),
        P("section", None),
    )
    outs = (
        P("section", None, "wshard", "seq", None),
        P("section", None, "wshard", "seq", None),
        P("section", "wshard", None),
        P("section", "wshard", None),
        P("section", None, None),
    ) + (P("section", None),) * 6
    return jax.shard_map(body, mesh=mesh, in_specs=specs, out_specs=outs, check_vma=False)
```

```python
import jax
import jax.numpy as jnp
from jax import lax
from jax.experimental import pallas as pl
from jax.experimental.pallas import tpu as pltpu
from jax.sharding import PartitionSpec as P

SPAN = 256
EPS = 1e-05
F32 = jnp.float32
BF16 = jnp.bfloat16
MESH = pl.DeviceIdType.MESH
VMEM_ASK = 60 * 1024 * 1024

HC = 128
NS = 128
WR = 528
FR = 272
END_ROWS = 320
AUX = 128
HEAD = 64
SIDE = 4
AXIS = "seq"


def dot_nn(a, b):
    return lax.dot_general(a, b, (((1,), (0,)), ((), ())), preferred_element_type=F32)


def dot_nt(a, b):
    return lax.dot_general(a, b, (((1,), (1,)), ((), ())), preferred_element_type=F32)


def dot_tn(a, b):
    return lax.dot_general(a, b, (((0,), (0,)), ((), ())), preferred_element_type=F32)


def three(x):
    hi = x.astype(BF16)
    rest = x - hi.astype(F32)
    mid = rest.astype(BF16)
    low = (rest - mid.astype(F32)).astype(BF16)
    return hi, mid, low


def exact_left(ones, x):
    hi, mid, low = three(x)
    return dot_nn(ones, hi) + dot_nn(ones, mid) + dot_nn(ones, low)


def exact_right(x, ones):
    hi, mid, low = three(x)
    return dot_nn(hi, ones) + dot_nn(mid, ones) + dot_nn(low, ones)


def iota(shape, dim):
    return lax.broadcasted_iota(jnp.int32, shape, dim)


def sigmoid(x):
    return 1.0 / (1.0 + jnp.exp(-x))


def softplus(x):
    return jnp.maximum(x, 0.0) + jnp.log1p(jnp.exp(-jnp.abs(x)))


def conv_rows(vbuf, con, mask):
    z = vbuf[pl.ds(8, SPAN), :] * con[3:4, :] + con[4:5, :]
    for k in (1, 2, 3):
        z = z + vbuf[pl.ds(8 - k, SPAN), :] * con[3 - k : 4 - k, :] * mask[:, k - 1 : k]
    return z


def block_terms(dt, vec, mask, docr):
    step = softplus(dt + vec[0])
    log_decay = -step * vec[1]
    rows, cols = iota((SPAN, SPAN), 0), iota((SPAN, SPAN), 1)
    lower = rows >= cols
    running = exact_left(lower.astype(F32).astype(BF16), log_decay)
    turned = running.T
    allowed = lower & (mask[:, 8:9] == docr)
    decays = []
    for h in (0, 1):
        gaps = running[:, h * HEAD : h * HEAD + 1] - turned[h * HEAD : h * HEAD + 1, :]
        decays.append(jnp.exp(jnp.where(allowed, gaps, -1e30)))
    reach = jnp.exp(running) * mask[:, 6:7]
    total = running[SPAN - 1 :, :]
    tail = jnp.exp(total - running) * mask[:, 7:8]
    carry = jnp.exp(total) * mask[SPAN - 1 :, 6:7]
    return step, log_decay, decays, reach, tail, carry


def layer_constants(con):
    return con[5:6, :HC], con[5:6, HC : 2 * HC], con[5:6, 2 * HC : 3 * HC], con[6:7, :HC]


def pre_gain_of(con):
    return jnp.concatenate([con[k : k + 1, 3 * HC : 4 * HC] for k in range(8)], axis=1)


def head_ones():
    return (iota((16, HC), 0) == iota((16, HC), 1) // HEAD).astype(F32).astype(BF16)


def head_firsts():
    return (iota((HC, 16), 0) == iota((HC, 16), 1) * HEAD).astype(F32).astype(BF16)


def lanes_of(columns, rows):
    lane = iota((rows, AUX), 1)
    out = jnp.zeros((rows, AUX), F32)
    for k, column in enumerate(columns):
        out = jnp.where(lane == k, column.astype(F32), out)
    return out.astype(BF16)


def at_block(b):
    return pl.ds(pl.multiple_of(b * SPAN, SPAN), SPAN)


def fwd_step(layer, b, s):
    vh = s.vh.at[layer, b]
    rows = at_block(b)

    @pl.when(b == 0)
    def _():
        vh[0:8, :] = jnp.zeros((8, 3 * HC), F32)
        s.state[...] = jnp.zeros_like(s.state)

    @pl.when(b != 0)
    def _():
        vh[0:8, :] = s.vh[layer, jnp.maximum(b - 1, 0), SPAN:, :]

    width = s.wo.shape[2]
    chunk = s.wt.shape[3]
    mask = s.mask[rows, :]
    con = s.cons[layer]
    vec = layer_constants(con)
    conv = con[:, : 3 * HC]
    proj = dot_nt(s.n[layer, rows, 0:chunk], s.wt[layer, 0])
    for k in range(1, SIDE):
        proj = proj + dot_nt(s.n[layer, rows, k * chunk : (k + 1) * chunk], s.wt[layer, k])
    gate = proj[:, :HC]
    v = proj[:, HC : 4 * HC].astype(BF16).astype(F32)
    dt = dot_nn(proj[:, 4 * HC :].astype(BF16), head_ones())
    vh[8:, :] = v
    z = conv_rows(vh, conv, mask)
    act = z * sigmoid(z)
    xc = act[:, :HC]
    b16 = act[:, HC : 2 * HC].astype(BF16)
    c16 = act[:, 2 * HC :].astype(BF16)
    step, _, decays, reach, tail, carry = block_terms(dt, vec, mask, s.docr[b, 0:1, :])
    xs = xc * step
    xs16 = xs.astype(BF16)
    scores = dot_nt(c16, b16)
    within = [dot_nn((scores * d).astype(BF16), xs16) for d in decays]
    first = iota((SPAN, HC), 1) < HEAD
    st = s.state[...]
    s.st[layer, b] = st
    scan = jnp.where(first, within[0], within[1]) + dot_nn(c16, st.astype(BF16)) * reach
    s.state[...] = st * carry + dot_tn(b16, (xs * tail).astype(BF16))
    mixed = (scan + xc * vec[2]).astype(BF16)
    g = mixed.astype(F32) * (gate * sigmoid(gate))
    s.part[rows, :width] = dot_nn((g * vec[3]).astype(BF16), s.wo[layer]).astype(BF16)
    s.part[rows, width:] = lanes_of(three(jnp.sum(g * g, axis=1, keepdims=True)), SPAN)
    s.gate[layer, rows, :] = gate
    s.dt[layer, rows, :] = dt
    s.mix[layer, rows, :] = mixed
    s.scan[layer, rows, :] = scan


def bwd_step(layer, b, s):
    rows_b = at_block(b)
    vbuf = s.vh.at[layer, b]
    gin, gout, small, dzbuf, dstate = s.gin, s.gout, s.small, s.dz, s.state

    @pl.when(b == s.vh.shape[1] - 1)
    def _():
        dzbuf[SPAN:, :] = jnp.zeros((8, 3 * HC), F32)
        dstate[...] = jnp.zeros_like(dstate)
        gin[...] = jnp.zeros_like(gin)
        gout[...] = jnp.zeros_like(gout)
        small[...] = jnp.zeros_like(small)

    width = s.wo.shape[2]
    chunk = s.wt.shape[3]
    mask = s.mask[rows_b, :]
    con = s.cons[layer]
    vec = layer_constants(con)
    conv = con[:, : 3 * HC]
    cot = s.c[layer, rows_b, :width]
    aux = s.c[layer, rows_b, width:].astype(F32)
    r = aux[:, 0:1] + aux[:, 1:2] + aux[:, 2:3]
    pull = aux[:, 3:4] + aux[:, 4:5]
    gate = s.gate[layer, rows_b, :]
    sg = sigmoid(gate)
    silu = gate * sg
    mixed = s.mix[layer, rows_b, :].astype(F32)
    g = mixed * silu
    gain = vec[3]
    dy = dot_nt(cot, s.wo[layer])
    gr = g * r
    gout[...] += dot_tn((gr * gain).astype(BF16), cot)
    d_gain = jnp.sum(dy * gr, axis=0, keepdims=True)
    dg = dy * (r * gain) - g * pull
    dm16 = (dg * silu).astype(BF16)
    dm = dm16.astype(F32)
    dgate = dg * mixed * (sg * (1.0 + gate * (1.0 - sg)))

    z = conv_rows(vbuf, conv, mask)
    sz = sigmoid(z)
    act = z * sz
    xc = act[:, :HC]
    b16 = act[:, HC : 2 * HC].astype(BF16)
    c16 = act[:, 2 * HC :].astype(BF16)
    dt = s.dt[layer, rows_b, :]
    step, log_decay, decays, reach, tail, carry = block_terms(dt, vec, mask, s.docr[b, 0:1, :])
    xs16 = (xc * step).astype(BF16)
    xs = xs16.astype(F32)
    scores = dot_nt(c16, b16)
    first = iota((SPAN, HC), 1) < HEAD
    zero16 = jnp.zeros((SPAN, HC), BF16)
    dscores = jnp.zeros((SPAN, SPAN), F32)
    dxs = []
    for h in (0, 1):
        own = jnp.where(first, dm16, zero16) if h == 0 else jnp.where(first, zero16, dm16)
        dp = dot_nt(own, xs16)
        dscores = dscores + dp * decays[h]
        dxs.append(dot_tn((scores * decays[h]).astype(BF16), dm16))
    ds16 = dscores.astype(BF16)
    st = s.st[layer, b]
    dst = dstate[...]
    dst16 = dst.astype(BF16)
    dcs16 = (dm * reach).astype(BF16)
    dc = dot_nn(ds16, b16) + dot_nt(dcs16, st.astype(BF16))
    db = dot_tn(ds16, c16) + dot_nt((xs * tail).astype(BF16), dst16)
    dxs_tail = dot_nn(b16, dst16) * tail
    dxs_all = jnp.where(first, dxs[0], dxs[1]) + dxs_tail
    dstate[...] = dst * carry + dot_tn(c16, dcs16)

    d_total = jnp.sum(xs * dxs_tail, axis=0, keepdims=True) + carry * jnp.sum(
        dst * st, axis=0, keepdims=True
    )
    flow = dm * s.scan[layer, rows_b, :] - xs * dxs_all
    rows, cols = iota((SPAN, SPAN), 0), iota((SPAN, SPAN), 1)
    upper = (cols >= rows).astype(F32).astype(BF16)
    flow = exact_left(upper, flow) + d_total
    same_head = ((iota((HC, HC), 0) < HEAD) == (iota((HC, HC), 1) < HEAD)).astype(F32).astype(BF16)
    d_log = exact_right(flow, same_head)
    d_step = exact_right(dxs_all * xc, same_head) - d_log * vec[1]
    d_alog = jnp.sum(d_log * log_decay, axis=0, keepdims=True)
    d_dt = d_step * sigmoid(dt + vec[0])
    d_skip = jnp.sum(dm * xc, axis=0, keepdims=True)
    d_xc = dm * vec[2] + dxs_all * step

    dact = sz * (1.0 + z * (1.0 - sz))
    dzbuf[:SPAN, 0:HC] = d_xc * dact[:, :HC]
    dzbuf[:SPAN, HC : 2 * HC] = db * dact[:, HC : 2 * HC]
    dzbuf[:SPAN, 2 * HC :] = dc * dact[:, 2 * HC :]
    dz = dzbuf[:SPAN, :]
    dv = dz * conv[3:4, :]
    small[3:4, : 3 * HC] += jnp.sum(dz * vbuf[pl.ds(8, SPAN), :], axis=0, keepdims=True)
    small[4:5, : 3 * HC] += jnp.sum(dz, axis=0, keepdims=True)
    for k in (1, 2, 3):
        dv = dv + dzbuf[pl.ds(k, SPAN), :] * conv[3 - k : 4 - k, :] * mask[:, 2 + k : 3 + k]
        small[3 - k : 4 - k, : 3 * HC] += jnp.sum(
            dz * vbuf[pl.ds(8 - k, SPAN), :] * mask[:, k - 1 : k], axis=0, keepdims=True
        )
    dzbuf[SPAN:, :] = dz[:8, :]
    small[5:6, 0:HC] += d_gain
    small[5:6, HC : 2 * HC] += d_skip
    small[6:7, 0:HC] += jnp.sum(d_dt, axis=0, keepdims=True)
    small[6:7, HC : 2 * HC] += d_alog

    gp = jnp.concatenate([dgate.astype(BF16), dv.astype(BF16)], axis=1)
    gdt = dot_nn(d_dt.astype(BF16), head_firsts()).astype(BF16)
    wide = 4 * HC
    n = s.n[layer, rows_b, :]
    gin[:wide] += dot_nn(gp.T, n)
    gin[wide:] += dot_tn(gdt, n)
    for k in range(SIDE):
        cols_k = slice(k * chunk, (k + 1) * chunk)
        term = dot_nn(gp, s.wt[layer, k, :wide]) + dot_nn(gdt, s.wt[layer, k, wide:])
        s.part[rows_b, cols_k] = term.astype(BF16)
        d_pre = jnp.sum(term * n[:, cols_k].astype(F32), axis=0, keepdims=True)
        small[2 * k : 2 * k + 1, 3 * HC :] += d_pre[:, :HC]
        small[2 * k + 1 : 2 * k + 2, 3 * HC :] += d_pre[:, HC:]


def place_of(half, f, s):
    f, s = lax.rem(f, SIDE), lax.rem(s, SIDE)
    return s * SIDE + f if half == 0 else f * SIDE + s


def ring_places():
    me = lax.axis_index(AXIS)
    return me % SIDE, me // SIDE


def ring_neighbours():
    x, y = ring_places()
    steps = ((1, 0), (3, 0), (0, 1), (0, 3))
    return [{AXIS: place_of(0, x + dx, y + dy)} for dx, dy in steps]


def plane_neighbours():
    z = lax.axis_index("wshard")
    return [{"wshard": lax.rem(z + 1, SIDE)}, {"wshard": lax.rem(z + 3, SIDE)}]


def plane_across():
    return {"wshard": lax.rem(lax.axis_index("wshard") + 2, SIDE)}


def other_core():
    return {"section": 1 - lax.axis_index("section")}


def greet(targets):
    barrier = pltpu.get_barrier_semaphore()
    for target in targets:
        pl.semaphore_signal(barrier, inc=1, device_id=target, device_id_type=MESH)


def greeted(count):
    pl.semaphore_wait(pltpu.get_barrier_semaphore(), count)


def run(*parts, until=None):
    live = list(parts)
    while live if until is None else until in live:
        for part in list(live):
            try:
                next(part)
            except StopIteration:
                live.remove(part)
    return live


class Sender:
    def __init__(self, send, recv):
        self.send, self.recv, self.used, self.copies, self.free = send, recv, 0, {}, set()

    def make(self, name, source, target, to):
        copy = pltpu.make_async_remote_copy(
            src_ref=source, dst_ref=target, send_sem=self.send.at[self.used],
            recv_sem=self.recv.at[self.used], device_id=to, device_id_type=MESH,
        )
        self.used += 1
        self.copies[name] = copy
        return copy

    def go(self, name, source, target, to):
        self.make(name, source, target, to).start()
        self.free.add(name)

    def arrived(self, name):
        self.copies[name].wait_recv()

    def sent(self):
        for name in self.copies:
            if name in self.free:
                self.copies[name].wait_send()


def rows_at(ref, start, size):
    return ref.at[pl.ds(pl.multiple_of(start, 16), size)]


def spread_steps(x_ref, o_ref, out, own, tag=""):
    x, y = ring_places()
    rows = x_ref.shape[0]
    half_rows, quarter = rows // 2, rows // 4
    mine = pltpu.make_async_copy(x_ref, rows_at(o_ref, place_of(0, x, y) * rows, rows), own)
    mine.start()
    firsts = ((x, y), (y, x))

    def go(name, half, block, offset, size, to, source=None):
        place = rows_at(o_ref, block * rows + half * half_rows + offset, size)
        out.go((tag, half, name), place if source is None else source, place, {AXIS: to})

    def across(half, d):
        f, s = firsts[half]
        block = place_of(half, f + d, s)
        source = x_ref.at[pl.ds(half * half_rows, half_rows)] if d == 0 else None
        go(("t1", d), half, block, 0, half_rows, place_of(half, f, s + 1), source)
        go(("t2", d), half, block, 0, half_rows, place_of(half, f, s + 3), source)

    def onward(half, d):
        f, s = firsts[half]
        out.arrived((tag, half, ("t1", d)))
        go(("u1", d), half, place_of(half, f + d, s + 3), 0, quarter, place_of(half, f, s + 1))
        out.arrived((tag, half, ("t2", d)))
        go(("u2", d), half, place_of(half, f + d, s + 1), quarter, quarter, place_of(half, f, s + 3))

    for half in (0, 1):
        f, s = firsts[half]
        source = x_ref.at[pl.ds(half * half_rows, half_rows)]
        block = place_of(half, f, s)
        go("s1", half, block, 0, half_rows, place_of(half, f + 1, s), source)
        go("s2", half, block, 0, half_rows, place_of(half, f + 3, s), source)
    for half in (0, 1):
        across(half, 0)
    yield
    for half in (0, 1):
        f, s = firsts[half]
        out.arrived((tag, half, "s1"))
        go("s3", half, place_of(half, f + 3, s), 0, quarter, place_of(half, f + 1, s))
        out.arrived((tag, half, "s2"))
        go("s4", half, place_of(half, f + 1, s), quarter, quarter, place_of(half, f + 3, s))
    for half in (0, 1):
        across(half, 3)
        across(half, 1)
    yield
    for half in (0, 1):
        onward(half, 0)
    for half in (0, 1):
        out.arrived((tag, half, "s3"))
        out.arrived((tag, half, "s4"))
        across(half, 2)
    yield
    for d in (3, 1, 2):
        for half in (0, 1):
            onward(half, d)
        yield
    for half in (0, 1):
        for d in range(SIDE):
            out.arrived((tag, half, ("u1", d)))
            out.arrived((tag, half, ("u2", d)))
    mine.wait()


def collect_scratch(rows, cols):
    half_rows, quarter = rows // 2, rows // 4
    return [
        pltpu.VMEM((2, SIDE, 2, quarter, cols), BF16),
        pltpu.VMEM((2, SIDE, 2, half_rows, cols), BF16),
        pltpu.VMEM((2, SIDE, 2, half_rows, cols), BF16),
        pltpu.VMEM((2, SIDE, half_rows, cols), BF16),
        pltpu.VMEM((2, SIDE, half_rows, cols), BF16),
        pltpu.VMEM((rows, cols), F32),
    ]


def collect_steps(x_ref, buffers, out, wide):
    cols = pl.ds(0, wide)
    far, near, stage, stage2, last = [a.at[..., cols] for a in buffers[:5]]
    x_ref, o_ref = x_ref.at[:, cols], buffers[5].at[:, cols]
    x, y = ring_places()
    rows = o_ref.shape[0]
    half_rows, quarter = rows // 2, rows // 4
    firsts = ((x, y), (y, x))
    order = (2, 1, 3, 0)

    def go(name, half, source, target, to):
        out.go((half, name), source, target, {AXIS: to})

    def start_of(half, f, s):
        return pl.multiple_of(place_of(half, f, s) * rows + half * half_rows, 16)

    for d in order:
        for half in (0, 1):
            f, s = firsts[half]
            start = start_of(half, f + d, s + 2)
            go(("a1", d), half, rows_at(x_ref, start, quarter), far.at[half, d, 0],
               place_of(half, f, s + 1))
            go(("a2", d), half, rows_at(x_ref, start + quarter, quarter), far.at[half, d, 1],
               place_of(half, f, s + 3))
    yield
    for d in order:
        for half in (0, 1):
            f, s = firsts[half]
            for side, step in enumerate((1, 3)):
                start = start_of(half, f + d, s + step)
                plain, through = quarter * (1 - side), quarter * side
                stage[half, d, side, pl.ds(plain, quarter)] = x_ref[
                    pl.ds(pl.multiple_of(start + plain, 16), quarter), :
                ]
                out.arrived((half, (("a1", "a2")[side], d)))
                stage[half, d, side, pl.ds(through, quarter)] = (
                    x_ref[pl.ds(pl.multiple_of(start + through, 16), quarter), :].astype(F32)
                    + far[half, d, side].astype(F32)
                ).astype(BF16)
                go((("b1", "b2")[side], d), half, stage.at[half, d, side], near.at[half, d, side],
                   place_of(half, f, s + step))
        if d in (1, 0):
            yield

    def summed(half, d):
        f, s = firsts[half]
        out.arrived((half, ("b1", d)))
        out.arrived((half, ("b2", d)))
        return (
            x_ref[pl.ds(start_of(half, f + d, s), half_rows), :].astype(F32)
            + near[half, d, 0].astype(F32) + near[half, d, 1].astype(F32)
        )

    for d in order[:3]:
        for half in (0, 1):
            f, s = firsts[half]
            stage2[half, d] = summed(half, d).astype(BF16)
            go(("first", d), half, stage2.at[half, d], last.at[half, d], place_of(half, f + d, s))
        yield
    for half in (0, 1):
        o_ref[pl.ds(half * half_rows, half_rows), :] = summed(half, 0)
    yield
    for half in (0, 1):
        own = pl.ds(half * half_rows, half_rows)
        total = o_ref[own, :]
        for d in (1, 3, 2):
            out.arrived((half, ("first", d)))
            total = total + last[half, d].astype(F32)
        o_ref[own, :] = total


def half_of(rows):
    return rows // 32 * 16


def fold_scratch(count):
    scratch = [pltpu.VMEM((8, 4 * HC), F32)] * 2 + [pltpu.VMEM((3, 8, 4 * HC), F32)]
    for rows, cols in ((FR, 256), (HC // SIDE, 1024)):
        scratch += [pltpu.VMEM((SIDE, rows, cols), BF16)] * 3
        scratch += [pltpu.VMEM((2, rows - half_of(rows), cols), BF16)]
        scratch += [pltpu.VMEM((2, rows, cols), BF16)]
    scratch += [pltpu.VMEM((2 * NS, 1024), BF16), pltpu.VMEM((count, 16, 1024), BF16)]
    scratch += [pltpu.VMEM((SIDE, 16, 256), BF16)] * 3 + [pltpu.VMEM((3, 16, 256), BF16)]
    return scratch


def bc_steps(gin, buffers, out):
    me, count = lax.axis_index(AXIS), lax.axis_size(AXIS)
    terms, landing, mine = buffers[13], buffers[14], buffers[15]
    terms[...] = gin[2 * HC : 4 * HC, :].astype(BF16)
    for d in range(1, count):
        to = lax.rem(me + d, count)
        out.go(("bc", d), rows_at(terms, to * 16, 16), landing.at[d], {AXIS: to})
    yield
    yield
    total = terms[pl.ds(pl.multiple_of(me * 16, 16), 16), :].astype(F32)
    for d in range(1, count):
        out.arrived(("bc", d))
        total = total + landing[d].astype(F32)
    for k in range(SIDE):
        mine[k] = total[:, k * 256 : (k + 1) * 256].astype(BF16)
    yield


def fold_steps(layer, gin, gout, fin_ref, fout_ref, buffers, out):
    z = lax.axis_index("wshard")
    up, down = plane_neighbours()
    owner = lax.axis_index("section") == layer
    ours_in, land_in, total_in, far_in, near_in = buffers[3:8]
    ours_out, land_out, total_out, far_out, near_out = buffers[8:13]
    piece = HC // SIDE
    for k in range(SIDE):
        cols = slice(k * 256, (k + 1) * 256)
        ours_in[k, : 2 * HC] = gin[: 2 * HC, cols].astype(BF16)
        ours_in[k, 2 * HC :] = gin[4 * HC :, cols].astype(BF16)
        ours_out[k] = gout[k * piece : (k + 1) * piece, :].astype(BF16)
    arrays = (
        (ours_in, land_in, total_in, far_in, near_in, fin_ref),
        (ours_out, land_out, total_out, far_out, near_out, fout_ref),
    )

    def at(d):
        return lax.rem(z + d, SIDE)

    swaps, legs = {}, {}
    parts = []
    for ours in (ours_in, ours_out):
        half = half_of(ours.shape[1])
        parts.append((pl.ds(0, half), pl.ds(half, ours.shape[1] - half)))
    for d in (2, 1, 3, 0):
        for k, (ours, land, *_) in enumerate(arrays):
            swaps[k, d] = out.make(("swap", k, d), ours.at[at(d)], land.at[at(d)], other_core())
    for k, (_, _, total, far, near, _) in enumerate(arrays):
        for side, to in enumerate((up, down)):
            some = parts[k][side]
            legs[k, "far", side] = out.make(
                ("far", k, side), total.at[at(2), some], far.at[side, pl.ds(0, some.size)], to
            )
        legs[k, "near", 0] = out.make(("near", k, 0), total.at[at(1)], near.at[0], up)
        legs[k, "near", 1] = out.make(("near", k, 1), total.at[at(3)], near.at[1], down)

    @pl.when(jnp.logical_not(owner))
    def _():
        for copy in swaps.values():
            copy.start()

    yield

    def add_cores(d):
        for k, (ours, land, total, *_) in enumerate(arrays):
            swaps[k, d].wait_recv()
            total[at(d)] = (ours[at(d)].astype(F32) + land[at(d)].astype(F32)).astype(BF16)

    @pl.when(owner)
    def _():
        add_cores(2)
        for k in (0, 1):
            legs[k, "far", 0].start()
            legs[k, "far", 1].start()

    yield
    for side, d in ((0, 1), (1, 3)):
        @pl.when(owner)
        def _():
            add_cores(d)
            for k, (_, _, total, far, _, _) in enumerate(arrays):
                legs[k, "far", side].wait_recv()
                some = parts[k][side]
                total[at(d), some] = (
                    total[at(d), some].astype(F32) + far[side, pl.ds(0, some.size)].astype(F32)
                ).astype(BF16)
                legs[k, "near", side].start()

        yield

    @pl.when(owner)
    def _():
        add_cores(0)
        for k, (_, _, total, _, near, done) in enumerate(arrays):
            legs[k, "near", 0].wait_recv()
            legs[k, "near", 1].wait_recv()
            done[...] = (
                total[at(0)].astype(F32) + near[0].astype(F32) + near[1].astype(F32)
            ).astype(BF16)
        for leg in legs.values():
            leg.wait_send()

    @pl.when(jnp.logical_not(owner))
    def _():
        for copy in swaps.values():
            copy.wait_send()


def fold_small(layer, small, gains, done_ref, bc_ref, buffers, out):
    small[:, 3 * HC :] = small[:, 3 * HC :] / gains
    owner = lax.axis_index("section") == layer
    z = lax.axis_index("wshard")
    land, total, planes = buffers[:3]
    mine, land_bc, total_bc, planes_bc = buffers[15:19]
    up, down = plane_neighbours()
    swaps = [
        out.make("small", small, land, other_core()), out.make("bc", mine, land_bc, other_core()),
    ]
    legs = []
    for k, (d, to) in enumerate(((1, up), (3, down), (2, plane_across()))):
        legs.append(out.make(("small", k), total, planes.at[k], to))
        legs.append(out.make(
            ("bc", k), total_bc.at[lax.rem(z + d, SIDE)], planes_bc.at[k], to))

    @pl.when(jnp.logical_not(owner))
    def _():
        for swap in swaps:
            swap.start()

    @pl.when(owner)
    def _():
        for swap in swaps:
            swap.wait_recv()
        total[...] = small[...] + land[...]
        total_bc[...] = (mine[...].astype(F32) + land_bc[...].astype(F32)).astype(BF16)
        for leg in legs:
            leg.start()

    yield

    @pl.when(owner)
    def _():
        for leg in legs:
            leg.wait_recv()
        done_ref[...] = total[...] + planes[0] + planes[1] + planes[2]
        sum_bc = total_bc[z].astype(F32)
        for k in range(3):
            sum_bc = sum_bc + planes_bc[k].astype(F32)
        bc_ref[...] = sum_bc.astype(BF16)
        for leg in legs:
            leg.wait_send()

    @pl.when(jnp.logical_not(owner))
    def _():
        for swap in swaps:
            swap.wait_send()


def closing_steps(s, layer_sums, out, own):
    x, y = ring_places()
    z = lax.axis_index("wshard")
    first = lax.axis_index("section") == 0
    fin, bc, fout, small = [
        jnp.where(first, a[...], b[...]) for a, b in zip(layer_sums[0], layer_sums[1])
    ]
    s.turning[...] = fout
    turned = {AXIS: place_of(0, x, z), "wshard": y}
    turn = out.make("turn", s.turning, s.came, turned)

    @pl.when(z != y)
    def _():
        turn.start()

    s.block[0 : 2 * HC, :] = fin[: 2 * HC]
    s.block[2 * HC : 2 * HC + 16, :] = bc
    s.block[2 * HC + 16 : 2 * HC + 32, :] = fin[2 * HC :]
    hi, mid, _ = three(jnp.concatenate([small[:, :256], small[:, 256:]]))
    s.block[END_ROWS - 32 : END_ROWS - 16, :] = hi
    s.block[END_ROWS - 16 :, :] = mid
    main = spread_steps(s.block, s.gathered, out, own.at[2], "in")
    next(main)
    yield
    next(main)

    @pl.when(z != y)
    def _():
        turn.wait_recv()

    @pl.when(z == y)
    def _():
        s.came[...] = s.turning[...]

    for c in range(4):
        s.wide_rows[32 * c : 32 * (c + 1), :] = s.came[:, c * 256 : (c + 1) * 256]
    side = spread_steps(s.wide_rows, s.pieces, out, own.at[3], "out")
    live = [main, side]
    while live:
        for part in list(live):
            try:
                next(part)
            except StopIteration:
                live.remove(part)
        yield

    @pl.when(z != y)
    def _():
        turn.wait_send()


def norm_rows(u):
    return u * lax.rsqrt(jnp.mean(u * u, axis=1, keepdims=True) + EPS)


def payload_into(ref, c, branch, r, inner):
    width = c.shape[1]
    low = c.astype(BF16)
    pull = r * r * jnp.sum(low.astype(F32) * branch, axis=1, keepdims=True) / inner
    ref[:, :width] = low
    ref[:, width:] = lanes_of(list(three(r)) + list(three(pull))[:2], c.shape[0])


def constants_into(con, params):
    cw_ref, cb_ref, dtb_ref, alog_ref, skip_ref, pre_ref, gain_ref = params
    q = lax.axis_index(AXIS)
    inner = gain_ref.shape[1]
    own = pl.ds(pl.multiple_of(q * HC, HC), HC)
    con[...] = jnp.zeros_like(con)
    con[0:4, :HC] = cw_ref[0, :, own]
    con[0:4, HC : 3 * HC] = cw_ref[0, :, inner:]
    con[4:5, :HC] = cb_ref[:, own]
    con[4:5, HC : 3 * HC] = cb_ref[:, inner:]

    def lanes(ref):
        value = ref[...]
        lane = iota(value.shape, 1)
        two = [
            jnp.sum(jnp.where(lane == 2 * q + h, value, 0.0), axis=1, keepdims=True) for h in (0, 1)
        ]
        return jnp.where(iota((1, HC), 1) < HEAD, two[0], two[1])

    con[5:6, :HC] = lanes(dtb_ref)
    con[5:6, HC : 2 * HC] = jnp.exp(lanes(alog_ref))
    con[5:6, 2 * HC : 3 * HC] = lanes(skip_ref)
    con[6:7, :HC] = gain_ref[:, own]
    for k in range(8):
        con[k : k + 1, 3 * HC :] = pre_ref[:, k * HC : (k + 1) * HC]


def mask_steps(doc_ref, mask_ref, docr_ref):
    yield
    doc = doc_ref[lax.axis_index("section")].astype(F32)
    length = doc.shape[1]
    doc8 = jnp.broadcast_to(doc, (8, length))
    for b in range(length // SPAN):
        docr_ref[b] = doc8[:, b * SPAN : (b + 1) * SPAN]
    at = iota((8, length), 1)
    rows = []
    for k in (1, 2, 3):
        rows.append((pltpu.roll(doc8, k, 1) == doc8) & (at >= k))
    for k in (1, 2, 3):
        rows.append((pltpu.roll(doc8, length - k, 1) == doc8) & (at < length - k))
    before, final = doc8, doc8
    for b in range(length // SPAN):
        inside = (at >= b * SPAN) & (at < (b + 1) * SPAN)
        start = max(b * SPAN - 1, 0)
        end = (b + 1) * SPAN - 1
        before = jnp.where(inside, doc[:, start : start + 1], before)
        final = jnp.where(inside, doc[:, end : end + 1], final)
    rows += [before == doc8, final == doc8]
    sub = iota((8, length), 0)
    first = jnp.zeros((8, length), F32)
    for k, row in enumerate(rows):
        first = jnp.where((sub == k) & row, 1.0, first)
    both = jnp.concatenate([first, doc8, jnp.zeros((HC - 16, length), F32)])
    mask_ref[...] = both.T


def sems(count):
    return [pltpu.SemaphoreType.DMA((count,)), pltpu.SemaphoreType.DMA((count,))]


def weights_steps(layer, wo_ref, s, out, own):
    x, y = ring_places()
    z = lax.axis_index("wshard")
    holder = lax.axis_index("section") == layer

    def at(d):
        return lax.rem(z + d, SIDE)

    def to(d):
        return {"wshard": at(d)}

    hops = (2, 1, 3)
    mine = pltpu.make_async_copy(s.own_w, s.wt.at[layer, z], own.at[4])
    rows = {d: out.make(("w", d), s.own_w, s.wt.at[layer, z], to(d)) for d in hops}
    role = at(SIDE - y)
    target = s.wo.at[layer]
    source = wo_ref.at[0, pl.ds(pl.multiple_of(x * HC, HC), HC)]
    mine_wo = pltpu.make_async_copy(source, target, own.at[5])
    rows_wo = {d: out.make(("wo", d), source, target, to(d)) for d in hops}
    swaps = {}
    for d in range(SIDE):
        block = s.wt.at[layer, at(SIDE - d)]
        swaps[d] = out.make(("swap", d), block, block, other_core())
    swap_wo = out.make("swap_wo", target, target, other_core())

    @pl.when(holder)
    def _():
        mine.start()
        for copy in rows.values():
            copy.start()

    @pl.when(holder & (role == 0))
    def _():
        mine_wo.start()
        for copy in rows_wo.values():
            copy.start()

    yield

    @pl.when(holder)
    def _():
        mine.wait()
        swaps[0].start()

    yield
    for d in (1, 3, 2):
        @pl.when(holder)
        def _():
            rows[d].wait_recv()
            swaps[d].start()

        yield

    @pl.when(holder & (role == 0))
    def _():
        mine_wo.wait()

    for d in hops:
        @pl.when(holder & (role == d))
        def _():
            rows_wo[d].wait_recv()

    @pl.when(holder)
    def _():
        swap_wo.start()

    yield

    @pl.when(jnp.logical_not(holder))
    def _():
        for copy in swaps.values():
            copy.wait_recv()
        swap_wo.wait_recv()

    @pl.when(holder)
    def _():
        for copy in list(rows.values()) + list(swaps.values()) + [swap_wo]:
            copy.wait_send()

    @pl.when(holder & (role == 0))
    def _():
        for copy in rows_wo.values():
            copy.wait_send()


def hand_over(layer, rows, target, copy_sem, out, name):
    part = lax.axis_index("section")
    keep = pltpu.make_async_copy(rows, target.at[part], copy_sem)
    give = out.make(name, rows, target.at[part], other_core())

    @pl.when(part == layer)
    def _():
        keep.start()

    @pl.when(part != layer)
    def _():
        give.start()

    def finish():
        @pl.when(part == layer)
        def _():
            keep.wait()
            give.wait_recv()

        @pl.when(part != layer)
        def _():
            give.wait_send()

    return finish


class Scratch:
    def __init__(self, refs):
        self.__dict__.update(refs)


def scratch_shapes(count, rows, width, heads, params, doc_shape):
    length = count * rows
    blocks = length // SPAN
    wide = width + AUX
    half_rows, quarter = rows // 2, rows // 4
    shapes = {
        "n": ((2, length, width), BF16), "c": ((2, length, wide), BF16),
        "wt": ((2, SIDE, WR, 256), BF16), "wo": ((2, HC, width), BF16),
        "cons": ((2, 8, 4 * HC), F32), "mask": ((length, HC), F32),
        "docr": ((blocks, 8, SPAN), F32),
        "vh": ((2, blocks, SPAN + 8, 3 * HC), F32), "gate": ((2, length, HC), F32),
        "dt": ((2, length, HC), F32), "mix": ((2, length, HC), BF16),
        "scan": ((2, length, HC), F32), "st": ((2, blocks, NS, HC), F32),
        "state": ((NS, HC), F32), "dz": ((SPAN + 8, 3 * HC), F32),
        "part": ((length, wide), BF16), "gin": ((WR, width), F32), "gout": ((HC, width), F32),
        "small": ((8, 4 * HC), F32),
        "u": ((rows, width), F32), "h": ((2, rows, width), F32), "branch": ((rows, width), F32),
        "r": ((rows, HC), F32), "g": ((2, rows, width), F32),
        "own_n": ((rows, width), BF16), "own_c": ((rows, wide), BF16),
        "x_in": ((rows, width), BF16), "og_in": ((rows, width), BF16),
        "doc_in": (doc_shape, jnp.int32), "own_w": ((WR, 256), BF16), "dts": ((heads, 256), BF16),
        "turning": ((HC // SIDE, width), BF16), "came": ((HC // SIDE, width), BF16),
        "block": ((END_ROWS, 256), BF16), "wide_rows": ((HC, 256), BF16),
        "gathered": ((count * END_ROWS, 256), BF16), "pieces": ((count * HC, 256), BF16),
    }
    for k, p in enumerate(params):
        shapes["param%d" % k] = (p.shape, F32)
    for l in (0, 1):
        shapes["fin%d" % l] = ((FR, 256), BF16)
        shapes["bc%d" % l] = ((16, 256), BF16)
        shapes["fout%d" % l] = ((HC // SIDE, width), BF16)
        shapes["fsmall%d" % l] = ((8, 4 * HC), F32)
    return shapes


def layers_kernel(inner, names, x_ref, og_ref, w_ref, wo_ref, doc_ref, *refs):
    params, (hid_ref, ing_ref, next_ref, pieces_ref), refs = refs[:7], refs[7:11], refs[11:]
    s = Scratch(zip(names, refs))
    refs = refs[len(names) :]
    sem_pairs, (own, fetch), buffers = refs[:14], refs[14:16], refs[16:]
    collecting, folding = buffers[:6], buffers[6:]
    sems_of = [tuple(sem_pairs[2 * k : 2 * k + 2]) for k in range(7)]
    i = pl.program_id(0)
    blocks = s.vh.shape[1]
    phase, at = i // blocks, lax.rem(i, blocks)
    part, z = lax.axis_index("section"), lax.axis_index("wshard")
    q, count = lax.axis_index(AXIS), lax.axis_size(AXIS)
    x, y = ring_places()
    width = s.u.shape[1]
    wide = s.part.shape[1]
    handing = Sender(*sems_of[5])

    @pl.when(i == 0)
    def _():
        targets = [{AXIS: lax.rem(q + d, count)} for d in range(1, count)]
        targets += [{"wshard": lax.rem(z + d, SIDE)} for d in (1, 2, 3)] + [other_core()]
        greet(targets)

        @pl.when(z != y)
        def _():
            greet([{AXIS: place_of(0, x, z), "wshard": y}])

        held = [s.__dict__["param%d" % k] for k in range(7)]
        first = (w_ref.shape[0] - 2 * NS) // 2 // HC * HC
        pieces = list(zip(params, held))
        pieces += [(x_ref.at[part, 0], s.x_in)]
        pieces += [
            (w_ref.at[pl.ds(pl.multiple_of(q * HC, HC), HC)], s.own_w.at[pl.ds(0, HC)]),
            (w_ref.at[pl.ds(pl.multiple_of(first + q * HC, HC), HC)], s.own_w.at[pl.ds(HC, HC)]),
            (w_ref.at[pl.ds(2 * first, 2 * NS)], s.own_w.at[pl.ds(2 * HC, 2 * NS)]),
            (w_ref.at[pl.ds(2 * first + 2 * NS, s.dts.shape[0])], s.dts),
            (doc_ref, s.doc_in), (og_ref.at[part, 0], s.og_in),
        ]
        copies = [
            pltpu.make_async_copy(source, target, fetch.at[k])
            for k, (source, target) in enumerate(pieces)
        ]
        for copy in copies:
            copy.start()
        for copy in copies[:7]:
            copy.wait()
        constants_into(s.cons.at[part], held)
        copies[7].wait()
        u = s.x_in[...].astype(F32)
        s.u[...] = u
        normed = norm_rows(u)
        greeted(len(targets) + (z != y).astype(jnp.int32))
        out, planes = Sender(*sems_of[0]), Sender(*sems_of[1])
        planes.go("con", s.cons.at[part], s.cons.at[part], other_core())

        def prepare():
            for copy in copies[8:12]:
                copy.wait()
            heads = s.dts.shape[0]
            pick = (iota((16, heads), 1) == 2 * q + iota((16, heads), 0)) & (
                iota((16, heads), 0) < 2
            )
            pick = pick.astype(F32).astype(BF16)
            s.own_w[4 * HC :, :] = dot_nn(pick, s.dts[...]).astype(BF16)
            weights = weights_steps(0, wo_ref, s, planes, own)
            next(weights)
            yield
            for copy in copies[12:]:
                copy.wait()
            masks = mask_steps(s.doc_in, s.mask, s.docr)
            next(masks)
            yield
            yield from masks
            yield from weights

        planes.arrived("con")
        s.own_n[...] = (normed * pre_gain_of(s.cons[0])).astype(BF16)
        run(spread_steps(s.own_n, s.n.at[0], out, own.at[0]), prepare())
        out.sent()
        planes.sent()

    @pl.when(phase < 2)
    def _():
        fwd_step(phase, at, s)

    @pl.when(phase >= 2)
    def _():
        bwd_step(3 - phase, blocks - 1 - at, s)

    def normed_sums():
        total = collecting[-1]
        square = total[:, width : width + 1] + total[:, width + 1 : width + 2]
        square = square + total[:, width + 2 : width + 3]
        r = lax.rsqrt(square / inner + EPS)
        return total[:, :width] * r, r

    @pl.when(i == blocks - 1)
    def _():
        out, more, planes = Sender(*sems_of[2]), Sender(*sems_of[0]), Sender(*sems_of[6])
        weights = weights_steps(1, wo_ref, s, planes, own)
        collect = collect_steps(s.part, collecting, out, wide)
        live = run(collect, weights, until=collect)
        branch, r = normed_sums()
        h = s.u[...] + branch
        s.own_n[...] = (norm_rows(h) * pre_gain_of(s.cons[1])).astype(BF16)
        spread = spread_steps(s.own_n, s.n.at[1], more, own.at[0])
        next(spread)
        s.h[0] = h
        s.branch[...] = branch
        s.r[...] = jnp.broadcast_to(r, s.r.shape)
        run(spread, *live)
        out.sent()
        more.sent()
        planes.sent()

    @pl.when(i == 2 * blocks - 1)
    def _():
        out, more = Sender(*sems_of[2]), Sender(*sems_of[0])
        run(collect_steps(s.part, collecting, out, wide))
        branch, r = normed_sums()
        payload_into(s.own_c, s.og_in[...].astype(F32), branch, r, inner)
        spread = spread_steps(s.own_c, s.c.at[1], more, own.at[0])
        next(spread)
        s.h[1] = s.h[0] + branch
        run(spread)
        out.sent()
        more.sent()

    def input_gradient(layer, u, cot):
        g = collecting[-1][:, :width]
        ri = lax.rsqrt(jnp.mean(u * u, axis=1, keepdims=True) + EPS)
        gg = g * pre_gain_of(s.cons[layer])
        dot = jnp.sum(gg * u, axis=1, keepdims=True) / width
        return cot + gg * ri - u * (ri * ri * ri * dot)

    def sums_of(layer):
        return [s.__dict__[name + str(layer)] for name in ("fin", "bc", "fout", "fsmall")]

    def gradients(layer, out, folds):
        fin, bc, fout, fsmall = sums_of(layer)
        gains = s.cons[layer][:, 3 * HC :]
        fold = fold_steps(layer, s.gin, s.gout, fin, fout, folding, folds)
        sums = bc_steps(s.gin, folding, out)
        small = fold_small(layer, s.small, gains, fsmall, bc, folding, folds)
        return fold, sums, small

    @pl.when(i == 3 * blocks - 1)
    def _():
        out, folds, more = Sender(*sems_of[2]), Sender(*sems_of[3]), Sender(*sems_of[0])
        collect = collect_steps(s.part, collecting, out, width)
        fold, bc, small = gradients(1, out, folds)
        live = run(collect, fold, bc, until=collect)
        live = run(*live, until=bc) + [small]
        c = input_gradient(1, s.h[0], s.og_in[...].astype(F32))
        payload_into(s.own_c, c, s.branch[...], s.r[:, 0:1], inner)
        spread = spread_steps(s.own_c, s.c.at[0], more, own.at[0])
        next(spread)
        s.g[1] = c
        run(spread, *live)
        out.sent()
        more.sent()

    @pl.when(i == 4 * blocks - 1)
    def _():
        out, folds, more = Sender(*sems_of[2]), Sender(*sems_of[3]), Sender(*sems_of[4])
        finishers = [
            hand_over(0, s.h.at[0], hid_ref, own.at[6], handing, "h0"),
            hand_over(1, s.h.at[1], hid_ref, own.at[6], handing, "h1"),
            hand_over(1, s.g.at[1], ing_ref, own.at[7], handing, "g1"),
        ]
        collect = collect_steps(s.part, collecting, out, width)
        fold, bc, small = gradients(0, out, folds)
        live = run(collect, fold, bc, until=bc) + [small]
        live = run(*live, until=small)
        live = run(*live, until=fold)
        closing = closing_steps(s, (sums_of(0), sums_of(1)), more, own)
        if collect in live:
            live = run(closing, collect, until=collect)
        else:
            live = [closing]
        s.g[0] = input_gradient(0, s.u[...], s.g[1])
        finishers.append(hand_over(0, s.g.at[0], ing_ref, own.at[7], handing, "g0"))
        run(*live)
        copies = [
            pltpu.make_async_copy(s.gathered, next_ref, own.at[0]),
            pltpu.make_async_copy(s.pieces, pieces_ref, own.at[1]),
        ]
        for copy in copies:
            copy.start()
        out.sent()
        more.sent()
        for finish in finishers:
            finish()
        for copy in copies:
            copy.wait()


def layers(block_input, out_grad, w, wo, doc_ids, *params):
    hbm = pl.BlockSpec(memory_space=pl.ANY)
    rows, width = block_input.shape[2:]
    count = lax.axis_size(AXIS)
    inner = params[-1].shape[1]
    shapes = scratch_shapes(count, rows, width, params[2].shape[1], params, doc_ids.shape)

    def shape(dims, dtype=F32):
        return jax.ShapeDtypeStruct(dims, dtype)

    return pl.pallas_call(
        lambda *refs: layers_kernel(inner, list(shapes), *refs),
        grid=(4 * count * rows // SPAN,),
        in_specs=[hbm] * 12,
        out_specs=[hbm] * 4,
        out_shape=[
            shape((2, rows, width)), shape((2, rows, width)),
            shape((count * END_ROWS, 256), BF16), shape((count * HC, 256), BF16),
        ],
        scratch_shapes=[
            *[pltpu.VMEM(dims, dtype) for dims, dtype in shapes.values()],
            *sems(40), *sems(16), *sems(56), *sems(24), *sems(82), *sems(4), *sems(16),
            pltpu.SemaphoreType.DMA((8,)), pltpu.SemaphoreType.DMA((14,)),
            *collect_scratch(rows, width + AUX), *fold_scratch(count),
        ],
        compiler_params=pltpu.CompilerParams(
            collective_id=1, has_side_effects=True, vmem_limit_bytes=VMEM_ASK
        ),
        name="layers",
    )(block_input, out_grad, w, wo, doc_ids, *params)


def assemble_kernel(
    inner, all_ref, pieces_ref, gin_ref, gout_ref, convw_ref, convb_ref, pre_ref, gain_ref, heads_ref
):
    count = all_ref.shape[0]
    lane = iota((1, HC), 1)
    bc = jnp.zeros((5, 2 * HC), F32)
    pre = jnp.zeros((8, HC), F32)
    per_head = [jnp.zeros((1, HC), F32)] * 3
    for j in range(count):
        own = slice(j * HC, (j + 1) * HC)
        gin_ref[own, :] = all_ref[j, 0:HC, :].astype(F32)
        gin_ref[inner + j * HC : inner + (j + 1) * HC, :] = all_ref[j, HC : 2 * HC, :].astype(F32)
        at = 2 * inner + j * 16
        gin_ref[at : at + 16, :] = all_ref[j, 256:272, :].astype(F32)
        at = 2 * inner + 2 * NS + 2 * j
        gin_ref[at : at + 2, :] = all_ref[j, 272:288, :].astype(F32)[0:2, :]
        big, piece = j % SIDE, j // SIDE
        at = big * HC + piece * 32
        for c in range(4):
            gout_ref[at : at + 32, c * 256 : (c + 1) * 256] = (
                pieces_ref[j, 32 * c : 32 * (c + 1), :].astype(F32)
            )
        small = all_ref[j, END_ROWS - 32 : END_ROWS - 16, :].astype(F32)
        small = small + all_ref[j, END_ROWS - 16 :, :].astype(F32)
        convw_ref[:, own] = small[0:4, :HC]
        convb_ref[:, own] = small[4:5, :HC]
        gain_ref[:, own] = small[5:6, :HC]
        bc = bc + jnp.concatenate([small[0:5, HC:], small[8:13, :HC]], axis=1)
        pre = pre + small[8:16, HC:]
        skip = small[5:6, HC:]
        for h in (0, 1):
            here = lane == 2 * j + h
            mine = (lane >= h * HEAD) & (lane < (h + 1) * HEAD)
            values = (
                small[6:7, h * HEAD : h * HEAD + 1],
                small[6:7, HC + h * HEAD : HC + h * HEAD + 1],
                jnp.sum(jnp.where(mine, skip, 0.0), axis=1, keepdims=True),
            )
            per_head = [jnp.where(here, v, p) for v, p in zip(values, per_head)]
    convw_ref[:, inner:] = bc[0:4]
    convb_ref[:, inner:] = bc[4:5]
    for k in range(8):
        pre_ref[:, k * HC : (k + 1) * HC] = pre[k : k + 1]
    heads_ref[...] = jnp.concatenate(per_head + [jnp.zeros((5, HC), F32)])


def assemble(everyone, pieces, inner, columns, width, channels):
    def shape(*dims):
        return jax.ShapeDtypeStruct(dims, F32)

    vmem = pl.BlockSpec(memory_space=pltpu.VMEM)
    return pl.pallas_call(
        lambda *refs: assemble_kernel(inner, *refs),
        in_specs=[vmem] * 2,
        out_specs=[vmem] * 7,
        out_shape=[
            shape(columns, 256), shape(512, width), shape(4, channels), shape(1, channels),
            shape(1, width), shape(1, inner), shape(8, HC),
        ],
        compiler_params=pltpu.CompilerParams(vmem_limit_bytes=VMEM_ASK),
        name="assemble",
    )(everyone, pieces)


def body(
    block_input, doc_ids, out_grad, in_proj, out_proj, conv_weight, conv_bias,
    dt_bias, a_log, skip_scale, pre_gain, norm_gain,
):
    inner = norm_gain.shape[1]
    width = block_input.shape[3]
    heads = dt_bias.shape[1]
    hidden, input_grads, everyone, pieces = layers(
        block_input, out_grad, jnp.swapaxes(in_proj[0], 0, 1), out_proj, doc_ids,
        conv_weight, conv_bias, dt_bias, a_log, skip_scale, pre_gain, norm_gain,
    )
    everyone = everyone.reshape(-1, END_ROWS, 256)
    pieces = pieces.reshape(-1, HC, 256)
    gin, gout, convw, convb, pre, gain, per_head = assemble(
        everyone, pieces, inner, in_proj.shape[2], width, conv_weight.shape[2]
    )
    return (
        hidden[None, :, None], input_grads[None, :, None],
        jnp.swapaxes(gin, 0, 1)[None], gout[None], convw[None], convb,
        per_head[0:1, :heads], per_head[1:2, :heads], per_head[2:3, :heads], pre, gain,
    )


def solution(mesh):
    specs = (
        P(None, "wshard", "seq", None),
        P(None, "wshard", None),
        P(None, "wshard", "seq", None),
        P("section", "wshard", None),
        P("section", "wshard", None),
        P("section", None, None),
        P("section", None),
        P("section", None),
        P("section", None),
        P("section", None),
        P("section", None),
        P("section", None),
    )
    outs = (
        P("section", None, "wshard", "seq", None),
        P("section", None, "wshard", "seq", None),
        P("section", "wshard", None),
        P("section", "wshard", None),
        P("section", None, None),
    ) + (P("section", None),) * 6
    return jax.shard_map(body, mesh=mesh, in_specs=specs, out_specs=outs, check_vma=False)
```

```python
import jax
import jax.numpy as jnp
from jax import lax
from jax.experimental import pallas as pl
from jax.experimental.pallas import tpu as pltpu
from jax.sharding import PartitionSpec as P

SPAN = 256
EPS = 1e-05
F32 = jnp.float32
BF16 = jnp.bfloat16
MESH = pl.DeviceIdType.MESH
VMEM_ASK = 60 * 1024 * 1024

HC = 128
NS = 128
WR = 528
FR = 272
END_ROWS = 320
AUX = 128
HEAD = 64
SIDE = 4
AXIS = "seq"


def dot_nn(a, b):
    return lax.dot_general(a, b, (((1,), (0,)), ((), ())), preferred_element_type=F32)


def dot_nt(a, b):
    return lax.dot_general(a, b, (((1,), (1,)), ((), ())), preferred_element_type=F32)


def dot_tn(a, b):
    return lax.dot_general(a, b, (((0,), (0,)), ((), ())), preferred_element_type=F32)


def three(x):
    hi = x.astype(BF16)
    rest = x - hi.astype(F32)
    mid = rest.astype(BF16)
    low = (rest - mid.astype(F32)).astype(BF16)
    return hi, mid, low


def exact_left(ones, x):
    hi, mid, low = three(x)
    return dot_nn(ones, hi) + dot_nn(ones, mid) + dot_nn(ones, low)


def exact_right(x, ones):
    hi, mid, low = three(x)
    return dot_nn(hi, ones) + dot_nn(mid, ones) + dot_nn(low, ones)


def iota(shape, dim):
    return lax.broadcasted_iota(jnp.int32, shape, dim)


def sigmoid(x):
    return 1.0 / (1.0 + jnp.exp(-x))


def softplus(x):
    return jnp.maximum(x, 0.0) + jnp.log1p(jnp.exp(-jnp.abs(x)))


def conv_rows(vbuf, con, mask):
    z = vbuf[pl.ds(8, SPAN), :] * con[3:4, :] + con[4:5, :]
    for k in (1, 2, 3):
        z = z + vbuf[pl.ds(8 - k, SPAN), :] * con[3 - k : 4 - k, :] * mask[:, k - 1 : k]
    return z


def block_terms(dt, vec, mask, docr):
    step = softplus(dt + vec[0])
    log_decay = -step * vec[1]
    rows, cols = iota((SPAN, SPAN), 0), iota((SPAN, SPAN), 1)
    lower = rows >= cols
    running = exact_left(lower.astype(F32).astype(BF16), log_decay)
    turned = running.T
    allowed = lower & (mask[:, 8:9] == docr)
    decays = []
    for h in (0, 1):
        gaps = running[:, h * HEAD : h * HEAD + 1] - turned[h * HEAD : h * HEAD + 1, :]
        decays.append(jnp.exp(jnp.where(allowed, gaps, -1e30)))
    reach = jnp.exp(running) * mask[:, 6:7]
    total = running[SPAN - 1 :, :]
    tail = jnp.exp(total - running) * mask[:, 7:8]
    carry = jnp.exp(total) * mask[SPAN - 1 :, 6:7]
    return step, running, decays, reach, tail, carry


def layer_constants(con):
    return con[5:6, :HC], con[5:6, HC : 2 * HC], con[5:6, 2 * HC : 3 * HC], con[6:7, :HC]


def pre_gain_of(con):
    return jnp.concatenate([con[k : k + 1, 3 * HC : 4 * HC] for k in range(8)], axis=1)


def head_ones():
    return (iota((16, HC), 0) == iota((16, HC), 1) // HEAD).astype(F32).astype(BF16)


def head_firsts():
    return (iota((HC, 16), 0) == iota((HC, 16), 1) * HEAD).astype(F32).astype(BF16)


def lanes_of(columns, rows):
    lane = iota((rows, AUX), 1)
    out = jnp.zeros((rows, AUX), F32)
    for k, column in enumerate(columns):
        out = jnp.where(lane == k, column.astype(F32), out)
    return out.astype(BF16)


def at_block(b):
    return pl.ds(pl.multiple_of(b * SPAN, SPAN), SPAN)


def fwd_step(layer, b, s):
    vh = s.vh.at[layer, b]
    rows = at_block(b)

    @pl.when(b == 0)
    def _():
        vh[0:8, :] = jnp.zeros((8, 3 * HC), F32)
        s.state[...] = jnp.zeros_like(s.state)

    @pl.when(b != 0)
    def _():
        vh[0:8, :] = s.vh[layer, jnp.maximum(b - 1, 0), SPAN:, :]

    width = s.wo.shape[2]
    chunk = s.wt.shape[3]
    mask = s.mask[rows, :]
    con = s.cons[layer]
    vec = layer_constants(con)
    conv = con[:, : 3 * HC]
    proj = dot_nt(s.n[layer, rows, 0:chunk], s.wt[layer, 0])
    for k in range(1, SIDE):
        proj = proj + dot_nt(s.n[layer, rows, k * chunk : (k + 1) * chunk], s.wt[layer, k])
    gate = proj[:, :HC]
    v = proj[:, HC : 4 * HC].astype(BF16).astype(F32)
    dt = dot_nn(proj[:, 4 * HC :].astype(BF16), head_ones())
    vh[8:, :] = v
    z = conv_rows(vh, conv, mask)
    sz = sigmoid(z)
    act = z * sz
    xc = act[:, :HC]
    b16 = act[:, HC : 2 * HC].astype(BF16)
    c16 = act[:, 2 * HC :].astype(BF16)
    step, running, decays, reach, tail, carry = block_terms(dt, vec, mask, s.docr[b, 0:1, :])
    s.act[layer, rows, :] = act
    s.dact[layer, rows, :] = sz * (1.0 + z * (1.0 - sz))
    s.step[layer, rows, :] = step
    s.run[layer, rows, :] = running
    for h in (0, 1):
        s.decay[layer, b, h] = decays[h]
    xs = xc * step
    xs16 = xs.astype(BF16)
    scores = dot_nt(c16, b16)
    within = [dot_nn((scores * d).astype(BF16), xs16) for d in decays]
    first = iota((SPAN, HC), 1) < HEAD
    st = s.state[...]
    s.st[layer, b] = st
    scan = jnp.where(first, within[0], within[1]) + dot_nn(c16, st.astype(BF16)) * reach
    s.state[...] = st * carry + dot_tn(b16, (xs * tail).astype(BF16))
    mixed = (scan + xc * vec[2]).astype(BF16)
    g = mixed.astype(F32) * (gate * sigmoid(gate))
    s.part[rows, :width] = dot_nn((g * vec[3]).astype(BF16), s.wo[layer]).astype(BF16)
    s.part[rows, width:] = lanes_of(three(jnp.sum(g * g, axis=1, keepdims=True)), SPAN)
    s.gate[layer, rows, :] = gate
    s.dt[layer, rows, :] = dt
    s.mix[layer, rows, :] = mixed
    s.scan[layer, rows, :] = scan


def bwd_step(layer, b, s):
    rows_b = at_block(b)
    vbuf = s.vh.at[layer, b]
    gin, gout, small, dzbuf, dstate = s.gin, s.gout, s.small, s.dz, s.state

    @pl.when(b == s.vh.shape[1] - 1)
    def _():
        dzbuf[SPAN:, :] = jnp.zeros((8, 3 * HC), F32)
        dstate[...] = jnp.zeros_like(dstate)
        gin[...] = jnp.zeros_like(gin)
        gout[...] = jnp.zeros_like(gout)
        small[...] = jnp.zeros_like(small)

    width = s.wo.shape[2]
    chunk = s.wt.shape[3]
    mask = s.mask[rows_b, :]
    con = s.cons[layer]
    vec = layer_constants(con)
    conv = con[:, : 3 * HC]
    cot = s.c[layer, rows_b, :width]
    aux = s.c[layer, rows_b, width:].astype(F32)
    r = aux[:, 0:1] + aux[:, 1:2] + aux[:, 2:3]
    pull = aux[:, 3:4] + aux[:, 4:5]
    gate = s.gate[layer, rows_b, :]
    sg = sigmoid(gate)
    silu = gate * sg
    mixed = s.mix[layer, rows_b, :].astype(F32)
    g = mixed * silu
    gain = vec[3]
    dy = dot_nt(cot, s.wo[layer])
    gr = g * r
    gout[...] += dot_tn((gr * gain).astype(BF16), cot)
    d_gain = jnp.sum(dy * gr, axis=0, keepdims=True)
    dg = dy * (r * gain) - g * pull
    dm16 = (dg * silu).astype(BF16)
    dm = dm16.astype(F32)
    dgate = dg * mixed * (sg * (1.0 + gate * (1.0 - sg)))

    act = s.act[layer, rows_b, :]
    xc = act[:, :HC]
    b16 = act[:, HC : 2 * HC].astype(BF16)
    c16 = act[:, 2 * HC :].astype(BF16)
    step, running = s.step[layer, rows_b, :], s.run[layer, rows_b, :]
    log_decay = -step * vec[1]
    decays = [s.decay[layer, b, h] for h in (0, 1)]
    total = running[SPAN - 1 :, :]
    reach = jnp.exp(running) * mask[:, 6:7]
    tail = jnp.exp(total - running) * mask[:, 7:8]
    carry = jnp.exp(total) * mask[SPAN - 1 :, 6:7]
    xs16 = (xc * step).astype(BF16)
    xs = xs16.astype(F32)
    scores = dot_nt(c16, b16)
    first = iota((SPAN, HC), 1) < HEAD
    zero16 = jnp.zeros((SPAN, HC), BF16)
    dscores = jnp.zeros((SPAN, SPAN), F32)
    dxs = []
    for h in (0, 1):
        own = jnp.where(first, dm16, zero16) if h == 0 else jnp.where(first, zero16, dm16)
        dp = dot_nt(own, xs16)
        dscores = dscores + dp * decays[h]
        dxs.append(dot_tn((scores * decays[h]).astype(BF16), dm16))
    ds16 = dscores.astype(BF16)
    st = s.st[layer, b]
    dst = dstate[...]
    dst16 = dst.astype(BF16)
    dcs16 = (dm * reach).astype(BF16)
    dc = dot_nn(ds16, b16) + dot_nt(dcs16, st.astype(BF16))
    db = dot_tn(ds16, c16) + dot_nt((xs * tail).astype(BF16), dst16)
    dxs_tail = dot_nn(b16, dst16) * tail
    dxs_all = jnp.where(first, dxs[0], dxs[1]) + dxs_tail
    dstate[...] = dst * carry + dot_tn(c16, dcs16)

    d_total = jnp.sum(xs * dxs_tail, axis=0, keepdims=True) + carry * jnp.sum(
        dst * st, axis=0, keepdims=True
    )
    flow = dm * s.scan[layer, rows_b, :] - xs * dxs_all
    rows, cols = iota((SPAN, SPAN), 0), iota((SPAN, SPAN), 1)
    upper = (cols >= rows).astype(F32).astype(BF16)
    flow = exact_left(upper, flow) + d_total
    same_head = ((iota((HC, HC), 0) < HEAD) == (iota((HC, HC), 1) < HEAD)).astype(F32).astype(BF16)
    d_log = exact_right(flow, same_head)
    d_step = exact_right(dxs_all * xc, same_head) - d_log * vec[1]
    d_alog = jnp.sum(d_log * log_decay, axis=0, keepdims=True)
    d_dt = d_step * sigmoid(s.dt[layer, rows_b, :] + vec[0])
    d_skip = jnp.sum(dm * xc, axis=0, keepdims=True)
    d_xc = dm * vec[2] + dxs_all * step

    dact = s.dact[layer, rows_b, :]
    dzbuf[:SPAN, 0:HC] = d_xc * dact[:, :HC]
    dzbuf[:SPAN, HC : 2 * HC] = db * dact[:, HC : 2 * HC]
    dzbuf[:SPAN, 2 * HC :] = dc * dact[:, 2 * HC :]
    dz = dzbuf[:SPAN, :]
    dv = dz * conv[3:4, :]
    small[3:4, : 3 * HC] += jnp.sum(dz * vbuf[pl.ds(8, SPAN), :], axis=0, keepdims=True)
    small[4:5, : 3 * HC] += jnp.sum(dz, axis=0, keepdims=True)
    for k in (1, 2, 3):
        dv = dv + dzbuf[pl.ds(k, SPAN), :] * conv[3 - k : 4 - k, :] * mask[:, 2 + k : 3 + k]
        small[3 - k : 4 - k, : 3 * HC] += jnp.sum(
            dz * vbuf[pl.ds(8 - k, SPAN), :] * mask[:, k - 1 : k], axis=0, keepdims=True
        )
    dzbuf[SPAN:, :] = dz[:8, :]
    small[5:6, 0:HC] += d_gain
    small[5:6, HC : 2 * HC] += d_skip
    small[6:7, 0:HC] += jnp.sum(d_dt, axis=0, keepdims=True)
    small[6:7, HC : 2 * HC] += d_alog

    gp = jnp.concatenate([dgate.astype(BF16), dv.astype(BF16)], axis=1)
    gdt = dot_nn(d_dt.astype(BF16), head_firsts()).astype(BF16)
    wide = 4 * HC
    n = s.n[layer, rows_b, :]
    gin[:wide] += dot_nn(gp.T, n)
    gin[wide:] += dot_tn(gdt, n)
    for k in range(SIDE):
        cols_k = slice(k * chunk, (k + 1) * chunk)
        term = dot_nn(gp, s.wt[layer, k, :wide]) + dot_nn(gdt, s.wt[layer, k, wide:])
        s.part[rows_b, cols_k] = term.astype(BF16)
        d_pre = jnp.sum(term * n[:, cols_k].astype(F32), axis=0, keepdims=True)
        small[2 * k : 2 * k + 1, 3 * HC :] += d_pre[:, :HC]
        small[2 * k + 1 : 2 * k + 2, 3 * HC :] += d_pre[:, HC:]


def place_of(half, f, s):
    f, s = lax.rem(f, SIDE), lax.rem(s, SIDE)
    return s * SIDE + f if half == 0 else f * SIDE + s


def ring_places():
    me = lax.axis_index(AXIS)
    return me % SIDE, me // SIDE


def ring_neighbours():
    x, y = ring_places()
    steps = ((1, 0), (3, 0), (0, 1), (0, 3))
    return [{AXIS: place_of(0, x + dx, y + dy)} for dx, dy in steps]


def plane_neighbours():
    z = lax.axis_index("wshard")
    return [{"wshard": lax.rem(z + 1, SIDE)}, {"wshard": lax.rem(z + 3, SIDE)}]


def plane_across():
    return {"wshard": lax.rem(lax.axis_index("wshard") + 2, SIDE)}


def other_core():
    return {"section": 1 - lax.axis_index("section")}


def greet(targets):
    barrier = pltpu.get_barrier_semaphore()
    for target in targets:
        pl.semaphore_signal(barrier, inc=1, device_id=target, device_id_type=MESH)


def greeted(count):
    pl.semaphore_wait(pltpu.get_barrier_semaphore(), count)


def run(*parts, until=None):
    live = list(parts)
    while live if until is None else until in live:
        for part in list(live):
            try:
                next(part)
            except StopIteration:
                live.remove(part)
    return live


class Sender:
    def __init__(self, send, recv):
        self.send, self.recv, self.used, self.copies, self.free = send, recv, 0, {}, set()

    def make(self, name, source, target, to):
        copy = pltpu.make_async_remote_copy(
            src_ref=source, dst_ref=target, send_sem=self.send.at[self.used],
            recv_sem=self.recv.at[self.used], device_id=to, device_id_type=MESH,
        )
        self.used += 1
        self.copies[name] = copy
        return copy

    def go(self, name, source, target, to):
        self.make(name, source, target, to).start()
        self.free.add(name)

    def arrived(self, name):
        self.copies[name].wait_recv()

    def sent(self):
        for name in self.copies:
            if name in self.free:
                self.copies[name].wait_send()


def rows_at(ref, start, size):
    return ref.at[pl.ds(pl.multiple_of(start, 16), size)]


def spread_steps(x_ref, o_ref, out, own, tag=""):
    x, y = ring_places()
    rows = x_ref.shape[0]
    half_rows, quarter = rows // 2, rows // 4
    mine = pltpu.make_async_copy(x_ref, rows_at(o_ref, place_of(0, x, y) * rows, rows), own)
    mine.start()
    firsts = ((x, y), (y, x))

    def go(name, half, block, offset, size, to, source=None):
        place = rows_at(o_ref, block * rows + half * half_rows + offset, size)
        out.go((tag, half, name), place if source is None else source, place, {AXIS: to})

    def across(half, d):
        f, s = firsts[half]
        block = place_of(half, f + d, s)
        source = x_ref.at[pl.ds(half * half_rows, half_rows)] if d == 0 else None
        go(("t1", d), half, block, 0, half_rows, place_of(half, f, s + 1), source)
        go(("t2", d), half, block, 0, half_rows, place_of(half, f, s + 3), source)

    def onward(half, d):
        f, s = firsts[half]
        out.arrived((tag, half, ("t1", d)))
        go(("u1", d), half, place_of(half, f + d, s + 3), 0, quarter, place_of(half, f, s + 1))
        out.arrived((tag, half, ("t2", d)))
        go(("u2", d), half, place_of(half, f + d, s + 1), quarter, quarter, place_of(half, f, s + 3))

    for half in (0, 1):
        f, s = firsts[half]
        source = x_ref.at[pl.ds(half * half_rows, half_rows)]
        block = place_of(half, f, s)
        go("s1", half, block, 0, half_rows, place_of(half, f + 1, s), source)
        go("s2", half, block, 0, half_rows, place_of(half, f + 3, s), source)
    for half in (0, 1):
        across(half, 0)
    yield
    for half in (0, 1):
        f, s = firsts[half]
        out.arrived((tag, half, "s1"))
        go("s3", half, place_of(half, f + 3, s), 0, quarter, place_of(half, f + 1, s))
        out.arrived((tag, half, "s2"))
        go("s4", half, place_of(half, f + 1, s), quarter, quarter, place_of(half, f + 3, s))
    for half in (0, 1):
        across(half, 3)
        across(half, 1)
    yield
    for half in (0, 1):
        onward(half, 0)
    for half in (0, 1):
        out.arrived((tag, half, "s3"))
        out.arrived((tag, half, "s4"))
        across(half, 2)
    yield
    for d in (3, 1, 2):
        for half in (0, 1):
            onward(half, d)
        yield
    for half in (0, 1):
        for d in range(SIDE):
            out.arrived((tag, half, ("u1", d)))
            out.arrived((tag, half, ("u2", d)))
    mine.wait()


def collect_scratch(rows, cols):
    half_rows, quarter = rows // 2, rows // 4
    return [
        pltpu.VMEM((2, SIDE, 2, quarter, cols), BF16),
        pltpu.VMEM((2, SIDE, 2, half_rows, cols), BF16),
        pltpu.VMEM((2, SIDE, 2, half_rows, cols), BF16),
        pltpu.VMEM((2, SIDE, half_rows, cols), BF16),
        pltpu.VMEM((2, SIDE, half_rows, cols), BF16),
        pltpu.VMEM((rows, cols), F32),
    ]


def collect_steps(x_ref, buffers, out, wide):
    cols = pl.ds(0, wide)
    far, near, stage, stage2, last = [a.at[..., cols] for a in buffers[:5]]
    x_ref, o_ref = x_ref.at[:, cols], buffers[5].at[:, cols]
    x, y = ring_places()
    rows = o_ref.shape[0]
    half_rows, quarter = rows // 2, rows // 4
    firsts = ((x, y), (y, x))
    order = (2, 1, 3, 0)

    def go(name, half, source, target, to):
        out.go((half, name), source, target, {AXIS: to})

    def start_of(half, f, s):
        return pl.multiple_of(place_of(half, f, s) * rows + half * half_rows, 16)

    for d in order:
        for half in (0, 1):
            f, s = firsts[half]
            start = start_of(half, f + d, s + 2)
            go(("a1", d), half, rows_at(x_ref, start, quarter), far.at[half, d, 0],
               place_of(half, f, s + 1))
            go(("a2", d), half, rows_at(x_ref, start + quarter, quarter), far.at[half, d, 1],
               place_of(half, f, s + 3))
    yield
    for d in order:
        for half in (0, 1):
            f, s = firsts[half]
            for side, step in enumerate((1, 3)):
                start = start_of(half, f + d, s + step)
                plain, through = quarter * (1 - side), quarter * side
                stage[half, d, side, pl.ds(plain, quarter)] = x_ref[
                    pl.ds(pl.multiple_of(start + plain, 16), quarter), :
                ]
                out.arrived((half, (("a1", "a2")[side], d)))
                stage[half, d, side, pl.ds(through, quarter)] = (
                    x_ref[pl.ds(pl.multiple_of(start + through, 16), quarter), :].astype(F32)
                    + far[half, d, side].astype(F32)
                ).astype(BF16)
                go((("b1", "b2")[side], d), half, stage.at[half, d, side], near.at[half, d, side],
                   place_of(half, f, s + step))
        if d in (1, 0):
            yield

    def summed(half, d):
        f, s = firsts[half]
        out.arrived((half, ("b1", d)))
        out.arrived((half, ("b2", d)))
        return (
            x_ref[pl.ds(start_of(half, f + d, s), half_rows), :].astype(F32)
            + near[half, d, 0].astype(F32) + near[half, d, 1].astype(F32)
        )

    for d in order[:3]:
        for half in (0, 1):
            f, s = firsts[half]
            stage2[half, d] = summed(half, d).astype(BF16)
            go(("first", d), half, stage2.at[half, d], last.at[half, d], place_of(half, f + d, s))
        yield
    for half in (0, 1):
        o_ref[pl.ds(half * half_rows, half_rows), :] = summed(half, 0)
    yield
    for half in (0, 1):
        own = pl.ds(half * half_rows, half_rows)
        total = o_ref[own, :]
        for d in (1, 3, 2):
            out.arrived((half, ("first", d)))
            total = total + last[half, d].astype(F32)
        o_ref[own, :] = total


def half_of(rows):
    return rows // 32 * 16


def fold_scratch(count):
    scratch = [pltpu.VMEM((8, 4 * HC), F32)] * 2 + [pltpu.VMEM((3, 8, 4 * HC), F32)]
    for rows, cols in ((FR, 256), (HC // SIDE, 1024)):
        scratch += [pltpu.VMEM((SIDE, rows, cols), BF16)] * 3
        scratch += [pltpu.VMEM((2, rows - half_of(rows), cols), BF16)]
        scratch += [pltpu.VMEM((2, rows, cols), BF16)]
    scratch += [pltpu.VMEM((2 * NS, 1024), BF16), pltpu.VMEM((count, 16, 1024), BF16)]
    scratch += [pltpu.VMEM((SIDE, 16, 256), BF16)] * 3 + [pltpu.VMEM((3, 16, 256), BF16)]
    return scratch


def bc_steps(gin, buffers, out):
    me, count = lax.axis_index(AXIS), lax.axis_size(AXIS)
    terms, landing, mine = buffers[13], buffers[14], buffers[15]
    terms[...] = gin[2 * HC : 4 * HC, :].astype(BF16)
    for d in range(1, count):
        to = lax.rem(me + d, count)
        out.go(("bc", d), rows_at(terms, to * 16, 16), landing.at[d], {AXIS: to})
    yield
    yield
    total = terms[pl.ds(pl.multiple_of(me * 16, 16), 16), :].astype(F32)
    for d in range(1, count):
        out.arrived(("bc", d))
        total = total + landing[d].astype(F32)
    for k in range(SIDE):
        mine[k] = total[:, k * 256 : (k + 1) * 256].astype(BF16)
    yield


def fold_steps(layer, gin, gout, fin_ref, fout_ref, buffers, out):
    z = lax.axis_index("wshard")
    up, down = plane_neighbours()
    owner = lax.axis_index("section") == layer
    ours_in, land_in, total_in, far_in, near_in = buffers[3:8]
    ours_out, land_out, total_out, far_out, near_out = buffers[8:13]
    piece = HC // SIDE
    for k in range(SIDE):
        cols = slice(k * 256, (k + 1) * 256)
        ours_in[k, : 2 * HC] = gin[: 2 * HC, cols].astype(BF16)
        ours_in[k, 2 * HC :] = gin[4 * HC :, cols].astype(BF16)
        ours_out[k] = gout[k * piece : (k + 1) * piece, :].astype(BF16)
    arrays = (
        (ours_in, land_in, total_in, far_in, near_in, fin_ref),
        (ours_out, land_out, total_out, far_out, near_out, fout_ref),
    )

    def at(d):
        return lax.rem(z + d, SIDE)

    swaps, legs = {}, {}
    parts = []
    for ours in (ours_in, ours_out):
        half = half_of(ours.shape[1])
        parts.append((pl.ds(0, half), pl.ds(half, ours.shape[1] - half)))
    for d in (2, 1, 3, 0):
        for k, (ours, land, *_) in enumerate(arrays):
            swaps[k, d] = out.make(("swap", k, d), ours.at[at(d)], land.at[at(d)], other_core())
    for k, (_, _, total, far, near, _) in enumerate(arrays):
        for side, to in enumerate((up, down)):
            some = parts[k][side]
            legs[k, "far", side] = out.make(
                ("far", k, side), total.at[at(2), some], far.at[side, pl.ds(0, some.size)], to
            )
        legs[k, "near", 0] = out.make(("near", k, 0), total.at[at(1)], near.at[0], up)
        legs[k, "near", 1] = out.make(("near", k, 1), total.at[at(3)], near.at[1], down)

    @pl.when(jnp.logical_not(owner))
    def _():
        for copy in swaps.values():
            copy.start()

    yield

    def add_cores(d):
        for k, (ours, land, total, *_) in enumerate(arrays):
            swaps[k, d].wait_recv()
            total[at(d)] = (ours[at(d)].astype(F32) + land[at(d)].astype(F32)).astype(BF16)

    @pl.when(owner)
    def _():
        add_cores(2)
        for k in (0, 1):
            legs[k, "far", 0].start()
            legs[k, "far", 1].start()

    yield
    for side, d in ((0, 1), (1, 3)):
        @pl.when(owner)
        def _():
            add_cores(d)
            for k, (_, _, total, far, _, _) in enumerate(arrays):
                legs[k, "far", side].wait_recv()
                some = parts[k][side]
                total[at(d), some] = (
                    total[at(d), some].astype(F32) + far[side, pl.ds(0, some.size)].astype(F32)
                ).astype(BF16)
                legs[k, "near", side].start()

        yield

    @pl.when(owner)
    def _():
        add_cores(0)
        for k, (_, _, total, _, near, done) in enumerate(arrays):
            legs[k, "near", 0].wait_recv()
            legs[k, "near", 1].wait_recv()
            done[...] = (
                total[at(0)].astype(F32) + near[0].astype(F32) + near[1].astype(F32)
            ).astype(BF16)
        for leg in legs.values():
            leg.wait_send()

    @pl.when(jnp.logical_not(owner))
    def _():
        for copy in swaps.values():
            copy.wait_send()


def fold_small(layer, small, gains, done_ref, bc_ref, buffers, out):
    small[:, 3 * HC :] = small[:, 3 * HC :] / gains
    owner = lax.axis_index("section") == layer
    z = lax.axis_index("wshard")
    land, total, planes = buffers[:3]
    mine, land_bc, total_bc, planes_bc = buffers[15:19]
    up, down = plane_neighbours()
    swaps = [
        out.make("small", small, land, other_core()), out.make("bc", mine, land_bc, other_core()),
    ]
    legs = []
    for k, (d, to) in enumerate(((1, up), (3, down), (2, plane_across()))):
        legs.append(out.make(("small", k), total, planes.at[k], to))
        legs.append(out.make(
            ("bc", k), total_bc.at[lax.rem(z + d, SIDE)], planes_bc.at[k], to))

    @pl.when(jnp.logical_not(owner))
    def _():
        for swap in swaps:
            swap.start()

    @pl.when(owner)
    def _():
        for swap in swaps:
            swap.wait_recv()
        total[...] = small[...] + land[...]
        total_bc[...] = (mine[...].astype(F32) + land_bc[...].astype(F32)).astype(BF16)
        for leg in legs:
            leg.start()

    yield

    @pl.when(owner)
    def _():
        for leg in legs:
            leg.wait_recv()
        done_ref[...] = total[...] + planes[0] + planes[1] + planes[2]
        sum_bc = total_bc[z].astype(F32)
        for k in range(3):
            sum_bc = sum_bc + planes_bc[k].astype(F32)
        bc_ref[...] = sum_bc.astype(BF16)
        for leg in legs:
            leg.wait_send()

    @pl.when(jnp.logical_not(owner))
    def _():
        for swap in swaps:
            swap.wait_send()


def closing_steps(s, layer_sums, out, own):
    x, y = ring_places()
    z = lax.axis_index("wshard")
    first = lax.axis_index("section") == 0
    fin, bc, fout, small = [
        jnp.where(first, a[...], b[...]) for a, b in zip(layer_sums[0], layer_sums[1])
    ]
    s.turning[...] = fout
    turned = {AXIS: place_of(0, x, z), "wshard": y}
    turn = out.make("turn", s.turning, s.came, turned)

    @pl.when(z != y)
    def _():
        turn.start()

    s.block[0 : 2 * HC, :] = fin[: 2 * HC]
    s.block[2 * HC : 2 * HC + 16, :] = bc
    s.block[2 * HC + 16 : 2 * HC + 32, :] = fin[2 * HC :]
    hi, mid, _ = three(jnp.concatenate([small[:, :256], small[:, 256:]]))
    s.block[END_ROWS - 32 : END_ROWS - 16, :] = hi
    s.block[END_ROWS - 16 :, :] = mid
    main = spread_steps(s.block, s.gathered, out, own.at[2], "in")
    next(main)
    yield
    next(main)

    @pl.when(z != y)
    def _():
        turn.wait_recv()

    @pl.when(z == y)
    def _():
        s.came[...] = s.turning[...]

    for c in range(4):
        s.wide_rows[32 * c : 32 * (c + 1), :] = s.came[:, c * 256 : (c + 1) * 256]
    side = spread_steps(s.wide_rows, s.pieces, out, own.at[3], "out")
    live = [main, side]
    while live:
        for part in list(live):
            try:
                next(part)
            except StopIteration:
                live.remove(part)
        yield

    @pl.when(z != y)
    def _():
        turn.wait_send()


def norm_rows(u):
    return u * lax.rsqrt(jnp.mean(u * u, axis=1, keepdims=True) + EPS)


def payload_into(ref, c, branch, r, inner):
    width = c.shape[1]
    low = c.astype(BF16)
    pull = r * r * jnp.sum(low.astype(F32) * branch, axis=1, keepdims=True) / inner
    ref[:, :width] = low
    ref[:, width:] = lanes_of(list(three(r)) + list(three(pull))[:2], c.shape[0])


def constants_into(con, params):
    cw_ref, cb_ref, dtb_ref, alog_ref, skip_ref, pre_ref, gain_ref = params
    q = lax.axis_index(AXIS)
    inner = gain_ref.shape[1]
    own = pl.ds(pl.multiple_of(q * HC, HC), HC)
    con[...] = jnp.zeros_like(con)
    con[0:4, :HC] = cw_ref[0, :, own]
    con[0:4, HC : 3 * HC] = cw_ref[0, :, inner:]
    con[4:5, :HC] = cb_ref[:, own]
    con[4:5, HC : 3 * HC] = cb_ref[:, inner:]

    def lanes(ref):
        value = ref[...]
        lane = iota(value.shape, 1)
        two = [
            jnp.sum(jnp.where(lane == 2 * q + h, value, 0.0), axis=1, keepdims=True) for h in (0, 1)
        ]
        return jnp.where(iota((1, HC), 1) < HEAD, two[0], two[1])

    con[5:6, :HC] = lanes(dtb_ref)
    con[5:6, HC : 2 * HC] = jnp.exp(lanes(alog_ref))
    con[5:6, 2 * HC : 3 * HC] = lanes(skip_ref)
    con[6:7, :HC] = gain_ref[:, own]
    for k in range(8):
        con[k : k + 1, 3 * HC :] = pre_ref[:, k * HC : (k + 1) * HC]


def mask_steps(doc_ref, mask_ref, docr_ref):
    yield
    doc = doc_ref[lax.axis_index("section")].astype(F32)
    length = doc.shape[1]
    doc8 = jnp.broadcast_to(doc, (8, length))
    for b in range(length // SPAN):
        docr_ref[b] = doc8[:, b * SPAN : (b + 1) * SPAN]
    at = iota((8, length), 1)
    rows = []
    for k in (1, 2, 3):
        rows.append((pltpu.roll(doc8, k, 1) == doc8) & (at >= k))
    for k in (1, 2, 3):
        rows.append((pltpu.roll(doc8, length - k, 1) == doc8) & (at < length - k))
    before, final = doc8, doc8
    for b in range(length // SPAN):
        inside = (at >= b * SPAN) & (at < (b + 1) * SPAN)
        start = max(b * SPAN - 1, 0)
        end = (b + 1) * SPAN - 1
        before = jnp.where(inside, doc[:, start : start + 1], before)
        final = jnp.where(inside, doc[:, end : end + 1], final)
    rows += [before == doc8, final == doc8]
    sub = iota((8, length), 0)
    first = jnp.zeros((8, length), F32)
    for k, row in enumerate(rows):
        first = jnp.where((sub == k) & row, 1.0, first)
    both = jnp.concatenate([first, doc8, jnp.zeros((HC - 16, length), F32)])
    mask_ref[...] = both.T


def sems(count):
    return [pltpu.SemaphoreType.DMA((count,)), pltpu.SemaphoreType.DMA((count,))]


def weights_steps(layer, wo_ref, s, out, own):
    x, y = ring_places()
    z = lax.axis_index("wshard")
    holder = lax.axis_index("section") == layer

    def at(d):
        return lax.rem(z + d, SIDE)

    def to(d):
        return {"wshard": at(d)}

    hops = (2, 1, 3)
    mine = pltpu.make_async_copy(s.own_w, s.wt.at[layer, z], own.at[4])
    rows = {d: out.make(("w", d), s.own_w, s.wt.at[layer, z], to(d)) for d in hops}
    role = at(SIDE - y)
    target = s.wo.at[layer]
    source = wo_ref.at[0, pl.ds(pl.multiple_of(x * HC, HC), HC)]
    mine_wo = pltpu.make_async_copy(source, target, own.at[5])
    rows_wo = {d: out.make(("wo", d), source, target, to(d)) for d in hops}
    swaps = {}
    for d in range(SIDE):
        block = s.wt.at[layer, at(SIDE - d)]
        swaps[d] = out.make(("swap", d), block, block, other_core())
    swap_wo = out.make("swap_wo", target, target, other_core())

    @pl.when(holder)
    def _():
        mine.start()
        for copy in rows.values():
            copy.start()

    @pl.when(holder & (role == 0))
    def _():
        mine_wo.start()
        for copy in rows_wo.values():
            copy.start()

    yield

    @pl.when(holder)
    def _():
        mine.wait()
        swaps[0].start()

    yield
    for d in (1, 3, 2):
        @pl.when(holder)
        def _():
            rows[d].wait_recv()
            swaps[d].start()

        yield

    @pl.when(holder & (role == 0))
    def _():
        mine_wo.wait()

    for d in hops:
        @pl.when(holder & (role == d))
        def _():
            rows_wo[d].wait_recv()

    @pl.when(holder)
    def _():
        swap_wo.start()

    yield

    @pl.when(jnp.logical_not(holder))
    def _():
        for copy in swaps.values():
            copy.wait_recv()
        swap_wo.wait_recv()

    @pl.when(holder)
    def _():
        for copy in list(rows.values()) + list(swaps.values()) + [swap_wo]:
            copy.wait_send()

    @pl.when(holder & (role == 0))
    def _():
        for copy in rows_wo.values():
            copy.wait_send()


def hand_over(layer, rows, target, copy_sem, out, name):
    part = lax.axis_index("section")
    keep = pltpu.make_async_copy(rows, target.at[part], copy_sem)
    give = out.make(name, rows, target.at[part], other_core())

    @pl.when(part == layer)
    def _():
        keep.start()

    @pl.when(part != layer)
    def _():
        give.start()

    def finish():
        @pl.when(part == layer)
        def _():
            keep.wait()
            give.wait_recv()

        @pl.when(part != layer)
        def _():
            give.wait_send()

    return finish


class Scratch:
    def __init__(self, refs):
        self.__dict__.update(refs)


def scratch_shapes(count, rows, width, heads, params, doc_shape):
    length = count * rows
    blocks = length // SPAN
    wide = width + AUX
    half_rows, quarter = rows // 2, rows // 4
    shapes = {
        "n": ((2, length, width), BF16), "c": ((2, length, wide), BF16),
        "wt": ((2, SIDE, WR, 256), BF16), "wo": ((2, HC, width), BF16),
        "cons": ((2, 8, 4 * HC), F32), "mask": ((length, HC), F32),
        "docr": ((blocks, 8, SPAN), F32),
        "vh": ((2, blocks, SPAN + 8, 3 * HC), F32), "gate": ((2, length, HC), F32),
        "dt": ((2, length, HC), F32), "mix": ((2, length, HC), BF16),
        "scan": ((2, length, HC), F32), "st": ((2, blocks, NS, HC), F32),
        "state": ((NS, HC), F32), "dz": ((SPAN + 8, 3 * HC), F32),
        "part": ((length, wide), BF16),
        "act": ((2, length, 3 * HC), F32), "dact": ((2, length, 3 * HC), F32),
        "step": ((2, length, HC), F32), "run": ((2, length, HC), F32),
        "decay": ((2, blocks, 2, SPAN, SPAN), F32),
        "gin": ((WR, width), F32), "gout": ((HC, width), F32),
        "small": ((8, 4 * HC), F32),
        "u": ((rows, width), F32), "h": ((2, rows, width), F32), "branch": ((rows, width), F32),
        "r": ((rows, HC), F32), "g": ((2, rows, width), F32),
        "own_n": ((rows, width), BF16), "own_c": ((rows, wide), BF16),
        "x_in": ((rows, width), BF16), "og_in": ((rows, width), BF16),
        "doc_in": (doc_shape, jnp.int32), "own_w": ((WR, 256), BF16), "dts": ((heads, 256), BF16),
        "turning": ((HC // SIDE, width), BF16), "came": ((HC // SIDE, width), BF16),
        "block": ((END_ROWS, 256), BF16), "wide_rows": ((HC, 256), BF16),
        "gathered": ((count * END_ROWS, 256), BF16), "pieces": ((count * HC, 256), BF16),
    }
    for k, p in enumerate(params):
        shapes["param%d" % k] = (p.shape, F32)
    for l in (0, 1):
        shapes["fin%d" % l] = ((FR, 256), BF16)
        shapes["bc%d" % l] = ((16, 256), BF16)
        shapes["fout%d" % l] = ((HC // SIDE, width), BF16)
        shapes["fsmall%d" % l] = ((8, 4 * HC), F32)
    return shapes


def layers_kernel(inner, names, x_ref, og_ref, w_ref, wo_ref, doc_ref, *refs):
    params, (hid_ref, ing_ref, next_ref, pieces_ref), refs = refs[:7], refs[7:11], refs[11:]
    s = Scratch(zip(names, refs))
    refs = refs[len(names) :]
    sem_pairs, (own, fetch), buffers = refs[:14], refs[14:16], refs[16:]
    collecting, folding = buffers[:6], buffers[6:]
    sems_of = [tuple(sem_pairs[2 * k : 2 * k + 2]) for k in range(7)]
    i = pl.program_id(0)
    blocks = s.vh.shape[1]
    phase, at = i // blocks, lax.rem(i, blocks)
    part, z = lax.axis_index("section"), lax.axis_index("wshard")
    q, count = lax.axis_index(AXIS), lax.axis_size(AXIS)
    x, y = ring_places()
    width = s.u.shape[1]
    wide = s.part.shape[1]
    handing = Sender(*sems_of[5])

    @pl.when(i == 0)
    def _():
        targets = [{AXIS: lax.rem(q + d, count)} for d in range(1, count)]
        targets += [{"wshard": lax.rem(z + d, SIDE)} for d in (1, 2, 3)] + [other_core()]
        greet(targets)

        @pl.when(z != y)
        def _():
            greet([{AXIS: place_of(0, x, z), "wshard": y}])

        held = [s.__dict__["param%d" % k] for k in range(7)]
        first = (w_ref.shape[0] - 2 * NS) // 2 // HC * HC
        pieces = list(zip(params, held))
        pieces += [(x_ref.at[part, 0], s.x_in)]
        pieces += [
            (w_ref.at[pl.ds(pl.multiple_of(q * HC, HC), HC)], s.own_w.at[pl.ds(0, HC)]),
            (w_ref.at[pl.ds(pl.multiple_of(first + q * HC, HC), HC)], s.own_w.at[pl.ds(HC, HC)]),
            (w_ref.at[pl.ds(2 * first, 2 * NS)], s.own_w.at[pl.ds(2 * HC, 2 * NS)]),
            (w_ref.at[pl.ds(2 * first + 2 * NS, s.dts.shape[0])], s.dts),
            (doc_ref, s.doc_in), (og_ref.at[part, 0], s.og_in),
        ]
        copies = [
            pltpu.make_async_copy(source, target, fetch.at[k])
            for k, (source, target) in enumerate(pieces)
        ]
        for copy in copies:
            copy.start()
        for copy in copies[:7]:
            copy.wait()
        constants_into(s.cons.at[part], held)
        copies[7].wait()
        u = s.x_in[...].astype(F32)
        s.u[...] = u
        normed = norm_rows(u)
        greeted(len(targets) + (z != y).astype(jnp.int32))
        out, planes = Sender(*sems_of[0]), Sender(*sems_of[1])
        planes.go("con", s.cons.at[part], s.cons.at[part], other_core())

        def prepare():
            for copy in copies[8:12]:
                copy.wait()
            heads = s.dts.shape[0]
            pick = (iota((16, heads), 1) == 2 * q + iota((16, heads), 0)) & (
                iota((16, heads), 0) < 2
            )
            pick = pick.astype(F32).astype(BF16)
            s.own_w[4 * HC :, :] = dot_nn(pick, s.dts[...]).astype(BF16)
            weights = weights_steps(0, wo_ref, s, planes, own)
            next(weights)
            yield
            for copy in copies[12:]:
                copy.wait()
            masks = mask_steps(s.doc_in, s.mask, s.docr)
            next(masks)
            yield
            yield from masks
            yield from weights

        planes.arrived("con")
        s.own_n[...] = (normed * pre_gain_of(s.cons[0])).astype(BF16)
        run(spread_steps(s.own_n, s.n.at[0], out, own.at[0]), prepare())
        out.sent()
        planes.sent()

    @pl.when(phase < 2)
    def _():
        fwd_step(phase, at, s)

    @pl.when(phase >= 2)
    def _():
        bwd_step(3 - phase, blocks - 1 - at, s)

    def normed_sums():
        total = collecting[-1]
        square = total[:, width : width + 1] + total[:, width + 1 : width + 2]
        square = square + total[:, width + 2 : width + 3]
        r = lax.rsqrt(square / inner + EPS)
        return total[:, :width] * r, r

    @pl.when(i == blocks - 1)
    def _():
        out, more, planes = Sender(*sems_of[2]), Sender(*sems_of[0]), Sender(*sems_of[6])
        weights = weights_steps(1, wo_ref, s, planes, own)
        collect = collect_steps(s.part, collecting, out, wide)
        live = run(collect, weights, until=collect)
        branch, r = normed_sums()
        h = s.u[...] + branch
        s.own_n[...] = (norm_rows(h) * pre_gain_of(s.cons[1])).astype(BF16)
        spread = spread_steps(s.own_n, s.n.at[1], more, own.at[0])
        next(spread)
        s.h[0] = h
        s.branch[...] = branch
        s.r[...] = jnp.broadcast_to(r, s.r.shape)
        run(spread, *live)
        out.sent()
        more.sent()
        planes.sent()

    @pl.when(i == 2 * blocks - 1)
    def _():
        out, more = Sender(*sems_of[2]), Sender(*sems_of[0])
        run(collect_steps(s.part, collecting, out, wide))
        branch, r = normed_sums()
        payload_into(s.own_c, s.og_in[...].astype(F32), branch, r, inner)
        spread = spread_steps(s.own_c, s.c.at[1], more, own.at[0])
        next(spread)
        s.h[1] = s.h[0] + branch
        run(spread)
        out.sent()
        more.sent()

    def input_gradient(layer, u, cot):
        g = collecting[-1][:, :width]
        ri = lax.rsqrt(jnp.mean(u * u, axis=1, keepdims=True) + EPS)
        gg = g * pre_gain_of(s.cons[layer])
        dot = jnp.sum(gg * u, axis=1, keepdims=True) / width
        return cot + gg * ri - u * (ri * ri * ri * dot)

    def sums_of(layer):
        return [s.__dict__[name + str(layer)] for name in ("fin", "bc", "fout", "fsmall")]

    def gradients(layer, out, folds):
        fin, bc, fout, fsmall = sums_of(layer)
        gains = s.cons[layer][:, 3 * HC :]
        fold = fold_steps(layer, s.gin, s.gout, fin, fout, folding, folds)
        sums = bc_steps(s.gin, folding, out)
        small = fold_small(layer, s.small, gains, fsmall, bc, folding, folds)
        return fold, sums, small

    @pl.when(i == 3 * blocks - 1)
    def _():
        out, folds, more = Sender(*sems_of[2]), Sender(*sems_of[3]), Sender(*sems_of[0])
        collect = collect_steps(s.part, collecting, out, width)
        fold, bc, small = gradients(1, out, folds)
        live = run(collect, fold, bc, until=collect)
        live = run(*live, until=bc) + [small]
        c = input_gradient(1, s.h[0], s.og_in[...].astype(F32))
        payload_into(s.own_c, c, s.branch[...], s.r[:, 0:1], inner)
        spread = spread_steps(s.own_c, s.c.at[0], more, own.at[0])
        next(spread)
        s.g[1] = c
        run(spread, *live)
        out.sent()
        more.sent()

    @pl.when(i == 4 * blocks - 1)
    def _():
        out, folds, more = Sender(*sems_of[2]), Sender(*sems_of[3]), Sender(*sems_of[4])
        finishers = [
            hand_over(0, s.h.at[0], hid_ref, own.at[6], handing, "h0"),
            hand_over(1, s.h.at[1], hid_ref, own.at[6], handing, "h1"),
            hand_over(1, s.g.at[1], ing_ref, own.at[7], handing, "g1"),
        ]
        collect = collect_steps(s.part, collecting, out, width)
        fold, bc, small = gradients(0, out, folds)
        live = run(collect, fold, bc, until=bc) + [small]
        live = run(*live, until=small)
        live = run(*live, until=fold)
        closing = closing_steps(s, (sums_of(0), sums_of(1)), more, own)
        if collect in live:
            live = run(closing, collect, until=collect)
        else:
            live = [closing]
        s.g[0] = input_gradient(0, s.u[...], s.g[1])
        finishers.append(hand_over(0, s.g.at[0], ing_ref, own.at[7], handing, "g0"))
        run(*live)
        copies = [
            pltpu.make_async_copy(s.gathered, next_ref, own.at[0]),
            pltpu.make_async_copy(s.pieces, pieces_ref, own.at[1]),
        ]
        for copy in copies:
            copy.start()
        out.sent()
        more.sent()
        for finish in finishers:
            finish()
        for copy in copies:
            copy.wait()


def layers(block_input, out_grad, w, wo, doc_ids, *params):
    hbm = pl.BlockSpec(memory_space=pl.ANY)
    rows, width = block_input.shape[2:]
    count = lax.axis_size(AXIS)
    inner = params[-1].shape[1]
    shapes = scratch_shapes(count, rows, width, params[2].shape[1], params, doc_ids.shape)

    def shape(dims, dtype=F32):
        return jax.ShapeDtypeStruct(dims, dtype)

    return pl.pallas_call(
        lambda *refs: layers_kernel(inner, list(shapes), *refs),
        grid=(4 * count * rows // SPAN,),
        in_specs=[hbm] * 12,
        out_specs=[hbm] * 4,
        out_shape=[
            shape((2, rows, width)), shape((2, rows, width)),
            shape((count * END_ROWS, 256), BF16), shape((count * HC, 256), BF16),
        ],
        scratch_shapes=[
            *[pltpu.VMEM(dims, dtype) for dims, dtype in shapes.values()],
            *sems(40), *sems(16), *sems(56), *sems(24), *sems(82), *sems(4), *sems(16),
            pltpu.SemaphoreType.DMA((8,)), pltpu.SemaphoreType.DMA((14,)),
            *collect_scratch(rows, width + AUX), *fold_scratch(count),
        ],
        compiler_params=pltpu.CompilerParams(
            collective_id=1, has_side_effects=True, vmem_limit_bytes=VMEM_ASK
        ),
        name="layers",
    )(block_input, out_grad, w, wo, doc_ids, *params)


def assemble_kernel(
    inner, all_ref, pieces_ref, gin_ref, gout_ref, convw_ref, convb_ref, pre_ref, gain_ref,
    step_ref, alog_ref, skip_ref,
):
    count = all_ref.shape[0]
    lane = iota((1, HC), 1)
    bc = jnp.zeros((5, 2 * HC), F32)
    pre = jnp.zeros((8, HC), F32)
    per_head = [jnp.zeros((1, HC), F32)] * 3
    for j in range(count):
        own = slice(j * HC, (j + 1) * HC)
        gin_ref[own, :] = all_ref[j, 0:HC, :].astype(F32)
        gin_ref[inner + j * HC : inner + (j + 1) * HC, :] = all_ref[j, HC : 2 * HC, :].astype(F32)
        at = 2 * inner + j * 16
        gin_ref[at : at + 16, :] = all_ref[j, 256:272, :].astype(F32)
        at = 2 * inner + 2 * NS + 2 * j
        gin_ref[at : at + 2, :] = all_ref[j, 272:288, :].astype(F32)[0:2, :]
        big, piece = j % SIDE, j // SIDE
        at = big * HC + piece * 32
        for c in range(4):
            gout_ref[at : at + 32, c * 256 : (c + 1) * 256] = (
                pieces_ref[j, 32 * c : 32 * (c + 1), :].astype(F32)
            )
        small = all_ref[j, END_ROWS - 32 : END_ROWS - 16, :].astype(F32)
        small = small + all_ref[j, END_ROWS - 16 :, :].astype(F32)
        convw_ref[:, own] = small[0:4, :HC]
        convb_ref[:, own] = small[4:5, :HC]
        gain_ref[:, own] = small[5:6, :HC]
        bc = bc + jnp.concatenate([small[0:5, HC:], small[8:13, :HC]], axis=1)
        pre = pre + small[8:16, HC:]
        skip = small[5:6, HC:]
        for h in (0, 1):
            here = lane == 2 * j + h
            mine = (lane >= h * HEAD) & (lane < (h + 1) * HEAD)
            values = (
                small[6:7, h * HEAD : h * HEAD + 1],
                small[6:7, HC + h * HEAD : HC + h * HEAD + 1],
                jnp.sum(jnp.where(mine, skip, 0.0), axis=1, keepdims=True),
            )
            per_head = [jnp.where(here, v, p) for v, p in zip(values, per_head)]
    convw_ref[:, inner:] = bc[0:4]
    convb_ref[:, inner:] = bc[4:5]
    for k in range(8):
        pre_ref[:, k * HC : (k + 1) * HC] = pre[k : k + 1]
    for ref, value in zip((step_ref, alog_ref, skip_ref), per_head):
        ref[...] = value[:, : ref.shape[1]]


def assemble(everyone, pieces, inner, columns, width, channels, heads):
    def shape(*dims):
        return jax.ShapeDtypeStruct(dims, F32)

    vmem = pl.BlockSpec(memory_space=pltpu.VMEM)
    return pl.pallas_call(
        lambda *refs: assemble_kernel(inner, *refs),
        in_specs=[vmem] * 2,
        out_specs=[vmem] * 9,
        out_shape=[
            shape(columns, 256), shape(512, width), shape(4, channels), shape(1, channels),
            shape(1, width), shape(1, inner), *[shape(1, heads)] * 3,
        ],
        compiler_params=pltpu.CompilerParams(vmem_limit_bytes=VMEM_ASK),
        name="assemble",
    )(everyone, pieces)


def body(
    block_input, doc_ids, out_grad, in_proj, out_proj, conv_weight, conv_bias,
    dt_bias, a_log, skip_scale, pre_gain, norm_gain,
):
    inner = norm_gain.shape[1]
    width = block_input.shape[3]
    heads = dt_bias.shape[1]
    hidden, input_grads, everyone, pieces = layers(
        block_input, out_grad, jnp.swapaxes(in_proj[0], 0, 1), out_proj, doc_ids,
        conv_weight, conv_bias, dt_bias, a_log, skip_scale, pre_gain, norm_gain,
    )
    everyone = everyone.reshape(-1, END_ROWS, 256)
    pieces = pieces.reshape(-1, HC, 256)
    gin, gout, convw, convb, pre, gain, step, alog, skip = assemble(
        everyone, pieces, inner, in_proj.shape[2], width, conv_weight.shape[2], heads
    )
    return (
        hidden[None, :, None], input_grads[None, :, None],
        jnp.swapaxes(gin, 0, 1)[None], gout[None], convw[None], convb,
        step, alog, skip, pre, gain,
    )


def solution(mesh):
    specs = (
        P(None, "wshard", "seq", None),
        P(None, "wshard", None),
        P(None, "wshard", "seq", None),
        P("section", "wshard", None),
        P("section", "wshard", None),
        P("section", None, None),
        P("section", None),
        P("section", None),
        P("section", None),
        P("section", None),
        P("section", None),
        P("section", None),
    )
    outs = (
        P("section", None, "wshard", "seq", None),
        P("section", None, "wshard", "seq", None),
        P("section", "wshard", None),
        P("section", "wshard", None),
        P("section", None, None),
    ) + (P("section", None),) * 6
    return jax.shard_map(body, mesh=mesh, in_specs=specs, out_specs=outs, check_vma=False)
```

```python
import jax
import jax.numpy as jnp
from jax import lax
from jax.experimental import pallas as pl
from jax.experimental.pallas import tpu as pltpu
from jax.sharding import PartitionSpec as P

SPAN = 256
EPS = 1e-05
F32 = jnp.float32
BF16 = jnp.bfloat16
MESH = pl.DeviceIdType.MESH
VMEM_ASK = 60 * 1024 * 1024

HC = 128
NS = 128
WR = 528
FR = 272
END_ROWS = 320
AUX = 128
HEAD = 64
SIDE = 4
AXIS = "seq"


def dot_nn(a, b):
    return lax.dot_general(a, b, (((1,), (0,)), ((), ())), preferred_element_type=F32)


def dot_nt(a, b):
    return lax.dot_general(a, b, (((1,), (1,)), ((), ())), preferred_element_type=F32)


def dot_tn(a, b):
    return lax.dot_general(a, b, (((0,), (0,)), ((), ())), preferred_element_type=F32)


def three(x):
    hi = x.astype(BF16)
    rest = x - hi.astype(F32)
    mid = rest.astype(BF16)
    low = (rest - mid.astype(F32)).astype(BF16)
    return hi, mid, low


def exact_left(ones, x):
    hi, mid, low = three(x)
    return dot_nn(ones, hi) + dot_nn(ones, mid) + dot_nn(ones, low)


def exact_right(x, ones):
    hi, mid, low = three(x)
    return dot_nn(hi, ones) + dot_nn(mid, ones) + dot_nn(low, ones)


def iota(shape, dim):
    return lax.broadcasted_iota(jnp.int32, shape, dim)


def sigmoid(x):
    return 1.0 / (1.0 + jnp.exp(-x))


def softplus(x):
    return jnp.maximum(x, 0.0) + jnp.log1p(jnp.exp(-jnp.abs(x)))


def conv_rows(vbuf, con, mask):
    z = vbuf[pl.ds(8, SPAN), :] * con[3:4, :] + con[4:5, :]
    for k in (1, 2, 3):
        z = z + vbuf[pl.ds(8 - k, SPAN), :] * con[3 - k : 4 - k, :] * mask[:, k - 1 : k]
    return z


def block_terms(dt, vec, mask, docr):
    step = softplus(dt + vec[0])
    log_decay = -step * vec[1]
    rows, cols = iota((SPAN, SPAN), 0), iota((SPAN, SPAN), 1)
    lower = rows >= cols
    running = exact_left(lower.astype(F32).astype(BF16), log_decay)
    turned = running.T
    allowed = lower & (mask[:, 8:9] == docr)
    decays = []
    for h in (0, 1):
        gaps = running[:, h * HEAD : h * HEAD + 1] - turned[h * HEAD : h * HEAD + 1, :]
        decays.append(jnp.exp(jnp.where(allowed, gaps, -1e30)))
    reach = jnp.exp(running) * mask[:, 6:7]
    total = running[SPAN - 1 :, :]
    tail = jnp.exp(total - running) * mask[:, 7:8]
    carry = jnp.exp(total) * mask[SPAN - 1 :, 6:7]
    return step, running, decays, reach, tail, carry


def layer_constants(con):
    return con[5:6, :HC], con[5:6, HC : 2 * HC], con[5:6, 2 * HC : 3 * HC], con[6:7, :HC]


def pre_gain_of(con):
    return jnp.concatenate([con[k : k + 1, 3 * HC : 4 * HC] for k in range(8)], axis=1)


def head_ones():
    return (iota((16, HC), 0) == iota((16, HC), 1) // HEAD).astype(F32).astype(BF16)


def head_firsts():
    return (iota((HC, 16), 0) == iota((HC, 16), 1) * HEAD).astype(F32).astype(BF16)


def lanes_of(columns, rows):
    lane = iota((rows, AUX), 1)
    out = jnp.zeros((rows, AUX), F32)
    for k, column in enumerate(columns):
        out = jnp.where(lane == k, column.astype(F32), out)
    return out.astype(BF16)


def at_block(b):
    return pl.ds(pl.multiple_of(b * SPAN, SPAN), SPAN)


def fwd_step(layer, b, s):
    vh = s.vh.at[layer, b]
    rows = at_block(b)

    @pl.when(b == 0)
    def _():
        vh[0:8, :] = jnp.zeros((8, 3 * HC), F32)
        s.state[...] = jnp.zeros_like(s.state)

    @pl.when(b != 0)
    def _():
        vh[0:8, :] = s.vh[layer, jnp.maximum(b - 1, 0), SPAN:, :]

    width = s.wo.shape[2]
    chunk = s.wt.shape[3]
    mask = s.mask[rows, :]
    con = s.cons[layer]
    vec = layer_constants(con)
    conv = con[:, : 3 * HC]
    proj = dot_nt(s.n[layer, rows, 0:chunk], s.wt[layer, 0])
    for k in range(1, SIDE):
        proj = proj + dot_nt(s.n[layer, rows, k * chunk : (k + 1) * chunk], s.wt[layer, k])
    gate = proj[:, :HC]
    v = proj[:, HC : 4 * HC].astype(BF16).astype(F32)
    dt = dot_nn(proj[:, 4 * HC :].astype(BF16), head_ones())
    vh[8:, :] = v
    z = conv_rows(vh, conv, mask)
    sz = sigmoid(z)
    act = z * sz
    xc = act[:, :HC]
    b16 = act[:, HC : 2 * HC].astype(BF16)
    c16 = act[:, 2 * HC :].astype(BF16)
    step, running, decays, reach, tail, carry = block_terms(dt, vec, mask, s.docr[b, 0:1, :])
    s.act[layer, rows, :] = act
    s.dact[layer, rows, :] = sz * (1.0 + z * (1.0 - sz))
    s.step[layer, rows, :] = step
    s.run[layer, rows, :] = running
    for h in (0, 1):
        s.decay[layer, b, h] = decays[h]
    xs = xc * step
    xs16 = xs.astype(BF16)
    scores = dot_nt(c16, b16)
    within = [dot_nn((scores * d).astype(BF16), xs16) for d in decays]
    first = iota((SPAN, HC), 1) < HEAD
    st = s.state[...]
    s.st[layer, b] = st
    scan = jnp.where(first, within[0], within[1]) + dot_nn(c16, st.astype(BF16)) * reach
    s.state[...] = st * carry + dot_tn(b16, (xs * tail).astype(BF16))
    mixed = (scan + xc * vec[2]).astype(BF16)
    g = mixed.astype(F32) * (gate * sigmoid(gate))
    s.part[rows, :width] = dot_nn((g * vec[3]).astype(BF16), s.wo[layer]).astype(BF16)
    s.part[rows, width:] = lanes_of(three(jnp.sum(g * g, axis=1, keepdims=True)), SPAN)
    s.gate[layer, rows, :] = gate
    s.dt[layer, rows, :] = dt
    s.mix[layer, rows, :] = mixed
    s.scan[layer, rows, :] = scan


def bwd_step(layer, b, s):
    rows_b = at_block(b)
    vbuf = s.vh.at[layer, b]
    gin, gout, small, dzbuf, dstate = s.gin, s.gout, s.small, s.dz, s.state

    @pl.when(b == s.vh.shape[1] - 1)
    def _():
        dzbuf[SPAN:, :] = jnp.zeros((8, 3 * HC), F32)
        dstate[...] = jnp.zeros_like(dstate)
        gin[...] = jnp.zeros_like(gin)
        gout[...] = jnp.zeros_like(gout)
        small[...] = jnp.zeros_like(small)

    width = s.wo.shape[2]
    chunk = s.wt.shape[3]
    mask = s.mask[rows_b, :]
    con = s.cons[layer]
    vec = layer_constants(con)
    conv = con[:, : 3 * HC]
    cot = s.c[layer, rows_b, :width]
    aux = s.c[layer, rows_b, width:].astype(F32)
    r = aux[:, 0:1] + aux[:, 1:2] + aux[:, 2:3]
    pull = aux[:, 3:4] + aux[:, 4:5]
    gate = s.gate[layer, rows_b, :]
    sg = sigmoid(gate)
    silu = gate * sg
    mixed = s.mix[layer, rows_b, :].astype(F32)
    g = mixed * silu
    gain = vec[3]
    dy = dot_nt(cot, s.wo[layer])
    gr = g * r
    gout[...] += dot_tn((gr * gain).astype(BF16), cot)
    d_gain = jnp.sum(dy * gr, axis=0, keepdims=True)
    dg = dy * (r * gain) - g * pull
    dm16 = (dg * silu).astype(BF16)
    dm = dm16.astype(F32)
    dgate = dg * mixed * (sg * (1.0 + gate * (1.0 - sg)))

    act = s.act[layer, rows_b, :]
    xc = act[:, :HC]
    b16 = act[:, HC : 2 * HC].astype(BF16)
    c16 = act[:, 2 * HC :].astype(BF16)
    step, running = s.step[layer, rows_b, :], s.run[layer, rows_b, :]
    log_decay = -step * vec[1]
    decays = [s.decay[layer, b, h] for h in (0, 1)]
    total = running[SPAN - 1 :, :]
    reach = jnp.exp(running) * mask[:, 6:7]
    tail = jnp.exp(total - running) * mask[:, 7:8]
    carry = jnp.exp(total) * mask[SPAN - 1 :, 6:7]
    xs16 = (xc * step).astype(BF16)
    xs = xs16.astype(F32)
    scores = dot_nt(c16, b16)
    first = iota((SPAN, HC), 1) < HEAD
    zero16 = jnp.zeros((SPAN, HC), BF16)
    dscores = jnp.zeros((SPAN, SPAN), F32)
    dxs = []
    for h in (0, 1):
        own = jnp.where(first, dm16, zero16) if h == 0 else jnp.where(first, zero16, dm16)
        dp = dot_nt(own, xs16)
        dscores = dscores + dp * decays[h]
        dxs.append(dot_tn((scores * decays[h]).astype(BF16), dm16))
    ds16 = dscores.astype(BF16)
    st = s.st[layer, b]
    dst = dstate[...]
    dst16 = dst.astype(BF16)
    dcs16 = (dm * reach).astype(BF16)
    dc = dot_nn(ds16, b16) + dot_nt(dcs16, st.astype(BF16))
    db = dot_tn(ds16, c16) + dot_nt((xs * tail).astype(BF16), dst16)
    dxs_tail = dot_nn(b16, dst16) * tail
    dxs_all = jnp.where(first, dxs[0], dxs[1]) + dxs_tail
    dstate[...] = dst * carry + dot_tn(c16, dcs16)

    d_total = jnp.sum(xs * dxs_tail, axis=0, keepdims=True) + carry * jnp.sum(
        dst * st, axis=0, keepdims=True
    )
    flow = dm * s.scan[layer, rows_b, :] - xs * dxs_all
    rows, cols = iota((SPAN, SPAN), 0), iota((SPAN, SPAN), 1)
    upper = (cols >= rows).astype(F32).astype(BF16)
    flow = exact_left(upper, flow) + d_total
    same_head = ((iota((HC, HC), 0) < HEAD) == (iota((HC, HC), 1) < HEAD)).astype(F32).astype(BF16)
    d_log = exact_right(flow, same_head)
    d_step = exact_right(dxs_all * xc, same_head) - d_log * vec[1]
    d_alog = jnp.sum(d_log * log_decay, axis=0, keepdims=True)
    d_dt = d_step * sigmoid(s.dt[layer, rows_b, :] + vec[0])
    d_skip = jnp.sum(dm * xc, axis=0, keepdims=True)
    d_xc = dm * vec[2] + dxs_all * step

    dact = s.dact[layer, rows_b, :]
    dzbuf[:SPAN, 0:HC] = d_xc * dact[:, :HC]
    dzbuf[:SPAN, HC : 2 * HC] = db * dact[:, HC : 2 * HC]
    dzbuf[:SPAN, 2 * HC :] = dc * dact[:, 2 * HC :]
    dz = dzbuf[:SPAN, :]
    dv = dz * conv[3:4, :]
    small[3:4, : 3 * HC] += jnp.sum(dz * vbuf[pl.ds(8, SPAN), :], axis=0, keepdims=True)
    small[4:5, : 3 * HC] += jnp.sum(dz, axis=0, keepdims=True)
    for k in (1, 2, 3):
        dv = dv + dzbuf[pl.ds(k, SPAN), :] * conv[3 - k : 4 - k, :] * mask[:, 2 + k : 3 + k]
        small[3 - k : 4 - k, : 3 * HC] += jnp.sum(
            dz * vbuf[pl.ds(8 - k, SPAN), :] * mask[:, k - 1 : k], axis=0, keepdims=True
        )
    dzbuf[SPAN:, :] = dz[:8, :]
    small[5:6, 0:HC] += d_gain
    small[5:6, HC : 2 * HC] += d_skip
    small[6:7, 0:HC] += jnp.sum(d_dt, axis=0, keepdims=True)
    small[6:7, HC : 2 * HC] += d_alog

    gp = jnp.concatenate([dgate.astype(BF16), dv.astype(BF16)], axis=1)
    gdt = dot_nn(d_dt.astype(BF16), head_firsts()).astype(BF16)
    wide = 4 * HC
    n = s.n[layer, rows_b, :]
    gin[:wide] += dot_nn(gp.T, n)
    gin[wide:] += dot_tn(gdt, n)
    for k in range(SIDE):
        cols_k = slice(k * chunk, (k + 1) * chunk)
        term = dot_nn(gp, s.wt[layer, k, :wide]) + dot_nn(gdt, s.wt[layer, k, wide:])
        s.part[rows_b, cols_k] = term.astype(BF16)
        d_pre = jnp.sum(term * n[:, cols_k].astype(F32), axis=0, keepdims=True)
        small[2 * k : 2 * k + 1, 3 * HC :] += d_pre[:, :HC]
        small[2 * k + 1 : 2 * k + 2, 3 * HC :] += d_pre[:, HC:]


def place_of(half, f, s):
    f, s = lax.rem(f, SIDE), lax.rem(s, SIDE)
    return s * SIDE + f if half == 0 else f * SIDE + s


def ring_places():
    me = lax.axis_index(AXIS)
    return me % SIDE, me // SIDE


def ring_neighbours():
    x, y = ring_places()
    steps = ((1, 0), (3, 0), (0, 1), (0, 3))
    return [{AXIS: place_of(0, x + dx, y + dy)} for dx, dy in steps]


def plane_neighbours():
    z = lax.axis_index("wshard")
    return [{"wshard": lax.rem(z + 1, SIDE)}, {"wshard": lax.rem(z + 3, SIDE)}]


def plane_across():
    return {"wshard": lax.rem(lax.axis_index("wshard") + 2, SIDE)}


def other_core():
    return {"section": 1 - lax.axis_index("section")}


def greet(targets):
    barrier = pltpu.get_barrier_semaphore()
    for target in targets:
        pl.semaphore_signal(barrier, inc=1, device_id=target, device_id_type=MESH)


def greeted(count):
    pl.semaphore_wait(pltpu.get_barrier_semaphore(), count)


def run(*parts, until=None):
    live = list(parts)
    while live if until is None else until in live:
        for part in list(live):
            try:
                next(part)
            except StopIteration:
                live.remove(part)
    return live


class Sender:
    def __init__(self, send, recv):
        self.send, self.recv, self.used, self.copies, self.free = send, recv, 0, {}, set()

    def make(self, name, source, target, to):
        copy = pltpu.make_async_remote_copy(
            src_ref=source, dst_ref=target, send_sem=self.send.at[self.used],
            recv_sem=self.recv.at[self.used], device_id=to, device_id_type=MESH,
        )
        self.used += 1
        self.copies[name] = copy
        return copy

    def go(self, name, source, target, to):
        self.make(name, source, target, to).start()
        self.free.add(name)

    def arrived(self, name):
        self.copies[name].wait_recv()

    def sent(self):
        for name in self.copies:
            if name in self.free:
                self.copies[name].wait_send()


def rows_at(ref, start, size):
    return ref.at[pl.ds(pl.multiple_of(start, 16), size)]


def spread_steps(x_ref, o_ref, out, own, tag=""):
    x, y = ring_places()
    rows = x_ref.shape[0]
    half_rows, quarter = rows // 2, rows // 4
    mine = pltpu.make_async_copy(x_ref, rows_at(o_ref, place_of(0, x, y) * rows, rows), own)
    mine.start()
    firsts = ((x, y), (y, x))

    def go(name, half, block, offset, size, to, source=None):
        place = rows_at(o_ref, block * rows + half * half_rows + offset, size)
        out.go((tag, half, name), place if source is None else source, place, {AXIS: to})

    def across(half, d):
        f, s = firsts[half]
        block = place_of(half, f + d, s)
        source = x_ref.at[pl.ds(half * half_rows, half_rows)] if d == 0 else None
        go(("t1", d), half, block, 0, half_rows, place_of(half, f, s + 1), source)
        go(("t2", d), half, block, 0, half_rows, place_of(half, f, s + 3), source)

    def onward(half, d):
        f, s = firsts[half]
        out.arrived((tag, half, ("t1", d)))
        go(("u1", d), half, place_of(half, f + d, s + 3), 0, quarter, place_of(half, f, s + 1))
        out.arrived((tag, half, ("t2", d)))
        go(("u2", d), half, place_of(half, f + d, s + 1), quarter, quarter, place_of(half, f, s + 3))

    for half in (0, 1):
        f, s = firsts[half]
        source = x_ref.at[pl.ds(half * half_rows, half_rows)]
        block = place_of(half, f, s)
        go("s1", half, block, 0, half_rows, place_of(half, f + 1, s), source)
        go("s2", half, block, 0, half_rows, place_of(half, f + 3, s), source)
    for half in (0, 1):
        across(half, 0)
    yield
    for half in (0, 1):
        f, s = firsts[half]
        out.arrived((tag, half, "s1"))
        go("s3", half, place_of(half, f + 3, s), 0, quarter, place_of(half, f + 1, s))
        out.arrived((tag, half, "s2"))
        go("s4", half, place_of(half, f + 1, s), quarter, quarter, place_of(half, f + 3, s))
    for half in (0, 1):
        across(half, 3)
        across(half, 1)
    yield
    for half in (0, 1):
        onward(half, 0)
    for half in (0, 1):
        out.arrived((tag, half, "s3"))
        out.arrived((tag, half, "s4"))
        across(half, 2)
    yield
    for d in (3, 1, 2):
        for half in (0, 1):
            onward(half, d)
        yield
    for half in (0, 1):
        for d in range(SIDE):
            out.arrived((tag, half, ("u1", d)))
            out.arrived((tag, half, ("u2", d)))
    mine.wait()


def collect_scratch(rows, cols):
    half_rows, quarter = rows // 2, rows // 4
    return [
        pltpu.VMEM((2, SIDE, 2, quarter, cols), BF16),
        pltpu.VMEM((2, SIDE, 2, half_rows, cols), BF16),
        pltpu.VMEM((2, SIDE, 2, half_rows, cols), BF16),
        pltpu.VMEM((2, SIDE, half_rows, cols), BF16),
        pltpu.VMEM((2, SIDE, half_rows, cols), BF16),
        pltpu.VMEM((rows, cols), F32),
    ]


def collect_steps(x_ref, buffers, out, wide):
    cols = pl.ds(0, wide)
    far, near, stage, stage2, last = [a.at[..., cols] for a in buffers[:5]]
    x_ref, o_ref = x_ref.at[:, cols], buffers[5].at[:, cols]
    x, y = ring_places()
    rows = o_ref.shape[0]
    half_rows, quarter = rows // 2, rows // 4
    firsts = ((x, y), (y, x))
    order = (2, 1, 3, 0)

    def go(name, half, source, target, to):
        out.go((half, name), source, target, {AXIS: to})

    def start_of(half, f, s):
        return pl.multiple_of(place_of(half, f, s) * rows + half * half_rows, 16)

    for d in order:
        for half in (0, 1):
            f, s = firsts[half]
            start = start_of(half, f + d, s + 2)
            go(("a1", d), half, rows_at(x_ref, start, quarter), far.at[half, d, 0],
               place_of(half, f, s + 1))
            go(("a2", d), half, rows_at(x_ref, start + quarter, quarter), far.at[half, d, 1],
               place_of(half, f, s + 3))
    yield
    for d in order:
        for half in (0, 1):
            f, s = firsts[half]
            for side, step in enumerate((1, 3)):
                start = start_of(half, f + d, s + step)
                plain, through = quarter * (1 - side), quarter * side
                stage[half, d, side, pl.ds(plain, quarter)] = x_ref[
                    pl.ds(pl.multiple_of(start + plain, 16), quarter), :
                ]
                out.arrived((half, (("a1", "a2")[side], d)))
                stage[half, d, side, pl.ds(through, quarter)] = (
                    x_ref[pl.ds(pl.multiple_of(start + through, 16), quarter), :].astype(F32)
                    + far[half, d, side].astype(F32)
                ).astype(BF16)
                go((("b1", "b2")[side], d), half, stage.at[half, d, side], near.at[half, d, side],
                   place_of(half, f, s + step))
        if d in (1, 0):
            yield

    def summed(half, d):
        f, s = firsts[half]
        out.arrived((half, ("b1", d)))
        out.arrived((half, ("b2", d)))
        return (
            x_ref[pl.ds(start_of(half, f + d, s), half_rows), :].astype(F32)
            + near[half, d, 0].astype(F32) + near[half, d, 1].astype(F32)
        )

    for d in order[:3]:
        for half in (0, 1):
            f, s = firsts[half]
            stage2[half, d] = summed(half, d).astype(BF16)
            go(("first", d), half, stage2.at[half, d], last.at[half, d], place_of(half, f + d, s))
        yield
    for half in (0, 1):
        o_ref[pl.ds(half * half_rows, half_rows), :] = summed(half, 0)
    yield
    for half in (0, 1):
        own = pl.ds(half * half_rows, half_rows)
        total = o_ref[own, :]
        for d in (1, 3, 2):
            out.arrived((half, ("first", d)))
            total = total + last[half, d].astype(F32)
        o_ref[own, :] = total


def half_of(rows):
    return rows // 32 * 16


def fold_scratch(count):
    scratch = [pltpu.VMEM((8, 4 * HC), F32)] * 2 + [pltpu.VMEM((3, 8, 4 * HC), F32)]
    for rows, cols in ((FR, 256), (HC // SIDE, 1024)):
        scratch += [pltpu.VMEM((SIDE, rows, cols), BF16)] * 3
        scratch += [pltpu.VMEM((2, rows - half_of(rows), cols), BF16)]
        scratch += [pltpu.VMEM((2, rows, cols), BF16)]
    scratch += [pltpu.VMEM((2 * NS, 1024), BF16), pltpu.VMEM((count, 16, 1024), BF16)]
    scratch += [pltpu.VMEM((SIDE, 16, 256), BF16)] * 3 + [pltpu.VMEM((3, 16, 256), BF16)]
    return scratch


def bc_steps(gin, buffers, out):
    me, count = lax.axis_index(AXIS), lax.axis_size(AXIS)
    terms, landing, mine = buffers[13], buffers[14], buffers[15]
    terms[...] = gin[2 * HC : 4 * HC, :].astype(BF16)
    for d in range(1, count):
        to = lax.rem(me + d, count)
        out.go(("bc", d), rows_at(terms, to * 16, 16), landing.at[d], {AXIS: to})
    yield
    yield
    total = terms[pl.ds(pl.multiple_of(me * 16, 16), 16), :].astype(F32)
    for d in range(1, count):
        out.arrived(("bc", d))
        total = total + landing[d].astype(F32)
    for k in range(SIDE):
        mine[k] = total[:, k * 256 : (k + 1) * 256].astype(BF16)
    yield


def fold_steps(layer, gin, gout, fin_ref, fout_ref, buffers, out):
    z = lax.axis_index("wshard")
    up, down = plane_neighbours()
    owner = lax.axis_index("section") == layer
    ours_in, land_in, total_in, far_in, near_in = buffers[3:8]
    ours_out, land_out, total_out, far_out, near_out = buffers[8:13]
    piece = HC // SIDE
    for k in range(SIDE):
        cols = slice(k * 256, (k + 1) * 256)
        ours_in[k, : 2 * HC] = gin[: 2 * HC, cols].astype(BF16)
        ours_in[k, 2 * HC :] = gin[4 * HC :, cols].astype(BF16)
        ours_out[k] = gout[k * piece : (k + 1) * piece, :].astype(BF16)
    arrays = (
        (ours_in, land_in, total_in, far_in, near_in, fin_ref),
        (ours_out, land_out, total_out, far_out, near_out, fout_ref),
    )

    def at(d):
        return lax.rem(z + d, SIDE)

    swaps, legs = {}, {}
    parts = []
    for ours in (ours_in, ours_out):
        half = half_of(ours.shape[1])
        parts.append((pl.ds(0, half), pl.ds(half, ours.shape[1] - half)))
    for d in (2, 1, 3, 0):
        for k, (ours, land, *_) in enumerate(arrays):
            swaps[k, d] = out.make(("swap", k, d), ours.at[at(d)], land.at[at(d)], other_core())
    for k, (_, _, total, far, near, _) in enumerate(arrays):
        for side, to in enumerate((up, down)):
            some = parts[k][side]
            legs[k, "far", side] = out.make(
                ("far", k, side), total.at[at(2), some], far.at[side, pl.ds(0, some.size)], to
            )
        legs[k, "near", 0] = out.make(("near", k, 0), total.at[at(1)], near.at[0], up)
        legs[k, "near", 1] = out.make(("near", k, 1), total.at[at(3)], near.at[1], down)

    @pl.when(jnp.logical_not(owner))
    def _():
        for copy in swaps.values():
            copy.start()

    yield

    def add_cores(d):
        for k, (ours, land, total, *_) in enumerate(arrays):
            swaps[k, d].wait_recv()
            total[at(d)] = (ours[at(d)].astype(F32) + land[at(d)].astype(F32)).astype(BF16)

    @pl.when(owner)
    def _():
        add_cores(2)
        for k in (0, 1):
            legs[k, "far", 0].start()
            legs[k, "far", 1].start()

    yield
    for side, d in ((0, 1), (1, 3)):
        @pl.when(owner)
        def _():
            add_cores(d)
            for k, (_, _, total, far, _, _) in enumerate(arrays):
                legs[k, "far", side].wait_recv()
                some = parts[k][side]
                total[at(d), some] = (
                    total[at(d), some].astype(F32) + far[side, pl.ds(0, some.size)].astype(F32)
                ).astype(BF16)
                legs[k, "near", side].start()

        yield

    @pl.when(owner)
    def _():
        add_cores(0)
        for k, (_, _, total, _, near, done) in enumerate(arrays):
            legs[k, "near", 0].wait_recv()
            legs[k, "near", 1].wait_recv()
            done[...] = (
                total[at(0)].astype(F32) + near[0].astype(F32) + near[1].astype(F32)
            ).astype(BF16)
        for leg in legs.values():
            leg.wait_send()

    @pl.when(jnp.logical_not(owner))
    def _():
        for copy in swaps.values():
            copy.wait_send()


def fold_small(layer, small, gains, done_ref, bc_ref, buffers, out):
    small[:, 3 * HC :] = small[:, 3 * HC :] / gains
    owner = lax.axis_index("section") == layer
    z = lax.axis_index("wshard")
    land, total, planes = buffers[:3]
    mine, land_bc, total_bc, planes_bc = buffers[15:19]
    up, down = plane_neighbours()
    swaps = [
        out.make("small", small, land, other_core()), out.make("bc", mine, land_bc, other_core()),
    ]
    legs = []
    for k, (d, to) in enumerate(((1, up), (3, down), (2, plane_across()))):
        legs.append(out.make(("small", k), total, planes.at[k], to))
        legs.append(out.make(
            ("bc", k), total_bc.at[lax.rem(z + d, SIDE)], planes_bc.at[k], to))

    @pl.when(jnp.logical_not(owner))
    def _():
        for swap in swaps:
            swap.start()

    @pl.when(owner)
    def _():
        for swap in swaps:
            swap.wait_recv()
        total[...] = small[...] + land[...]
        total_bc[...] = (mine[...].astype(F32) + land_bc[...].astype(F32)).astype(BF16)
        for leg in legs:
            leg.start()

    yield

    @pl.when(owner)
    def _():
        for leg in legs:
            leg.wait_recv()
        done_ref[...] = total[...] + planes[0] + planes[1] + planes[2]
        sum_bc = total_bc[z].astype(F32)
        for k in range(3):
            sum_bc = sum_bc + planes_bc[k].astype(F32)
        bc_ref[...] = sum_bc.astype(BF16)
        for leg in legs:
            leg.wait_send()

    @pl.when(jnp.logical_not(owner))
    def _():
        for swap in swaps:
            swap.wait_send()


def closing_steps(s, layer_sums, out, own):
    x, y = ring_places()
    z = lax.axis_index("wshard")
    first = lax.axis_index("section") == 0
    fin, bc, fout, small = [
        jnp.where(first, a[...], b[...]) for a, b in zip(layer_sums[0], layer_sums[1])
    ]
    s.turning[...] = fout
    turned = {AXIS: place_of(0, x, z), "wshard": y}
    turn = out.make("turn", s.turning, s.came, turned)

    @pl.when(z != y)
    def _():
        turn.start()

    s.block[0 : 2 * HC, :] = fin[: 2 * HC]
    s.block[2 * HC : 2 * HC + 16, :] = bc
    s.block[2 * HC + 16 : 2 * HC + 32, :] = fin[2 * HC :]
    hi, mid, _ = three(jnp.concatenate([small[:, :256], small[:, 256:]]))
    s.block[END_ROWS - 32 : END_ROWS - 16, :] = hi
    s.block[END_ROWS - 16 :, :] = mid
    main = spread_steps(s.block, s.gathered, out, own.at[2], "in")
    next(main)
    yield
    next(main)

    @pl.when(z != y)
    def _():
        turn.wait_recv()

    @pl.when(z == y)
    def _():
        s.came[...] = s.turning[...]

    for c in range(4):
        s.wide_rows[32 * c : 32 * (c + 1), :] = s.came[:, c * 256 : (c + 1) * 256]
    side = spread_steps(s.wide_rows, s.pieces, out, own.at[3], "out")
    live = [main, side]
    while live:
        for part in list(live):
            try:
                next(part)
            except StopIteration:
                live.remove(part)
        yield

    @pl.when(z != y)
    def _():
        turn.wait_send()


def norm_rows(u):
    return u * lax.rsqrt(jnp.mean(u * u, axis=1, keepdims=True) + EPS)


def payload_into(ref, c, branch, r, inner):
    width = c.shape[1]
    low = c.astype(BF16)
    pull = r * r * jnp.sum(low.astype(F32) * branch, axis=1, keepdims=True) / inner
    ref[:, :width] = low
    ref[:, width:] = lanes_of(list(three(r)) + list(three(pull))[:2], c.shape[0])


def constants_into(con, params):
    cw_ref, cb_ref, dtb_ref, alog_ref, skip_ref, pre_ref, gain_ref = params
    q = lax.axis_index(AXIS)
    inner = gain_ref.shape[1]
    own = pl.ds(pl.multiple_of(q * HC, HC), HC)
    con[...] = jnp.zeros_like(con)
    con[0:4, :HC] = cw_ref[0, :, own]
    con[0:4, HC : 3 * HC] = cw_ref[0, :, inner:]
    con[4:5, :HC] = cb_ref[:, own]
    con[4:5, HC : 3 * HC] = cb_ref[:, inner:]

    def lanes(ref):
        value = ref[...]
        lane = iota(value.shape, 1)
        two = [
            jnp.sum(jnp.where(lane == 2 * q + h, value, 0.0), axis=1, keepdims=True) for h in (0, 1)
        ]
        return jnp.where(iota((1, HC), 1) < HEAD, two[0], two[1])

    con[5:6, :HC] = lanes(dtb_ref)
    con[5:6, HC : 2 * HC] = jnp.exp(lanes(alog_ref))
    con[5:6, 2 * HC : 3 * HC] = lanes(skip_ref)
    con[6:7, :HC] = gain_ref[:, own]
    for k in range(8):
        con[k : k + 1, 3 * HC :] = pre_ref[:, k * HC : (k + 1) * HC]


def mask_steps(doc_ref, mask_ref, docr_ref):
    yield
    doc = doc_ref[lax.axis_index("section")].astype(F32)
    length = doc.shape[1]
    doc8 = jnp.broadcast_to(doc, (8, length))
    for b in range(length // SPAN):
        docr_ref[b] = doc8[:, b * SPAN : (b + 1) * SPAN]
    at = iota((8, length), 1)
    rows = []
    for k in (1, 2, 3):
        rows.append((pltpu.roll(doc8, k, 1) == doc8) & (at >= k))
    for k in (1, 2, 3):
        rows.append((pltpu.roll(doc8, length - k, 1) == doc8) & (at < length - k))
    before, final = doc8, doc8
    for b in range(length // SPAN):
        inside = (at >= b * SPAN) & (at < (b + 1) * SPAN)
        start = max(b * SPAN - 1, 0)
        end = (b + 1) * SPAN - 1
        before = jnp.where(inside, doc[:, start : start + 1], before)
        final = jnp.where(inside, doc[:, end : end + 1], final)
    rows += [before == doc8, final == doc8]
    sub = iota((8, length), 0)
    first = jnp.zeros((8, length), F32)
    for k, row in enumerate(rows):
        first = jnp.where((sub == k) & row, 1.0, first)
    both = jnp.concatenate([first, doc8, jnp.zeros((HC - 16, length), F32)])
    mask_ref[...] = both.T


def sems(count):
    return [pltpu.SemaphoreType.DMA((count,)), pltpu.SemaphoreType.DMA((count,))]


def weights_steps(layer, wo_ref, s, out, own):
    x, y = ring_places()
    z = lax.axis_index("wshard")
    holder = lax.axis_index("section") == layer

    def at(d):
        return lax.rem(z + d, SIDE)

    def to(d):
        return {"wshard": at(d)}

    hops = (2, 1, 3)
    mine = pltpu.make_async_copy(s.own_w, s.wt.at[layer, z], own.at[4])
    rows = {d: out.make(("w", d), s.own_w, s.wt.at[layer, z], to(d)) for d in hops}
    role = at(SIDE - y)
    target = s.wo.at[layer]
    source = wo_ref.at[0, pl.ds(pl.multiple_of(x * HC, HC), HC)]
    mine_wo = pltpu.make_async_copy(source, target, own.at[5])
    rows_wo = {d: out.make(("wo", d), source, target, to(d)) for d in hops}
    swaps = {}
    for d in range(SIDE):
        block = s.wt.at[layer, at(SIDE - d)]
        swaps[d] = out.make(("swap", d), block, block, other_core())
    swap_wo = out.make("swap_wo", target, target, other_core())

    @pl.when(holder)
    def _():
        mine.start()
        for copy in rows.values():
            copy.start()

    @pl.when(holder & (role == 0))
    def _():
        mine_wo.start()
        for copy in rows_wo.values():
            copy.start()

    yield

    @pl.when(holder)
    def _():
        mine.wait()
        swaps[0].start()

    yield
    for d in (1, 3, 2):
        @pl.when(holder)
        def _():
            rows[d].wait_recv()
            swaps[d].start()

        yield

    @pl.when(holder & (role == 0))
    def _():
        mine_wo.wait()

    for d in hops:
        @pl.when(holder & (role == d))
        def _():
            rows_wo[d].wait_recv()

    @pl.when(holder)
    def _():
        swap_wo.start()

    yield

    @pl.when(jnp.logical_not(holder))
    def _():
        for copy in swaps.values():
            copy.wait_recv()
        swap_wo.wait_recv()

    @pl.when(holder)
    def _():
        for copy in list(rows.values()) + list(swaps.values()) + [swap_wo]:
            copy.wait_send()

    @pl.when(holder & (role == 0))
    def _():
        for copy in rows_wo.values():
            copy.wait_send()


def hand_over(layer, rows, target, copy_sem, out, name):
    part = lax.axis_index("section")
    keep = pltpu.make_async_copy(rows, target.at[part], copy_sem)
    give = out.make(name, rows, target.at[part], other_core())

    @pl.when(part == layer)
    def _():
        keep.start()

    @pl.when(part != layer)
    def _():
        give.start()

    def finish():
        @pl.when(part == layer)
        def _():
            keep.wait()
            give.wait_recv()

        @pl.when(part != layer)
        def _():
            give.wait_send()

    return finish


class Scratch:
    def __init__(self, refs):
        self.__dict__.update(refs)


def scratch_shapes(count, rows, width, heads, params, doc_shape):
    length = count * rows
    blocks = length // SPAN
    wide = width + AUX
    half_rows, quarter = rows // 2, rows // 4
    shapes = {
        "n": ((2, length, width), BF16), "c": ((2, length, wide), BF16),
        "wt": ((2, SIDE, WR, 256), BF16), "wo": ((2, HC, width), BF16),
        "cons": ((2, 8, 4 * HC), F32), "mask": ((length, HC), F32),
        "docr": ((blocks, 8, SPAN), F32),
        "vh": ((2, blocks, SPAN + 8, 3 * HC), F32), "gate": ((2, length, HC), F32),
        "dt": ((2, length, HC), F32), "mix": ((2, length, HC), BF16),
        "scan": ((2, length, HC), F32), "st": ((2, blocks, NS, HC), F32),
        "state": ((NS, HC), F32), "dz": ((SPAN + 8, 3 * HC), F32),
        "part": ((length, wide), BF16),
        "act": ((2, length, 3 * HC), F32), "dact": ((2, length, 3 * HC), F32),
        "step": ((2, length, HC), F32), "run": ((2, length, HC), F32),
        "decay": ((2, blocks, 2, SPAN, SPAN), F32),
        "gin": ((WR, width), F32), "gout": ((HC, width), F32),
        "small": ((8, 4 * HC), F32),
        "u": ((rows, width), F32), "h": ((2, rows, width), F32), "branch": ((rows, width), F32),
        "r": ((rows, HC), F32), "g": ((2, rows, width), F32),
        "own_n": ((rows, width), BF16), "own_c": ((rows, wide), BF16),
        "x_in": ((rows, width), BF16), "og_in": ((rows, width), BF16),
        "doc_in": (doc_shape, jnp.int32), "own_w": ((WR, 256), BF16), "dts": ((heads, 256), BF16),
        "turning": ((HC // SIDE, width), BF16), "came": ((HC // SIDE, width), BF16),
        "block": ((END_ROWS, 256), BF16), "wide_rows": ((HC, 256), BF16),
        "gathered": ((count * END_ROWS, 256), BF16), "pieces": ((count * HC, 256), BF16),
    }
    for k, p in enumerate(params):
        shapes["param%d" % k] = (p.shape, F32)
    for l in (0, 1):
        shapes["fin%d" % l] = ((FR, 256), BF16)
        shapes["bc%d" % l] = ((16, 256), BF16)
        shapes["fout%d" % l] = ((HC // SIDE, width), BF16)
        shapes["fsmall%d" % l] = ((8, 4 * HC), F32)
    return shapes


def layers_kernel(inner, names, x_ref, og_ref, w_ref, wo_ref, doc_ref, *refs):
    params, (hid_ref, ing_ref, next_ref, pieces_ref), refs = refs[:7], refs[7:11], refs[11:]
    s = Scratch(zip(names, refs))
    refs = refs[len(names) :]
    sem_pairs, (own, fetch), buffers = refs[:14], refs[14:16], refs[16:]
    collecting, folding = buffers[:6], buffers[6:]
    sems_of = [tuple(sem_pairs[2 * k : 2 * k + 2]) for k in range(7)]
    i = pl.program_id(0)
    blocks = s.vh.shape[1]
    phase, at = i // blocks, lax.rem(i, blocks)
    part, z = lax.axis_index("section"), lax.axis_index("wshard")
    q, count = lax.axis_index(AXIS), lax.axis_size(AXIS)
    x, y = ring_places()
    width = s.u.shape[1]
    wide = s.part.shape[1]
    handing = Sender(*sems_of[5])

    @pl.when(i == 0)
    def _():
        targets = [{AXIS: lax.rem(q + d, count)} for d in range(1, count)]
        targets += [{"wshard": lax.rem(z + d, SIDE)} for d in (1, 2, 3)] + [other_core()]
        greet(targets)

        @pl.when(z != y)
        def _():
            greet([{AXIS: place_of(0, x, z), "wshard": y}])

        held = [s.__dict__["param%d" % k] for k in range(7)]
        first = (w_ref.shape[0] - 2 * NS) // 2 // HC * HC
        pieces = list(zip(params, held))
        pieces += [(x_ref.at[part, 0], s.x_in)]
        pieces += [
            (w_ref.at[pl.ds(pl.multiple_of(q * HC, HC), HC)], s.own_w.at[pl.ds(0, HC)]),
            (w_ref.at[pl.ds(pl.multiple_of(first + q * HC, HC), HC)], s.own_w.at[pl.ds(HC, HC)]),
            (w_ref.at[pl.ds(2 * first, 2 * NS)], s.own_w.at[pl.ds(2 * HC, 2 * NS)]),
            (w_ref.at[pl.ds(2 * first + 2 * NS, s.dts.shape[0])], s.dts),
            (doc_ref, s.doc_in), (og_ref.at[part, 0], s.og_in),
        ]
        copies = [
            pltpu.make_async_copy(source, target, fetch.at[k])
            for k, (source, target) in enumerate(pieces)
        ]
        for copy in copies:
            copy.start()
        for copy in copies[:7]:
            copy.wait()
        constants_into(s.cons.at[part], held)
        copies[7].wait()
        u = s.x_in[...].astype(F32)
        s.u[...] = u
        normed = norm_rows(u)
        copies[12].wait()
        run(mask_steps(s.doc_in, s.mask, s.docr))
        greeted(len(targets) + (z != y).astype(jnp.int32))
        out, planes = Sender(*sems_of[0]), Sender(*sems_of[1])
        planes.go("con", s.cons.at[part], s.cons.at[part], other_core())

        def prepare():
            for copy in copies[8:12]:
                copy.wait()
            heads = s.dts.shape[0]
            pick = (iota((16, heads), 1) == 2 * q + iota((16, heads), 0)) & (
                iota((16, heads), 0) < 2
            )
            pick = pick.astype(F32).astype(BF16)
            s.own_w[4 * HC :, :] = dot_nn(pick, s.dts[...]).astype(BF16)
            weights = weights_steps(0, wo_ref, s, planes, own)
            next(weights)
            yield
            copies[13].wait()
            yield from weights

        planes.arrived("con")
        s.own_n[...] = (normed * pre_gain_of(s.cons[0])).astype(BF16)
        run(spread_steps(s.own_n, s.n.at[0], out, own.at[0]), prepare())
        out.sent()
        planes.sent()

    @pl.when(phase < 2)
    def _():
        fwd_step(phase, at, s)

    @pl.when(phase >= 2)
    def _():
        bwd_step(3 - phase, blocks - 1 - at, s)

    def normed_sums():
        total = collecting[-1]
        square = total[:, width : width + 1] + total[:, width + 1 : width + 2]
        square = square + total[:, width + 2 : width + 3]
        r = lax.rsqrt(square / inner + EPS)
        return total[:, :width] * r, r

    @pl.when(i == blocks - 1)
    def _():
        out, more, planes = Sender(*sems_of[2]), Sender(*sems_of[0]), Sender(*sems_of[6])
        weights = weights_steps(1, wo_ref, s, planes, own)
        collect = collect_steps(s.part, collecting, out, wide)
        live = run(collect, weights, until=collect)
        branch, r = normed_sums()
        h = s.u[...] + branch
        s.own_n[...] = (norm_rows(h) * pre_gain_of(s.cons[1])).astype(BF16)
        spread = spread_steps(s.own_n, s.n.at[1], more, own.at[0])
        next(spread)
        s.h[0] = h
        s.branch[...] = branch
        s.r[...] = jnp.broadcast_to(r, s.r.shape)
        run(spread, *live)
        out.sent()
        more.sent()
        planes.sent()

    @pl.when(i == 2 * blocks - 1)
    def _():
        out, more = Sender(*sems_of[2]), Sender(*sems_of[0])
        run(collect_steps(s.part, collecting, out, wide))
        branch, r = normed_sums()
        payload_into(s.own_c, s.og_in[...].astype(F32), branch, r, inner)
        spread = spread_steps(s.own_c, s.c.at[1], more, own.at[0])
        next(spread)
        s.h[1] = s.h[0] + branch
        run(spread)
        out.sent()
        more.sent()

    def input_gradient(layer, u, cot):
        g = collecting[-1][:, :width]
        ri = lax.rsqrt(jnp.mean(u * u, axis=1, keepdims=True) + EPS)
        gg = g * pre_gain_of(s.cons[layer])
        dot = jnp.sum(gg * u, axis=1, keepdims=True) / width
        return cot + gg * ri - u * (ri * ri * ri * dot)

    def sums_of(layer):
        return [s.__dict__[name + str(layer)] for name in ("fin", "bc", "fout", "fsmall")]

    def gradients(layer, out, folds):
        fin, bc, fout, fsmall = sums_of(layer)
        gains = s.cons[layer][:, 3 * HC :]
        fold = fold_steps(layer, s.gin, s.gout, fin, fout, folding, folds)
        sums = bc_steps(s.gin, folding, out)
        small = fold_small(layer, s.small, gains, fsmall, bc, folding, folds)
        return fold, sums, small

    @pl.when(i == 3 * blocks - 1)
    def _():
        out, folds, more = Sender(*sems_of[2]), Sender(*sems_of[3]), Sender(*sems_of[0])
        collect = collect_steps(s.part, collecting, out, width)
        fold, bc, small = gradients(1, out, folds)
        live = run(collect, fold, bc, until=collect)
        live = run(*live, until=bc) + [small]
        c = input_gradient(1, s.h[0], s.og_in[...].astype(F32))
        payload_into(s.own_c, c, s.branch[...], s.r[:, 0:1], inner)
        spread = spread_steps(s.own_c, s.c.at[0], more, own.at[0])
        next(spread)
        s.g[1] = c
        run(spread, *live)
        out.sent()
        more.sent()

    @pl.when(i == 4 * blocks - 1)
    def _():
        out, folds, more = Sender(*sems_of[2]), Sender(*sems_of[3]), Sender(*sems_of[4])
        finishers = [
            hand_over(0, s.h.at[0], hid_ref, own.at[6], handing, "h0"),
            hand_over(1, s.h.at[1], hid_ref, own.at[6], handing, "h1"),
            hand_over(1, s.g.at[1], ing_ref, own.at[7], handing, "g1"),
        ]
        collect = collect_steps(s.part, collecting, out, width)
        fold, bc, small = gradients(0, out, folds)
        live = run(collect, fold, bc, until=bc) + [small]
        live = run(*live, until=small)
        live = run(*live, until=fold)
        closing = closing_steps(s, (sums_of(0), sums_of(1)), more, own)
        if collect in live:
            live = run(closing, collect, until=collect)
        else:
            live = [closing]
        s.g[0] = input_gradient(0, s.u[...], s.g[1])
        finishers.append(hand_over(0, s.g.at[0], ing_ref, own.at[7], handing, "g0"))
        run(*live)
        copies = [
            pltpu.make_async_copy(s.gathered, next_ref, own.at[0]),
            pltpu.make_async_copy(s.pieces, pieces_ref, own.at[1]),
        ]
        for copy in copies:
            copy.start()
        out.sent()
        more.sent()
        for finish in finishers:
            finish()
        for copy in copies:
            copy.wait()


def layers(block_input, out_grad, w, wo, doc_ids, *params):
    hbm = pl.BlockSpec(memory_space=pl.ANY)
    rows, width = block_input.shape[2:]
    count = lax.axis_size(AXIS)
    inner = params[-1].shape[1]
    shapes = scratch_shapes(count, rows, width, params[2].shape[1], params, doc_ids.shape)

    def shape(dims, dtype=F32):
        return jax.ShapeDtypeStruct(dims, dtype)

    return pl.pallas_call(
        lambda *refs: layers_kernel(inner, list(shapes), *refs),
        grid=(4 * count * rows // SPAN,),
        in_specs=[hbm] * 12,
        out_specs=[hbm] * 4,
        out_shape=[
            shape((2, rows, width)), shape((2, rows, width)),
            shape((count * END_ROWS, 256), BF16), shape((count * HC, 256), BF16),
        ],
        scratch_shapes=[
            *[pltpu.VMEM(dims, dtype) for dims, dtype in shapes.values()],
            *sems(40), *sems(16), *sems(56), *sems(24), *sems(82), *sems(4), *sems(16),
            pltpu.SemaphoreType.DMA((8,)), pltpu.SemaphoreType.DMA((14,)),
            *collect_scratch(rows, width + AUX), *fold_scratch(count),
        ],
        compiler_params=pltpu.CompilerParams(
            collective_id=1, has_side_effects=True, vmem_limit_bytes=VMEM_ASK
        ),
        name="layers",
    )(block_input, out_grad, w, wo, doc_ids, *params)


def assemble_kernel(
    inner, all_ref, pieces_ref, gin_ref, gout_ref, convw_ref, convb_ref, pre_ref, gain_ref,
    step_ref, alog_ref, skip_ref,
):
    count = all_ref.shape[0]
    lane = iota((1, HC), 1)
    bc = jnp.zeros((5, 2 * HC), F32)
    pre = jnp.zeros((8, HC), F32)
    per_head = [jnp.zeros((1, HC), F32)] * 3
    for j in range(count):
        own = slice(j * HC, (j + 1) * HC)
        gin_ref[own, :] = all_ref[j, 0:HC, :].astype(F32)
        gin_ref[inner + j * HC : inner + (j + 1) * HC, :] = all_ref[j, HC : 2 * HC, :].astype(F32)
        at = 2 * inner + j * 16
        gin_ref[at : at + 16, :] = all_ref[j, 256:272, :].astype(F32)
        at = 2 * inner + 2 * NS + 2 * j
        gin_ref[at : at + 2, :] = all_ref[j, 272:288, :].astype(F32)[0:2, :]
        big, piece = j % SIDE, j // SIDE
        at = big * HC + piece * 32
        for c in range(4):
            gout_ref[at : at + 32, c * 256 : (c + 1) * 256] = (
                pieces_ref[j, 32 * c : 32 * (c + 1), :].astype(F32)
            )
        small = all_ref[j, END_ROWS - 32 : END_ROWS - 16, :].astype(F32)
        small = small + all_ref[j, END_ROWS - 16 :, :].astype(F32)
        convw_ref[:, own] = small[0:4, :HC]
        convb_ref[:, own] = small[4:5, :HC]
        gain_ref[:, own] = small[5:6, :HC]
        bc = bc + jnp.concatenate([small[0:5, HC:], small[8:13, :HC]], axis=1)
        pre = pre + small[8:16, HC:]
        skip = small[5:6, HC:]
        for h in (0, 1):
            here = lane == 2 * j + h
            mine = (lane >= h * HEAD) & (lane < (h + 1) * HEAD)
            values = (
                small[6:7, h * HEAD : h * HEAD + 1],
                small[6:7, HC + h * HEAD : HC + h * HEAD + 1],
                jnp.sum(jnp.where(mine, skip, 0.0), axis=1, keepdims=True),
            )
            per_head = [jnp.where(here, v, p) for v, p in zip(values, per_head)]
    convw_ref[:, inner:] = bc[0:4]
    convb_ref[:, inner:] = bc[4:5]
    for k in range(8):
        pre_ref[:, k * HC : (k + 1) * HC] = pre[k : k + 1]
    for ref, value in zip((step_ref, alog_ref, skip_ref), per_head):
        ref[...] = value[:, : ref.shape[1]]


def assemble(everyone, pieces, inner, columns, width, channels, heads):
    def shape(*dims):
        return jax.ShapeDtypeStruct(dims, F32)

    vmem = pl.BlockSpec(memory_space=pltpu.VMEM)
    return pl.pallas_call(
        lambda *refs: assemble_kernel(inner, *refs),
        in_specs=[vmem] * 2,
        out_specs=[vmem] * 9,
        out_shape=[
            shape(columns, 256), shape(512, width), shape(4, channels), shape(1, channels),
            shape(1, width), shape(1, inner), *[shape(1, heads)] * 3,
        ],
        compiler_params=pltpu.CompilerParams(vmem_limit_bytes=VMEM_ASK),
        name="assemble",
    )(everyone, pieces)


def body(
    block_input, doc_ids, out_grad, in_proj, out_proj, conv_weight, conv_bias,
    dt_bias, a_log, skip_scale, pre_gain, norm_gain,
):
    inner = norm_gain.shape[1]
    width = block_input.shape[3]
    heads = dt_bias.shape[1]
    hidden, input_grads, everyone, pieces = layers(
        block_input, out_grad, jnp.swapaxes(in_proj[0], 0, 1), out_proj, doc_ids,
        conv_weight, conv_bias, dt_bias, a_log, skip_scale, pre_gain, norm_gain,
    )
    everyone = everyone.reshape(-1, END_ROWS, 256)
    pieces = pieces.reshape(-1, HC, 256)
    gin, gout, convw, convb, pre, gain, step, alog, skip = assemble(
        everyone, pieces, inner, in_proj.shape[2], width, conv_weight.shape[2], heads
    )
    return (
        hidden[None, :, None], input_grads[None, :, None],
        jnp.swapaxes(gin, 0, 1)[None], gout[None], convw[None], convb,
        step, alog, skip, pre, gain,
    )


def solution(mesh):
    specs = (
        P(None, "wshard", "seq", None),
        P(None, "wshard", None),
        P(None, "wshard", "seq", None),
        P("section", "wshard", None),
        P("section", "wshard", None),
        P("section", None, None),
        P("section", None),
        P("section", None),
        P("section", None),
        P("section", None),
        P("section", None),
        P("section", None),
    )
    outs = (
        P("section", None, "wshard", "seq", None),
        P("section", None, "wshard", "seq", None),
        P("section", "wshard", None),
        P("section", "wshard", None),
        P("section", None, None),
    ) + (P("section", None),) * 6
    return jax.shard_map(body, mesh=mesh, in_specs=specs, out_specs=outs, check_vma=False)
```
